32 devices in a mesh: dp: 4 (over y, x), expert: 8 (over z, core).
Axes of the slice: x: 2, y: 2, z: 4, core: 2. Of those that a mesh axis runs over, the one named last changes fastest.
Arguments:
- hidden_in: bfloat16 [32768, 768], P(('dp', 'expert')), may hold values from -6 to 6
- token_ids: int32 [32768], P(('dp', 'expert')), may hold values from 0 to 50256, as said below
- hash_table: int32 [50257], replicated, may hold values from 0 to 7, as said below
- segment_ids: int32 [32768], P(('dp', 'expert')), may hold values from 0 to 8, as said below
- ln1_gain: float32 [768], replicated, may hold values from 0.5 to 1.5
- ln1_bias: float32 [768], replicated, may hold values from -2 to 2
- qkv_weight: bfloat16 [768, 2304], replicated, may hold values from -0.21875 to 0.21875
- proj_weight: bfloat16 [768, 768], replicated, may hold values from -0.875 to 0.875
- ln2_gain: float32 [768], replicated, may hold values from 0.5 to 1.5
- ln2_bias: float32 [768], replicated, may hold values from -2 to 2
- expert_in: bfloat16 [8, 768, 3072], P('expert'), may hold values from -0.21875 to 0.21875
- expert_out: bfloat16 [8, 3072, 768], P('expert'), may hold values from -0.109375 to 0.109375
- out_grad: bfloat16 [32768, 768], P(('dp', 'expert'))
Outputs:
- block_out: bfloat16 [32768, 768], P(('dp', 'expert'))
- input_grad: float32 [32768, 768], P(('dp', 'expert'))
- ln1_gain_grad: float32 [768], replicated
- ln1_bias_grad: float32 [768], replicated
- qkv_grad: float32 [768, 2304], replicated
- proj_grad: float32 [768, 768], replicated
- ln2_gain_grad: float32 [768], replicated
- ln2_bias_grad: float32 [768], replicated
- expert_in_grad: float32 [8, 768, 3072], P('expert')
- expert_out_grad: float32 [8, 3072, 768], P('expert')
- load: float32 [8], replicated
The draws below stay inside these ranges and needn't reach their ends.
Inputs may be any that keep to these rules, and one draw needn't show every extreme that they name: hash_table[v] is the expert of token id v; every expert is the expert of 50257 // 8 ids or more. `token_ids`: of the 1024 tokens of one device at most 256 have the same expert; one expert has exactly 256 tokens on every device. `segment_ids`: within each sequence of 1024 tokens the ids start at 0, never fall and end at 8; no new document starts between places 1024 // 4 and 768 of a sequence.
All inputs are finite; a program needn't handle non-finite values.
Results may differ from the reference program's by a relative error of at most 0.0095.
Values may be sent and summed in bfloat16 or wider, within the bound.
No kernel may reach another device: no remote copies, remote signals or barrier semaphores. Data moves between devices by JAX's collectives and lax.ppermute only.
A program may use at most 320 MiB of HBM per device.

```python
import jax
import jax.numpy as jnp
from jax import lax

D = 768
HEADS = 12
HEAD = 64
FF = 3072
VOCAB = 50257
TOK_DEV = 1024
SEQ_LEN = 1024
EXPERTS = 8
CAP = 256
TOKENS = 32768


def vocab_order(key):
    return jax.random.permutation(jax.random.fold_in(key, 101), VOCAB)


def draw_hash_table(key, part):
    order = vocab_order(key)
    ranks = jnp.arange(VOCAB, dtype=jnp.int32) % EXPERTS
    return jnp.zeros((VOCAB,), jnp.int32).at[order].set(ranks)


def draw_token_ids(key, part):
    order = vocab_order(key)
    key = jax.random.fold_in(key, 2)
    device_count = TOKENS // TOK_DEV
    others = EXPERTS - 1
    rest = TOK_DEV - CAP
    first_tier = rest // 2
    tier_size = others // 3
    hot = jax.random.randint(jax.random.fold_in(key, 7), (), 0, EXPERTS)
    slot = jnp.arange(TOK_DEV, dtype=jnp.int32)
    offset = jnp.maximum(slot - CAP, 0)
    rank = jnp.where(offset < first_tier, offset % tier_size, tier_size + (offset - first_tier) % (others - tier_size))

    def one_block(block_key):
        shuffle = jax.random.permutation(jax.random.fold_in(block_key, 1), others)
        expert = jnp.where(slot < CAP, hot, (hot + 1 + shuffle[rank]) % EXPERTS)
        expert = expert[jax.random.permutation(jax.random.fold_in(block_key, 2), TOK_DEV)]
        pick = jax.random.randint(jax.random.fold_in(block_key, 3), (TOK_DEV,), 0, VOCAB // EXPERTS)
        return order[expert + EXPERTS * pick].astype(jnp.int32)
    block_keys = jax.random.split(jax.random.fold_in(key, 9), device_count)
    return jax.vmap(one_block)(block_keys).reshape(-1)


def draw_segment_ids(key, part):
    key = jax.random.fold_in(key, 3)
    seq_count = TOKENS // SEQ_LEN
    quarter = SEQ_LEN // 4
    early = jax.random.randint(jax.random.fold_in(key, 1), (seq_count, 4), 1, quarter)
    late = jax.random.randint(jax.random.fold_in(key, 2), (seq_count, 4), 3 * quarter, SEQ_LEN)
    cuts = jnp.concatenate([early, late], 1)
    position = jnp.arange(SEQ_LEN, dtype=jnp.int32)
    seg = jnp.sum((cuts[:, None, :] <= position[None, :, None]).astype(jnp.int32), -1)
    return seg.reshape(-1).astype(jnp.int32)


def draw_out_grad(key, part):
    key = jax.random.fold_in(key, 4)
    position = jnp.arange(TOKENS, dtype=jnp.float32)
    rise = 3.0 ** (position / (TOKENS - 1))
    base = jax.random.normal(jax.random.fold_in(key, 1), (TOKENS, D), jnp.float32)
    return (base * rise[:, None]).astype(jnp.bfloat16)


def level_of(key, dims, cuts, smallest, largest):
    loudness = 1.0
    for dim, shards_of in cuts:
        heights = jax.random.uniform(jax.random.fold_in(jax.random.fold_in(key, 6), dim), (shards_of,), jnp.float32, smallest / len(cuts), largest / len(cuts))
        loudness = loudness * jnp.repeat(jnp.exp(heights), dims[dim] // shards_of).reshape((-1,) + (1,) * (len(dims) - 1 - dim))
    return loudness


def gaussian(rng, shape, scale, limit, pieces=(), kind=jnp.bfloat16):
    entries = scale * jax.random.normal(rng, shape, jnp.float32)
    if pieces:
        entries = entries * level_of(rng, shape, pieces, -0.22, 0.18)
    return jnp.clip(entries, -limit, limit).astype(kind)


def setup_inputs(seed: int = 0) -> dict:
    splits = jax.random.split(jax.random.key(seed), 14)
    return {
        "hidden_in": gaussian(splits[0], (TOKENS, D), 1.0, 6.0, ((0, 32),)),
        "token_ids": draw_token_ids(jax.random.fold_in(splits[13], 71), 0),
        "hash_table": draw_hash_table(jax.random.fold_in(splits[13], 71), 0),
        "segment_ids": draw_segment_ids(jax.random.fold_in(splits[13], 71), 0),
        "ln1_gain": jnp.clip(1.0 + 0.1 * jax.random.normal(splits[4], (D,), jnp.float32), 0.5, 1.5),
        "ln1_bias": gaussian(splits[5], (D,), 0.3, 2.0, (), jnp.float32),
        "qkv_weight": gaussian(splits[6], (D, 3 * D), D ** -0.5, 0.21875),
        "proj_weight": gaussian(splits[7], (D, D), (D // 16) ** -0.5, 0.875),
        "ln2_gain": jnp.clip(1.0 + 0.1 * jax.random.normal(splits[8], (D,), jnp.float32), 0.5, 1.5),
        "ln2_bias": gaussian(splits[9], (D,), 0.3, 2.0, (), jnp.float32),
        "expert_in": gaussian(splits[10], (EXPERTS, D, FF), D ** -0.5, 0.21875, ((0, 8),)),
        "expert_out": gaussian(splits[11], (EXPERTS, FF, D), FF ** -0.5, 0.109375, ((0, 8),)),
        "out_grad": draw_out_grad(jax.random.fold_in(splits[13], 71), 0),
    }


@jax.custom_vjp
def low(v):
    return lax.optimization_barrier(v.astype(jnp.bfloat16)).astype(jnp.float32)

@jax.custom_vjp
def low_back(v):
    return v

def low_keep(v):
    return (low(v), None)

def low_pass(kept, grad):
    return (grad,)

def back_keep(v):
    return (v, None)

def back_low(kept, grad):
    return (low(grad),)
low.defvjp(low_keep, low_pass)
low_back.defvjp(back_keep, back_low)
EPSILON = 1e-05
HIGHEST = lax.Precision.HIGHEST

def layer_norm(values_in, gain, bias):
    centred = values_in - lax.optimization_barrier(jnp.mean(values_in, -1, keepdims=True))
    spread = lax.optimization_barrier(jnp.mean(centred * centred, -1, keepdims=True))
    return centred * lax.rsqrt(spread + EPSILON) * gain + bias

def rotate(tensor, position):
    half = HEAD // 2
    freq = 10000.0 ** (-jnp.arange(half, dtype=jnp.float32) / half)
    angle = position.astype(jnp.float32)[:, None] * freq[None, :]
    cosine = jnp.cos(angle)[:, None, :]
    sine = jnp.sin(angle)[:, None, :]
    first = tensor[..., :half]
    second = tensor[..., half:]
    return jnp.concatenate([first * cosine - second * sine, second * cosine + first * sine], -1)

def attend(raw_seq, seg_seq):
    length = raw_seq.shape[0]
    position = jnp.arange(length, dtype=jnp.int32)
    split = raw_seq.reshape(length, 3, HEADS, HEAD)
    query = low(rotate(split[:, 0], position))
    keys = low(rotate(split[:, 1], position))
    values = low(split[:, 2])
    scores = low_back(jnp.einsum('qhd,khd->hqk', query, keys, precision=HIGHEST) * 0.125)
    allowed = (position[None, :] <= position[:, None]) & (seg_seq[None, :] == seg_seq[:, None])
    scores = jnp.where(allowed[None], scores, -1e+30)
    weights = low(jax.nn.softmax(scores, axis=-1))
    mixed = jnp.einsum('hqk,khd->qhd', weights, values, precision=HIGHEST)
    return mixed.reshape(length, D)

def reference(hidden_in, token_ids, hash_table, segment_ids, ln1_gain, ln1_bias, qkv_weight, proj_weight, ln2_gain, ln2_bias, expert_in, expert_out, out_grad):
    chosen = hash_table[token_ids].astype(jnp.int32)
    order = jnp.argsort(chosen, stable=True).astype(jnp.int32)
    inverse = jnp.argsort(order).astype(jnp.int32)
    counts = lax.optimization_barrier(jnp.sum((chosen[:, None] == jnp.arange(EXPERTS, dtype=jnp.int32)[None, :]).astype(jnp.int32), 0))
    starts = (jnp.cumsum(counts) - counts).astype(jnp.int32)
    capacity_rows = 2 * TOKENS // EXPERTS
    seg_seqs = segment_ids.reshape(-1, SEQ_LEN)
    tags = jnp.concatenate([chosen[order], jnp.full((capacity_rows,), -1, jnp.int32)])
    slots = (starts[:, None] + jnp.arange(capacity_rows, dtype=jnp.int32)[None, :]).reshape(-1)

    def run_experts(h_two, weight_in, weight_out):
        padded = jnp.concatenate([h_two[order], jnp.zeros((capacity_rows, D), jnp.float32)])

        def per_expert(index):
            window = lax.dynamic_slice_in_dim(padded, starts[index], capacity_rows, 0)
            owned = (lax.dynamic_slice_in_dim(tags, starts[index], capacity_rows, 0) == index).astype(jnp.float32)
            inner = low_back(jnp.dot(window, weight_in[index], precision=HIGHEST))
            activated = low(jax.nn.gelu(inner))
            return jnp.dot(activated, weight_out[index], precision=HIGHEST) * owned[:, None]
        produced = lax.map(jax.checkpoint(per_expert), jnp.arange(EXPERTS, dtype=jnp.int32))
        sorted_out = jnp.zeros((TOKENS + capacity_rows, D), jnp.float32).at[slots].add(produced.reshape(-1, D))
        return sorted_out[inverse]

    def forward(hidden, gain_one, bias_one, weight_qkv, weight_proj, gain_two, bias_two, weight_in, weight_out):
        h_one = low(layer_norm(hidden, gain_one, bias_one))
        raw = low_back(jnp.dot(h_one, weight_qkv, precision=HIGHEST))
        raw_seqs = raw.reshape(-1, SEQ_LEN, 3 * D)
        mixed = lax.map(jax.checkpoint(lambda packed: attend(packed[0], packed[1])), (raw_seqs, seg_seqs))
        mixed = low(low_back(mixed.reshape(-1, D)))
        branch = low_back(jnp.dot(mixed, weight_proj, precision=HIGHEST))
        middle = hidden + branch
        h_two = low(low_back(layer_norm(middle, gain_two, bias_two)))
        result = low(low_back(run_experts(h_two, weight_in, weight_out)))
        return middle + result
    params = (hidden_in.astype(jnp.float32), ln1_gain.astype(jnp.float32), ln1_bias.astype(jnp.float32), qkv_weight.astype(jnp.float32), proj_weight.astype(jnp.float32), ln2_gain.astype(jnp.float32), ln2_bias.astype(jnp.float32), expert_in.astype(jnp.float32), expert_out.astype(jnp.float32))
    block_out, pull = jax.vjp(forward, *params)
    grads = pull(out_grad.astype(jnp.float32))
    load = counts.astype(jnp.float32) * (EXPERTS / TOKENS)
    return (block_out.astype(jnp.bfloat16), grads[0], grads[1], grads[2], grads[3], grads[4], grads[5], grads[6], grads[7], grads[8], load)
```

```python
import functools
import numpy as np
import jax
import jax.numpy as jnp
from jax import lax
from jax.experimental import pallas as pl
from jax.experimental.pallas import tpu as pltpu
from jax.sharding import PartitionSpec as P

HEAD = 64
EPSILON = 1e-05
BF = jnp.bfloat16
F32 = jnp.float32
I32 = jnp.int32
PAIR = 2 * HEAD
NEG = -1e30


def params(mib):
    return pltpu.CompilerParams(vmem_limit_bytes=mib << 20)


def cost(flops, bytes_accessed, transcendentals=0):
    return pl.CostEstimate(flops=1, bytes_accessed=1, transcendentals=0)


def dot(left, right, left_dim=1, right_dim=0):
    return lax.dot_general(
        left, right, (((left_dim,), (right_dim,)), ((), ())), preferred_element_type=F32
    )


def whole(shape):
    return pl.BlockSpec(shape, lambda *_: (0,) * len(shape))


def iota(shape, dim):
    return lax.broadcasted_iota(I32, shape, dim)


def norm_parts(rows):
    centred = rows - jnp.mean(rows, -1, keepdims=True)
    inv_scale = lax.rsqrt(jnp.mean(centred * centred, -1, keepdims=True) + EPSILON)
    return centred * inv_scale, inv_scale


def norm_back(grad_out, normed, inv_scale, gain):
    scaled = grad_out * gain
    centre = jnp.mean(scaled, -1, keepdims=True)
    along = jnp.mean(scaled * normed, -1, keepdims=True)
    return inv_scale * (scaled - centre - normed * along)


def one_hot_rows(target, first, count):
    return (iota((count, target.shape[1]), 0) + first == target).astype(F32).astype(BF)


def route_kernel(experts, half, block, ids_ref, table_ref, grad_ref, target_ref, counts_ref, sent_ref, place):
    tokens = ids_ref.shape[1]
    rows = table_ref.shape[0]
    padded = counts_ref.shape[0]
    step = pl.program_id(0)

    @pl.when(step == 0)
    def _():
        ids = ids_ref[...]
        picked = (iota((rows, tokens), 0) == (ids >> 7)).astype(F32).astype(BF)
        found = dot(table_ref[...], picked, 0, 0)
        chosen = jnp.sum(
            jnp.where(iota((128, tokens), 0) == (ids & 127), found, 0.0), 0, keepdims=True
        ).astype(I32)
        member = (iota((padded, tokens), 0) == chosen).astype(F32)
        earlier = (iota((tokens, tokens), 0) < iota((tokens, tokens), 1)).astype(F32).astype(BF)
        rank = dot(member.astype(BF), earlier)
        slot = jnp.sum(member * rank, 0, keepdims=True).astype(I32)
        place[...] = chosen * (2 * half) + slot
        later = (slot >= half).astype(I32)
        target_ref[...] = later * (experts * half) + chosen * half + slot - later * half
        counts_ref[...] = jnp.broadcast_to(jnp.sum(member, 1, keepdims=True), counts_ref.shape)

    sent_ref[...] = dot(one_hot_rows(place[...], step * block, block), grad_ref[...]).astype(BF)


def route(token_ids, hash_table, out_grad, experts, half):
    tokens, width = out_grad.shape
    slots = 2 * tokens
    block = 256
    padded = max(experts, 16)
    rows = -(-hash_table.shape[0] // (128 * 128)) * 128
    table = jnp.pad(hash_table, (0, rows * 128 - hash_table.shape[0])).reshape(rows, 128).astype(BF)
    target, counts, sent = pl.pallas_call(
        functools.partial(route_kernel, experts, half, block),
        name="route",
        grid=(slots // block,),
        in_specs=[whole((1, tokens)), whole((rows, 128)), whole((tokens, width))],
        out_specs=[
            whole((1, tokens)),
            whole((padded, 128)),
            pl.BlockSpec((block, width), lambda s: (s, 0)),
        ],
        out_shape=[
            jax.ShapeDtypeStruct((1, tokens), I32),
            jax.ShapeDtypeStruct((padded, 128), F32),
            jax.ShapeDtypeStruct((slots, width), BF),
        ],
        scratch_shapes=[pltpu.VMEM((1, tokens), I32)],
        compiler_params=params(40),
        cost_estimate=cost(2 * slots * tokens * width, 8 * tokens * width),
    )(token_ids.reshape(1, tokens), table, out_grad)
    return target, counts[:experts, 0], sent


def swap_halves(rows):
    half = HEAD // 2
    width = rows.shape[1]
    low = (iota(rows.shape, 1) & half) == 0
    return jnp.where(low, pltpu.roll(rows, width - half, 1), pltpu.roll(rows, half, 1))


def pre_kernel(x_ref, gain_ref, bias_ref, weight_ref, cos_ref, sin_ref, qkv_ref, h_ref):
    width = x_ref.shape[1]
    normed, _ = norm_parts(x_ref[...].astype(F32))
    h_one = (normed * gain_ref[...] + bias_ref[...]).astype(BF)
    h_ref[...] = h_one
    cosine, sine = cos_ref[...], sin_ref[...]
    for part in range(3):
        raw = dot(h_one, weight_ref[:, part * width : (part + 1) * width])
        for pair in range(width // PAIR):
            piece = raw[:, pair * PAIR : (pair + 1) * PAIR]
            if part < 2:
                piece = piece * cosine + swap_halves(piece) * sine
            if part == 0:
                piece = piece * 0.125
            start = part * width + pair * PAIR
            qkv_ref[:, start : start + PAIR] = piece.astype(BF)


def angle_tables(tokens):
    half = HEAD // 2
    freq = np.float32(10000.0) ** (-np.arange(half, dtype=np.float32) / np.float32(half))
    angle = np.arange(tokens, dtype=np.float32)[:, None] * freq[None, :].astype(np.float32)
    cosine = np.cos(angle).astype(np.float32)
    sine = np.sin(angle).astype(np.float32)
    cosine = np.concatenate([cosine, cosine], 1)
    sine = np.concatenate([-sine, sine], 1)
    return np.concatenate([cosine, cosine], 1), np.concatenate([sine, sine], 1)


def first_half(x, gain, bias, weight, cosine, sine):
    tokens, width = x.shape
    block = 256
    row = lambda w: pl.BlockSpec((block, w), lambda s: (s, 0))
    return pl.pallas_call(
        pre_kernel,
        name="norm_project",
        grid=(tokens // block,),
        in_specs=[
            row(width), whole((1, width)), whole((1, width)), whole(weight.shape), row(PAIR), row(PAIR),
        ],
        out_specs=[row(3 * width), row(width)],
        out_shape=[
            jax.ShapeDtypeStruct((tokens, 3 * width), BF),
            jax.ShapeDtypeStruct((tokens, width), BF),
        ],
        compiler_params=params(40),
        cost_estimate=cost(6 * tokens * width * width, 6 * width * width + 12 * tokens * width),
    )(x, gain, bias, weight, cosine, sine)


def head_lanes(rows, head):
    return jnp.where((iota((1, PAIR), 1) >= HEAD) == bool(head), rows, jnp.zeros_like(rows))


def attend_kernel(block, q_ref, k_ref, v_ref, seg_row_ref, seg_col_ref, mixed_ref, lse_ref, stats):
    tokens = q_ref.shape[0]
    pair = pl.program_id(0)
    upper = iota((1, PAIR), 1) >= HEAD
    for first in range(0, tokens, block):
        last = first + block
        query = q_ref[first:last, :]
        allowed = seg_col_ref[first:last, :] == seg_row_ref[:, :last]
        allowed &= iota((block, last), 1) <= iota((block, last), 0) + first
        halves = []
        for head in range(2):
            scores = dot(head_lanes(query, head), k_ref[:last, :], 1, 1)
            scores = jnp.where(allowed, scores, NEG)
            top = jnp.max(scores, -1, keepdims=True)
            weights = jnp.exp(scores - top)
            total = jnp.sum(weights, -1, keepdims=True)
            halves.append(dot(weights.astype(BF), v_ref[:last, :]) * (1.0 / total))
            lane = iota((1, 128), 1) == 2 * pair + head
            stats[first:last, :] = jnp.where(lane, top + jnp.log(total), stats[first:last, :])
        mixed_ref[first:last, :] = jnp.where(upper, halves[1], halves[0]).astype(BF)

    @pl.when(pair == pl.num_programs(0) - 1)
    def _():
        lse_ref[...] = stats[...].T


def attend(qkv, seg_row, seg_col):
    tokens, width = qkv.shape[0], qkv.shape[1] // 3
    pairs = width // PAIR
    column = lambda part: pl.BlockSpec((tokens, PAIR), lambda g: (0, part * pairs + g))
    return pl.pallas_call(
        functools.partial(attend_kernel, 256),
        name="attend",
        grid=(pairs,),
        in_specs=[column(0), column(1), column(2), whole((1, tokens)), whole((tokens, 1))],
        out_specs=[column(0), whole((128, tokens))],
        out_shape=[
            jax.ShapeDtypeStruct((tokens, width), BF),
            jax.ShapeDtypeStruct((128, tokens), F32),
        ],
        scratch_shapes=[pltpu.VMEM((tokens, 128), F32)],
        compiler_params=params(40),
        cost_estimate=cost(8 * tokens * tokens * width, 8 * tokens * width, tokens * tokens * width // HEAD),
    )(qkv, qkv, qkv, seg_row, seg_col)


def middle_kernel(block, mixed_ref, weight_ref, x_ref, gain_ref, bias_ref, target_ref, middle_ref, sent_ref, h_two):
    tokens = x_ref.shape[0]
    step = pl.program_id(0)

    @pl.when(step == 0)
    def _():
        for first in range(0, tokens, block):
            rows = slice(first, first + block)
            middle = x_ref[rows, :].astype(F32) + dot(mixed_ref[rows, :], weight_ref[...])
            middle_ref[rows, :] = middle
            normed, _ = norm_parts(middle)
            h_two[rows, :] = (normed * gain_ref[...] + bias_ref[...]).astype(BF)

    sent_ref[...] = dot(one_hot_rows(target_ref[...], step * block, block), h_two[...]).astype(BF)


def middle_part(mixed, weight, x, gain, bias, target):
    tokens, width = x.shape
    block = 256
    slots = 2 * tokens
    return pl.pallas_call(
        functools.partial(middle_kernel, block),
        name="project_dispatch",
        grid=(slots // block,),
        in_specs=[
            whole((tokens, width)), whole(weight.shape), whole((tokens, width)),
            whole((1, width)), whole((1, width)), whole((1, tokens)),
        ],
        out_specs=[whole((tokens, width)), pl.BlockSpec((block, width), lambda s: (s, 0))],
        out_shape=[
            jax.ShapeDtypeStruct((tokens, width), F32),
            jax.ShapeDtypeStruct((slots, width), BF),
        ],
        scratch_shapes=[pltpu.VMEM((tokens, width), BF)],
        compiler_params=params(40),
        cost_estimate=cost(2 * slots * tokens * width + 2 * tokens * width * width, 16 * tokens * width),
    )(mixed, weight, x, gain, bias, target)


ROOT = 0.7978845608028654
CUBE = 0.044715


def once(shape):
    return pl.BlockSpec(shape, lambda *_: (0,) * len(shape), pipeline_mode=pl.Buffered(1))


def slope_kernel(grads_ref, wout_ref, out_ref):
    experts, rows, width = grads_ref.shape
    half = rows // 2
    for chunk in range(2):
        grads = grads_ref[:, chunk * half : (chunk + 1) * half, :].reshape(experts * half, width)
        out_ref[chunk * experts * half : (chunk + 1) * experts * half, :] = dot(grads, wout_ref[...], 1, 1)


def grads_inside(grads, weight_out):
    experts, rows, width = grads.shape
    count = experts * rows
    units = weight_out.shape[0]
    tile = 512
    return pl.pallas_call(
        slope_kernel,
        name="grads_inside",
        grid=(units // tile,),
        in_specs=[once(grads.shape), pl.BlockSpec((tile, width), lambda s: (s, 0))],
        out_specs=pl.BlockSpec((count, tile), lambda s: (0, s)),
        out_shape=jax.ShapeDtypeStruct((count, units), F32),
        compiler_params=params(48),
        cost_estimate=cost(2 * count * width * units, 4 * count * units),
    )(grads, weight_out)


def expert_kernel(block, has_previous, groups, perm_ref, rows_ref, grads_ref, slope_ref, win_ref, *refs):
    refs = list(refs)
    previous_ref = refs.pop(0) if has_previous else None
    act_ref, back_ref, back = refs[-3:]
    grad_refs = refs[:-3]
    count, width = rows_ref.shape
    step = pl.program_id(0)

    @pl.when(step == 0)
    def _():
        back[...] = jnp.zeros_like(back)

    weight_in = win_ref[...]
    all_grads = grads_ref[...].reshape(count, width)
    din = dout = None
    for first in range(0, count, block):
        span = slice(first, first + block)
        rows, grads = rows_ref[span, :], all_grads[span, :]
        inner = dot(rows, weight_in)
        square = inner * inner
        tanh = jnp.tanh(inner * (ROOT + (ROOT * CUBE) * square))
        gate = 0.5 + 0.5 * tanh
        act = inner * gate
        slope = gate + act * (1.0 - tanh) * (ROOT + (3.0 * ROOT * CUBE) * square)
        act = act.astype(BF)
        act_ref[span, :] = act
        grad_inner = (slope_ref[span, :] * slope).astype(BF)
        back[span, :] += dot(grad_inner, weight_in, 1, 1)
        part_in = dot(rows, grad_inner, 0, 0)
        part_out = dot(act, grads, 0, 0)
        din = part_in if din is None else din + part_in
        dout = part_out if dout is None else dout + part_out
    if has_previous:
        din = din + previous_ref[0, 0]
        dout = dout + previous_ref[0, 1]
        swap = perm_ref[groups + step % 2] == 1
        early = jnp.where(swap, din, dout).astype(BF)
        late = jnp.where(swap, dout, din).astype(BF)
        keep_ref = grad_refs[4]
        for group in range(2):

            @pl.when(step == group)
            def _():
                grad_refs[2 * group][...] = early
                grad_refs[2 * group + 1][...] = late

        @pl.when(step >= 2)
        def _():
            keep_ref[0, 0] = early
            keep_ref[0, 1] = late
    else:
        grad_refs[0][0, 0] = din
        grad_refs[0][0, 1] = dout

    @pl.when(step == groups - 1)
    def _():
        back_ref[...] = back[...].astype(BF)


def expert_rows(chunk, rows, grads, slopes, weight_in, perm, previous=None):
    count, width = rows.shape
    experts, slots, _ = grads.shape
    groups = 4
    units = weight_in.shape[1]
    tile = units // groups
    grad_spec = pl.BlockSpec((1, 2, tile, width), lambda s, perm: (s, 0, 0, 0))
    in_specs = [
        once((count, width)),
        pl.BlockSpec((experts, slots // 2, width), lambda s, perm: (0, chunk, 0), pipeline_mode=pl.Buffered(1)),
        pl.BlockSpec((count, tile), lambda s, perm: (chunk, perm[s])),
        pl.BlockSpec((width, tile), lambda s, perm: (0, perm[s])),
    ]
    operands = [rows, grads, slopes, weight_in]
    if previous is None:
        grad_specs = [grad_spec]
        grad_shapes = [jax.ShapeDtypeStruct((groups, 2, tile, width), F32)]
    else:
        in_specs.append(grad_spec)
        operands.append(previous)
        grad_specs = [
            *([once((tile, width))] * 4),
            pl.BlockSpec((1, 2, tile, width), lambda s, perm: (jnp.maximum(s - 2, 0), 0, 0, 0)),
        ]
        grad_shapes = [jax.ShapeDtypeStruct((tile, width), BF)] * 4
        grad_shapes += [jax.ShapeDtypeStruct((2, 2, tile, width), BF)]
    return pl.pallas_call(
        functools.partial(expert_kernel, 512, previous is not None, groups),
        name="expert_rows",
        grid_spec=pltpu.PrefetchScalarGridSpec(
            num_scalar_prefetch=1,
            grid=(groups,),
            in_specs=in_specs,
            out_specs=grad_specs
            + [pl.BlockSpec((count, tile), lambda s, perm: (0, perm[s])), whole((count, width))],
            scratch_shapes=[pltpu.VMEM((count, width), F32)],
        ),
        out_shape=grad_shapes
        + [jax.ShapeDtypeStruct((count, units), BF), jax.ShapeDtypeStruct((count, width), BF)],
        compiler_params=params(60),
        cost_estimate=cost(8 * count * width * units, 12 * width * units + 6 * count * units, count * units),
    )(perm, *operands)


def result_kernel(act_ref, wout_ref, out_ref, total):
    step = pl.program_id(0)

    @pl.when(step == 0)
    def _():
        total[...] = jnp.zeros_like(total)

    total[...] += dot(act_ref[...], wout_ref[...])

    @pl.when(step == pl.num_programs(0) - 1)
    def _():
        out_ref[...] = total[...].astype(BF)


def expert_result(act, weight_out):
    count, units = act.shape
    width = weight_out.shape[1]
    tile = 768
    return pl.pallas_call(
        result_kernel,
        name="expert_result",
        grid=(units // tile,),
        in_specs=[pl.BlockSpec((count, tile), lambda s: (0, s)), pl.BlockSpec((tile, width), lambda s: (s, 0))],
        out_specs=whole((count, width)),
        out_shape=jax.ShapeDtypeStruct((count, width), BF),
        scratch_shapes=[pltpu.VMEM((count, width), F32)],
        compiler_params=params(48),
        cost_estimate=cost(2 * count * width * units, 2 * count * units),
    )(act, weight_out)


def assemble_kernel(flags_ref, *refs):
    sources, (in_ref, out_ref) = refs[:8], refs[8:]
    step = pl.program_id(0)
    for group in range(4):
        first, second = sources[2 * group], sources[2 * group + 1]
        flag = flags_ref[4 + group // 2]

        @pl.when((step == group) & (flag == 0))
        def _():
            in_ref[...] = first[...].astype(F32)
            out_ref[...] = second[...].astype(F32)

        @pl.when((step == group) & (flag != 0))
        def _():
            in_ref[...] = second[...].astype(F32)
            out_ref[...] = first[...].astype(F32)


def assemble(flags, sources):
    tile, width = sources[0].shape
    return pl.pallas_call(
        assemble_kernel,
        name="assemble",
        grid_spec=pltpu.PrefetchScalarGridSpec(
            num_scalar_prefetch=1,
            grid=(4,),
            in_specs=[whole((tile, width))] * 8,
            out_specs=[
                pl.BlockSpec((tile, width), lambda s, flags: (0, flags[s])),
                pl.BlockSpec((tile, width), lambda s, flags: (flags[s], 0)),
            ],
        ),
        out_shape=[
            jax.ShapeDtypeStruct((width, 4 * tile), F32),
            jax.ShapeDtypeStruct((4 * tile, width), F32),
        ],
        compiler_params=params(48),
        cost_estimate=cost(8 * tile * width, 48 * tile * width),
    )(flags, *sources)


def gather_rows(block, target_ref, sources):
    count = sources[0].shape[0]
    target = target_ref[...]
    total = None
    for chunk, source in enumerate(sources):
        picked = (iota((block, count), 1) + chunk * count == target).astype(F32).astype(BF)
        part = dot(picked, source[...])
        total = part if total is None else total + part
    return total


def back_kernel(
    block, back_first_ref, back_second_ref, target_ref, middle_ref, mixed_ref, out_grad_ref, gain_ref, weight_ref, sel_ref,
    grad_middle_ref, grad_mixed_ref, branch_ref, delta_ref, small_ref,
):
    step = pl.program_id(0)
    grad_h = gather_rows(block, target_ref, (back_first_ref, back_second_ref))
    normed, inv_scale = norm_parts(middle_ref[...])
    gain = gain_ref[...]
    grad_middle = out_grad_ref[...].astype(F32) + norm_back(grad_h, normed, inv_scale, gain)
    grad_middle_ref[...] = grad_middle
    branch = grad_middle.astype(BF)
    branch_ref[...] = branch
    mixed = mixed_ref[...]
    grad_mixed = dot(branch, weight_ref[...], 1, 1).astype(BF)
    grad_mixed_ref[...] = grad_mixed
    product = grad_mixed.astype(F32) * mixed.astype(F32)
    high = product.astype(BF)
    low = (product - high.astype(F32)).astype(BF)
    sel = sel_ref[...]
    delta_ref[...] = dot(sel, high, 1, 1) + dot(sel, low, 1, 1)
    gain_grad = jnp.sum(grad_h * normed, 0, keepdims=True)
    bias_grad = jnp.sum(grad_h, 0, keepdims=True)

    @pl.when(step == 0)
    def _():
        small_ref[0:1, :] = gain_grad
        small_ref[1:2, :] = bias_grad

    @pl.when(step > 0)
    def _():
        small_ref[0:1, :] += gain_grad
        small_ref[1:2, :] += bias_grad


def middle_back(back_first, back_second, target_col, middle, mixed, out_grad, gain, weight):
    tokens, width = middle.shape
    slots = 2 * back_first.shape[0]
    block = 256
    heads = np.zeros((16, width), np.float32)
    for head in range(width // HEAD):
        heads[head, head * HEAD : (head + 1) * HEAD] = 1.0
    row = lambda w: pl.BlockSpec((block, w), lambda s: (s, 0))
    return pl.pallas_call(
        functools.partial(back_kernel, block),
        name="middle_back",
        grid=(tokens // block,),
        in_specs=[
            once((slots // 2, width)), once((slots // 2, width)), row(1), row(width), row(width), row(width),
            whole((1, width)), whole(weight.shape), whole((16, width)),
        ],
        out_specs=[
            row(width), row(width), row(width), pl.BlockSpec((16, block), lambda s: (0, s)),
            whole((8, width)),
        ],
        out_shape=[
            jax.ShapeDtypeStruct((tokens, width), F32),
            jax.ShapeDtypeStruct((tokens, width), BF),
            jax.ShapeDtypeStruct((tokens, width), BF),
            jax.ShapeDtypeStruct((16, tokens), F32),
            jax.ShapeDtypeStruct((8, width), F32),
        ],
        compiler_params=params(48),
        cost_estimate=cost(2 * slots * tokens * width + 4 * tokens * width * width, 24 * tokens * width),
    )(back_first, back_second, target_col, middle, mixed, out_grad, gain, weight, jnp.asarray(heads, BF))


def attend_back_kernel(
    block, start, q_ref, k_ref, v_ref, do_ref, lse_ref, delta_ref, seg_row_ref, seg_col_ref, cos_ref, sin_ref,
    dq_ref, dk_ref, dv_ref, total,
):
    tokens = q_ref.shape[0]
    pair = pl.program_id(0) + start
    cosine, sine = cos_ref[...], sin_ref[...]
    lse = [lse_ref[pl.ds(2 * pair + head, 1), :] for head in range(2)]
    delta = [delta_ref[pl.ds(2 * pair + head, 1), :] for head in range(2)]
    for first in range(0, tokens, block):
        last = first + block
        span = tokens - first
        keys, values = k_ref[first:last, :], v_ref[first:last, :]
        allowed = seg_col_ref[first:last, :] == seg_row_ref[:, first:]
        allowed &= iota((block, span), 0) <= iota((block, span), 1)
        dk = dv = dq = None
        for head in range(2):
            query = head_lanes(q_ref[first:, :], head)
            grads = head_lanes(do_ref[first:, :], head)
            scores = dot(keys, query, 1, 1)
            chance = jnp.where(allowed, jnp.exp(scores - lse[head][:, first:]), 0.0)
            grad_weights = dot(values, grads, 1, 1)
            grad_scores = (chance * (grad_weights - delta[head][:, first:])).astype(BF)
            part_v = dot(chance.astype(BF), grads)
            part_k = dot(grad_scores, query)
            part_q = dot(grad_scores, head_lanes(keys, head), 0, 0)
            dk = part_k if dk is None else dk + part_k
            dv = part_v if dv is None else dv + part_v
            dq = part_q if dq is None else dq + part_q
        dv_ref[first:last, :] = dv.astype(BF)
        cos_k, sin_k = cosine[first:last, :], sine[first:last, :]
        dk_ref[first:last, :] = (dk * cos_k - swap_halves(dk) * sin_k).astype(BF)
        if first == 0:
            total[...] = dq
        else:
            total[first:, :] += dq
    dq = total[...] * 0.125
    dq_ref[...] = (dq * cosine - swap_halves(dq) * sine).astype(BF)


def attend_back(qkv, grad_mixed, lse, delta, seg_row, seg_col, cosine, sine, start, count):
    tokens, width = grad_mixed.shape
    pairs = width // PAIR
    column = lambda part: pl.BlockSpec((tokens, PAIR), lambda g: (0, part * pairs + start + g))
    out = jax.ShapeDtypeStruct((tokens, count * PAIR), BF)
    return pl.pallas_call(
        functools.partial(attend_back_kernel, 256, start),
        name="attend_back",
        grid=(count,),
        in_specs=[
            column(0), column(1), column(2), column(0), whole(lse.shape), whole(delta.shape),
            whole((1, tokens)), whole((tokens, 1)), whole((tokens, PAIR)), whole((tokens, PAIR)),
        ],
        out_specs=[pl.BlockSpec((tokens, PAIR), lambda g: (0, g))] * 3,
        out_shape=[out] * 3,
        scratch_shapes=[pltpu.VMEM((tokens, PAIR), F32)],
        compiler_params=params(48),
        cost_estimate=cost(20 * tokens * tokens * PAIR * count, 14 * tokens * PAIR * count, 2 * tokens * tokens * count),
    )(qkv, qkv, qkv, grad_mixed, lse, delta, seg_row, seg_col, cosine, sine)


def shared_kernel(side_ref, h_ref, dq_ref, dk_ref, dv_ref, mixed_ref, branch_ref, keep_ref, send_ref):
    parts = [dot(h_ref[...], ref[...], 0, 0) for ref in (dq_ref, dk_ref, dv_ref)]
    parts.append(dot(mixed_ref[...], branch_ref[...], 0, 0))
    second = side_ref[0] == 1
    for part in range(2):
        keep_ref[part] = jnp.where(second, parts[2 + part], parts[part])
        send_ref[part] = jnp.where(second, parts[part], parts[2 + part]).astype(BF)


def shared_grads(side, h_one, grads, mixed, branch, which):
    tokens, width = h_one.shape
    columns = grads[0].shape[1]
    block = 256
    row = pl.BlockSpec((tokens, block), lambda s, side: (0, s))
    out = pl.BlockSpec((2, block, columns), lambda s, side: (0, s, 0))
    return pl.pallas_call(
        shared_kernel,
        name="shared_grads",
        grid_spec=pltpu.PrefetchScalarGridSpec(
            num_scalar_prefetch=1,
            grid=(width // block,),
            in_specs=[row] + [once((tokens, columns))] * 3
            + [row, pl.BlockSpec((tokens, columns), lambda s, side: (0, which), pipeline_mode=pl.Buffered(1))],
            out_specs=[out, out],
        ),
        out_shape=[
            jax.ShapeDtypeStruct((2, width, columns), F32),
            jax.ShapeDtypeStruct((2, width, columns), BF),
        ],
        compiler_params=params(40),
        cost_estimate=cost(8 * tokens * width * columns, 16 * width * columns + 12 * tokens * columns),
    )(side, h_one, *grads, mixed, branch)


def final_kernel(x_ref, *refs):
    grad_refs = refs[:6]
    grad_middle_ref, weight_ref, gain_ref, input_grad_ref, small_ref = refs[6:]
    step = pl.program_id(0)
    width = x_ref.shape[1]
    columns = grad_refs[0].shape[1]
    normed, inv_scale = norm_parts(x_ref[...].astype(F32))
    grad_h = None
    for index, ref in enumerate(grad_refs):
        start = (index % 3) * width + (index // 3) * columns
        piece = dot(ref[...], weight_ref[:, start : start + columns], 1, 1)
        grad_h = piece if grad_h is None else grad_h + piece
    input_grad_ref[...] = grad_middle_ref[...] + norm_back(grad_h, normed, inv_scale, gain_ref[...])
    gain_grad = jnp.sum(grad_h * normed, 0, keepdims=True)
    bias_grad = jnp.sum(grad_h, 0, keepdims=True)

    @pl.when(step == 0)
    def _():
        small_ref[0:1, :] = gain_grad
        small_ref[1:2, :] = bias_grad

    @pl.when(step > 0)
    def _():
        small_ref[0:1, :] += gain_grad
        small_ref[1:2, :] += bias_grad


def final_part(x, grads, grad_middle, weight, gain):
    tokens, width = x.shape
    columns = grads[0].shape[1]
    block = 256
    row = lambda w: pl.BlockSpec((block, w), lambda s: (s, 0))
    return pl.pallas_call(
        final_kernel,
        name="first_back",
        grid=(tokens // block,),
        in_specs=[row(width)] + [row(columns)] * 6 + [row(width), once(weight.shape), whole((1, width))],
        out_specs=[row(width), whole((8, width))],
        out_shape=[
            jax.ShapeDtypeStruct((tokens, width), F32),
            jax.ShapeDtypeStruct((8, width), F32),
        ],
        compiler_params=params(48),
        cost_estimate=cost(6 * tokens * width * width, 6 * width * width + 16 * tokens * width),
    )(x, *grads, grad_middle, weight, gain)


def output_kernel(block, first_ref, second_ref, target_ref, middle_ref, out_ref):
    out_ref[...] = (middle_ref[...] + gather_rows(block, target_ref, (first_ref, second_ref))).astype(BF)


def block_output(first, second, target_col, middle):
    tokens, width = middle.shape
    slots = 2 * first.shape[0]
    block = 256
    row = lambda w: pl.BlockSpec((block, w), lambda s: (s, 0))
    return pl.pallas_call(
        functools.partial(output_kernel, block),
        name="block_output",
        grid=(tokens // block,),
        in_specs=[once((slots // 2, width)), once((slots // 2, width)), row(1), row(width)],
        out_specs=row(width),
        out_shape=jax.ShapeDtypeStruct((tokens, width), BF),
        compiler_params=params(40),
        cost_estimate=cost(2 * slots * tokens * width, 10 * tokens * width),
    )(first, second, target_col, middle)


def partner(axis, bit):
    return [(i, i ^ bit) for i in range(lax.axis_size(axis))]


def side(axis, bit):
    return (lax.axis_index(axis) // bit) % 2


def axis_bits(axis):
    bits, bit = [], 1
    while bit < lax.axis_size(axis):
        bits.append((axis, bit))
        bit *= 2
    return bits


def reduce_step(total, axis, bit):
    if total.shape[0] == 1:
        total = total.astype(BF)
        return total.astype(F32) + lax.ppermute(total, axis, partner(axis, bit)).astype(F32)
    mine = side(axis, bit)
    half = total.shape[0] // 2
    keep = lax.dynamic_slice_in_dim(total, mine * half, half, 0)
    send = lax.dynamic_slice_in_dim(total, (1 - mine) * half, half, 0)
    return keep + lax.ppermute(send.astype(BF), axis, partner(axis, bit)).astype(F32)


def gather_step(total, axis, bit):
    got = lax.ppermute(total, axis, partner(axis, bit))
    return jnp.where(side(axis, bit) == 0, jnp.concatenate([total, got], 0), jnp.concatenate([got, total], 0))


def sum_small(rows):
    for axis, bit in axis_bits("expert") + axis_bits("dp"):
        rows = rows + lax.ppermute(rows, axis, partner(axis, bit))
    return rows


def local(
    hidden_in, token_ids, hash_table, segment_ids, ln1_gain, ln1_bias, qkv_weight, proj_weight,
    ln2_gain, ln2_bias, expert_in, expert_out, out_grad,
):
    tokens, width = hidden_in.shape
    experts = lax.axis_size("expert")
    devices = lax.axis_size("dp") * experts
    half = tokens // experts
    row = lambda vector: vector.reshape(1, width)
    cosine, sine = (jnp.asarray(table) for table in angle_tables(tokens))
    seg_row, seg_col = segment_ids.reshape(1, tokens), segment_ids.reshape(tokens, 1)
    weight_in, weight_out = expert_in[0], expert_out[0]

    def exchange(rows):
        sent = rows.reshape(experts, rows.shape[0] // experts, width)
        return lax.all_to_all(sent, "expert", split_axis=0, concat_axis=0, tiled=True)

    def exchange_half(rows):
        return exchange(rows).reshape(tokens, width)

    def split(rows):
        return rows[:tokens], rows[tokens:]

    x_side, y_side = side("dp", 1), side("dp", 2)
    perm = jnp.stack([1 - x_side, 3 - y_side, x_side, 2 + y_side, y_side, x_side]).astype(I32)
    tie = lambda *values: lax.optimization_barrier(values)

    target, counts, sent_grads = route(token_ids, hash_table, out_grad, experts, half)
    target_col = target.reshape(tokens, 1)
    sent_grads, hidden_in = tie(sent_grads, hidden_in)
    grad_rows = exchange(sent_grads)
    qkv, h_one = first_half(hidden_in, row(ln1_gain), row(ln1_bias), qkv_weight, cosine, sine)
    mixed, lse = attend(qkv, seg_row, seg_col)
    middle, sent_rows = middle_part(mixed, proj_weight, hidden_in, row(ln2_gain), row(ln2_bias), target)
    sent_first, sent_second = split(sent_rows)
    sent_first, grad_rows = tie(sent_first, grad_rows)
    rows_first = exchange_half(sent_first)
    slopes = grads_inside(grad_rows, weight_out)
    sent_second, rows_first, slopes = tie(sent_second, rows_first, slopes)
    rows_second = exchange_half(sent_second)

    previous, act_first, back_first = expert_rows(0, rows_first, grad_rows, slopes, weight_in, perm)
    back_first, rows_second = tie(back_first, rows_second)
    back_first = exchange_half(back_first)
    early_x, late_x, early_y, late_y, keep, act_second, back_second = expert_rows(
        1, rows_second, grad_rows, slopes, weight_in, perm, previous
    )
    across_x = lambda value: lax.ppermute(value, "dp", partner("dp", 1))
    across_y = lambda value: lax.ppermute(value, "dp", partner("dp", 2))
    back_second, back_first = tie(back_second, back_first)
    back_second = exchange_half(back_second)
    early_x, early_y = across_x(early_x), across_y(early_y)
    late_x, late_y = across_x(late_x), across_y(late_y)
    result_first = expert_result(act_first, weight_out)
    result_second = expert_result(act_second, weight_out)
    result_first, result_second, back_second, early_x, early_y = tie(
        result_first, result_second, back_second, early_x, early_y
    )

    plus = lambda *values: sum(value.astype(F32) for value in values).astype(BF)
    send_x, send_y = plus(keep[0, 0], early_x), plus(keep[1, 0], early_y)
    send_x, send_y, back_second = tie(send_x, send_y, back_second)
    other_x, other_y = across_y(send_x), across_x(send_y)
    grad_middle, grad_mixed, branch, delta, small_two = middle_back(
        back_first, back_second, target_col, middle, mixed, out_grad, row(ln2_gain), proj_weight
    )
    grad_mixed, late_x, late_y, result_first = tie(grad_mixed, late_x, late_y, result_first)
    result_first = exchange_half(result_first)

    pairs = width // PAIR
    back_of = lambda grads, start: attend_back(
        qkv, grads, lse, delta, seg_row, seg_col, cosine, sine, start, pairs // 2
    )
    core_side = jnp.reshape(side("expert", 1), (1,)).astype(I32)
    across_core = lambda value: lax.ppermute(value, "expert", partner("expert", 1))
    grads_low = back_of(grad_mixed, 0)
    low, send_low = shared_grads(core_side, h_one, grads_low, mixed, branch, 0)
    other_x, other_y, send_low, grad_mixed = tie(other_x, other_y, send_low, grad_mixed)
    total_x, total_y = plus(keep[0, 1], late_x, other_x), plus(keep[1, 1], late_y, other_y)
    total_x, total_y, grad_mixed = tie(total_x, total_y, grad_mixed)
    near_x, near_y = across_y(total_x), across_x(total_y)
    got_low = across_core(send_low)
    grads_high = back_of(grad_mixed, pairs // 2)
    high, send_high = shared_grads(core_side, h_one, grads_high, mixed, branch, 1)
    near_x, near_y, got_low, send_high, result_first = tie(near_x, near_y, got_low, send_high, result_first)
    result_second = exchange_half(result_second)
    far_x, far_y = across_x(total_x), across_y(total_y)

    low = (low + got_low.astype(F32)).reshape(8, width // 4, width // 2)
    high = (high + across_core(send_high).astype(F32)).reshape(8, width // 4, width // 2)
    far_bits = axis_bits("expert")[1:]
    low_order = axis_bits("dp") + far_bits
    high_order = axis_bits("dp")[::-1] + far_bits

    def reduce_both(low, high, step):
        return reduce_step(low, *low_order[step]), reduce_step(high, *high_order[step])

    low, high = reduce_both(low, high, 0)
    input_grad, small_one = final_part(
        hidden_in, list(grads_low) + list(grads_high), grad_middle, qkv_weight, row(ln1_gain)
    )
    low, high, far_x, far_y, small_one = tie(low, high, far_x, far_y, small_one)
    small = jnp.concatenate(
        [small_one[:2], small_two[:2], jnp.pad(counts, (0, width - experts))[None], jnp.zeros((3, width), F32)], 0
    )
    low, high = reduce_both(low, high, 1)
    low, high, small, near_x, near_y = tie(low, high, small, near_x, near_y)
    last_x, last_y = across_x(near_x), across_y(near_y)
    small = sum_small(small)
    for step in range(2, len(low_order)):
        low, high = reduce_both(low, high, step)
    block_out = block_output(result_first, result_second, target_col, middle)
    low, high, last_x, last_y, block_out, small = tie(low, high, last_x, last_y, block_out, small)
    sums_x = [total_x, near_x, far_x, last_x]
    sums_y = [total_y, near_y, far_y, last_y]
    flags = jnp.stack([x_side, 1 - x_side, 2 + y_side, 3 - y_side, y_side, x_side]).astype(I32)
    grad_in, grad_out = assemble(flags, sums_x + sums_y)
    low, high = low.astype(BF), high.astype(BF)
    for step in (2, 1, 0):
        low, high = gather_step(low, *low_order[step]), gather_step(high, *high_order[step])
        if step == 1:
            low, high, grad_in, grad_out = tie(low, high, grad_in, grad_out)
    low, high = gather_step(low, "expert", 1), gather_step(high, "expert", 1)
    low = low.reshape(4, width, width // 2).astype(F32)
    high = high.reshape(4, width, width // 2).astype(F32)
    qkv_grad = jnp.concatenate([low[0], high[0], low[1], high[1], low[2], high[2]], 1)
    proj_sum = jnp.concatenate([low[3], high[3]], 1)
    load = small[4, :experts] * (experts / (tokens * devices))
    return (
        block_out,
        input_grad,
        small[0],
        small[1],
        qkv_grad,
        proj_sum,
        small[2],
        small[3],
        grad_in[None],
        grad_out[None],
        load,
    )


def solution(mesh):
    split, copied, owned = P(("dp", "expert")), P(), P("expert")
    in_specs = (
        split, split, copied, split, copied, copied, copied, copied, copied, copied, owned, owned, split,
    )
    out_specs = (
        split, split, copied, copied, copied, copied, copied, copied, owned, owned, copied,
    )
    return jax.shard_map(local, mesh=mesh, in_specs=in_specs, out_specs=out_specs, check_vma=False)
```

```python
import functools
import numpy as np
import jax
import jax.numpy as jnp
from jax import lax
from jax.experimental import pallas as pl
from jax.experimental.pallas import tpu as pltpu
from jax.sharding import PartitionSpec as P

HEAD = 64
EPSILON = 1e-05
BF = jnp.bfloat16
F32 = jnp.float32
I32 = jnp.int32
PAIR = 2 * HEAD
NEG = -1e30


def params(mib):
    return pltpu.CompilerParams(vmem_limit_bytes=mib << 20)


def cost(flops, bytes_accessed, transcendentals=0):
    return pl.CostEstimate(flops=1, bytes_accessed=1, transcendentals=0)


def dot(left, right, left_dim=1, right_dim=0):
    return lax.dot_general(
        left, right, (((left_dim,), (right_dim,)), ((), ())), preferred_element_type=F32
    )


def whole(shape):
    return pl.BlockSpec(shape, lambda *_: (0,) * len(shape))


def iota(shape, dim):
    return lax.broadcasted_iota(I32, shape, dim)


def norm_parts(rows):
    centred = rows - jnp.mean(rows, -1, keepdims=True)
    inv_scale = lax.rsqrt(jnp.mean(centred * centred, -1, keepdims=True) + EPSILON)
    return centred * inv_scale, inv_scale


def norm_back(grad_out, normed, inv_scale, gain):
    scaled = grad_out * gain
    centre = jnp.mean(scaled, -1, keepdims=True)
    along = jnp.mean(scaled * normed, -1, keepdims=True)
    return inv_scale * (scaled - centre - normed * along)


def one_hot_rows(target, first, count):
    return (iota((count, target.shape[1]), 0) + first == target).astype(F32).astype(BF)


def route_kernel(experts, half, block, ids_ref, table_ref, grad_ref, target_ref, place, counts_ref, sent_ref):
    tokens = ids_ref.shape[1]
    rows = table_ref.shape[0]
    padded = counts_ref.shape[0]
    step = pl.program_id(0)

    @pl.when(step == 0)
    def _():
        ids = ids_ref[...]
        picked = (iota((rows, tokens), 0) == (ids >> 7)).astype(F32).astype(BF)
        found = dot(table_ref[...], picked, 0, 0)
        chosen = jnp.sum(
            jnp.where(iota((128, tokens), 0) == (ids & 127), found, 0.0), 0, keepdims=True
        ).astype(I32)
        member = (iota((padded, tokens), 0) == chosen).astype(F32)
        earlier = (iota((tokens, tokens), 0) < iota((tokens, tokens), 1)).astype(F32).astype(BF)
        rank = dot(member.astype(BF), earlier)
        slot = jnp.sum(member * rank, 0, keepdims=True).astype(I32)
        place[...] = chosen * (2 * half) + slot
        later = (slot >= half).astype(I32)
        target_ref[...] = later * (experts * half) + chosen * half + slot - later * half
        counts_ref[...] = jnp.broadcast_to(jnp.sum(member, 1, keepdims=True), counts_ref.shape)

    sent_ref[...] = dot(one_hot_rows(place[...], step * block, block), grad_ref[...]).astype(BF)


def route(token_ids, hash_table, out_grad, experts, half):
    tokens, width = out_grad.shape
    slots = 2 * tokens
    block = 256
    padded = max(experts, 16)
    rows = -(-hash_table.shape[0] // (128 * 128)) * 128
    table = jnp.pad(hash_table, (0, rows * 128 - hash_table.shape[0])).reshape(rows, 128).astype(BF)
    target, place, counts, sent = pl.pallas_call(
        functools.partial(route_kernel, experts, half, block),
        name="route",
        grid=(slots // block,),
        in_specs=[whole((1, tokens)), whole((rows, 128)), whole((tokens, width))],
        out_specs=[
            whole((1, tokens)),
            whole((1, tokens)),
            whole((padded, 128)),
            pl.BlockSpec((block, width), lambda s: (s, 0)),
        ],
        out_shape=[
            jax.ShapeDtypeStruct((1, tokens), I32),
            jax.ShapeDtypeStruct((1, tokens), I32),
            jax.ShapeDtypeStruct((padded, 128), F32),
            jax.ShapeDtypeStruct((slots, width), BF),
        ],
        compiler_params=params(62),
        cost_estimate=cost(2 * slots * tokens * width, 8 * tokens * width),
    )(token_ids.reshape(1, tokens), table, out_grad)
    return target, place, counts[:experts, 0], sent


def swap_halves(rows):
    half = HEAD // 2
    width = rows.shape[1]
    low = (iota(rows.shape, 1) & half) == 0
    return jnp.where(low, pltpu.roll(rows, width - half, 1), pltpu.roll(rows, half, 1))


def pre_kernel(x_ref, gain_ref, bias_ref, weight_ref, cos_ref, sin_ref, qkv_ref, h_ref):
    width = x_ref.shape[1]
    normed, _ = norm_parts(x_ref[...].astype(F32))
    h_one = (normed * gain_ref[...] + bias_ref[...]).astype(BF)
    h_ref[...] = h_one
    cosine, sine = cos_ref[...], sin_ref[...]
    for part in range(3):
        raw = dot(h_one, weight_ref[:, part * width : (part + 1) * width])
        for pair in range(width // PAIR):
            piece = raw[:, pair * PAIR : (pair + 1) * PAIR]
            if part < 2:
                piece = piece * cosine + swap_halves(piece) * sine
            if part == 0:
                piece = piece * 0.125
            start = part * width + pair * PAIR
            qkv_ref[:, start : start + PAIR] = piece.astype(BF)


def angle_tables(tokens):
    half = HEAD // 2
    freq = np.float32(10000.0) ** (-np.arange(half, dtype=np.float32) / np.float32(half))
    angle = np.arange(tokens, dtype=np.float32)[:, None] * freq[None, :].astype(np.float32)
    cosine = np.cos(angle).astype(np.float32)
    sine = np.sin(angle).astype(np.float32)
    cosine = np.concatenate([cosine, cosine], 1)
    sine = np.concatenate([-sine, sine], 1)
    return np.concatenate([cosine, cosine], 1), np.concatenate([sine, sine], 1)


def first_half(x, gain, bias, weight, cosine, sine):
    tokens, width = x.shape
    block = 256
    row = lambda w: pl.BlockSpec((block, w), lambda s: (s, 0))
    return pl.pallas_call(
        pre_kernel,
        name="norm_project",
        grid=(tokens // block,),
        in_specs=[
            row(width), whole((1, width)), whole((1, width)), whole(weight.shape), row(PAIR), row(PAIR),
        ],
        out_specs=[row(3 * width), row(width)],
        out_shape=[
            jax.ShapeDtypeStruct((tokens, 3 * width), BF),
            jax.ShapeDtypeStruct((tokens, width), BF),
        ],
        compiler_params=params(62),
        cost_estimate=cost(6 * tokens * width * width, 6 * width * width + 12 * tokens * width),
    )(x, gain, bias, weight, cosine, sine)


def head_lanes(rows, head):
    return jnp.where((iota((1, PAIR), 1) >= HEAD) == bool(head), rows, jnp.zeros_like(rows))


def attend_kernel(block, q_ref, k_ref, v_ref, seg_row_ref, seg_col_ref, mixed_ref, lse_ref, stats):
    tokens = q_ref.shape[0]
    pair = pl.program_id(0)
    upper = iota((1, PAIR), 1) >= HEAD
    for first in range(0, tokens, block):
        last = first + block
        query = q_ref[first:last, :]
        allowed = seg_col_ref[first:last, :] == seg_row_ref[:, :last]
        allowed &= iota((block, last), 1) <= iota((block, last), 0) + first
        halves = []
        for head in range(2):
            scores = dot(head_lanes(query, head), k_ref[:last, :], 1, 1)
            scores = jnp.where(allowed, scores, NEG)
            top = jnp.max(scores, -1, keepdims=True)
            weights = jnp.exp(scores - top)
            total = jnp.sum(weights, -1, keepdims=True)
            halves.append(dot(weights.astype(BF), v_ref[:last, :]) * (1.0 / total))
            lane = iota((1, 128), 1) == 2 * pair + head
            stats[first:last, :] = jnp.where(lane, top + jnp.log(total), stats[first:last, :])
        mixed_ref[first:last, :] = jnp.where(upper, halves[1], halves[0]).astype(BF)

    @pl.when(pair == pl.num_programs(0) - 1)
    def _():
        lse_ref[...] = stats[...].T


def attend(qkv, seg_row, seg_col):
    tokens, width = qkv.shape[0], qkv.shape[1] // 3
    pairs = width // PAIR
    column = lambda part: pl.BlockSpec((tokens, PAIR), lambda g: (0, part * pairs + g))
    return pl.pallas_call(
        functools.partial(attend_kernel, 256),
        name="attend",
        grid=(pairs,),
        in_specs=[column(0), column(1), column(2), whole((1, tokens)), whole((tokens, 1))],
        out_specs=[column(0), whole((128, tokens))],
        out_shape=[
            jax.ShapeDtypeStruct((tokens, width), BF),
            jax.ShapeDtypeStruct((128, tokens), F32),
        ],
        scratch_shapes=[pltpu.VMEM((tokens, 128), F32)],
        compiler_params=params(62),
        cost_estimate=cost(8 * tokens * tokens * width, 8 * tokens * width, tokens * tokens * width // HEAD),
    )(qkv, qkv, qkv, seg_row, seg_col)


def middle_kernel(block, mixed_ref, weight_ref, x_ref, gain_ref, bias_ref, target_ref, middle_ref, sent_ref, h_two):
    tokens = x_ref.shape[0]
    step = pl.program_id(0)

    @pl.when(step == 0)
    def _():
        for first in range(0, tokens, block):
            rows = slice(first, first + block)
            middle = x_ref[rows, :].astype(F32) + dot(mixed_ref[rows, :], weight_ref[...])
            middle_ref[rows, :] = middle
            normed, _ = norm_parts(middle)
            h_two[rows, :] = (normed * gain_ref[...] + bias_ref[...]).astype(BF)

    sent_ref[...] = dot(one_hot_rows(target_ref[...], step * block, block), h_two[...]).astype(BF)


def middle_part(mixed, weight, x, gain, bias, target):
    tokens, width = x.shape
    block = 256
    slots = 2 * tokens
    return pl.pallas_call(
        functools.partial(middle_kernel, block),
        name="project_dispatch",
        grid=(slots // block,),
        in_specs=[
            whole((tokens, width)), whole(weight.shape), whole((tokens, width)),
            whole((1, width)), whole((1, width)), whole((1, tokens)),
        ],
        out_specs=[whole((tokens, width)), pl.BlockSpec((block, width), lambda s: (s, 0))],
        out_shape=[
            jax.ShapeDtypeStruct((tokens, width), F32),
            jax.ShapeDtypeStruct((slots, width), BF),
        ],
        scratch_shapes=[pltpu.VMEM((tokens, width), BF)],
        compiler_params=params(62),
        cost_estimate=cost(2 * slots * tokens * width + 2 * tokens * width * width, 16 * tokens * width),
    )(mixed, weight, x, gain, bias, target)


ROOT = 0.7978845608028654
CUBE = 0.044715


def once(shape):
    return pl.BlockSpec(shape, lambda *_: (0,) * len(shape), pipeline_mode=pl.Buffered(1))


def slope_kernel(grads_ref, wout_ref, out_ref):
    experts, rows, width = grads_ref.shape
    half = rows // 2
    for chunk in range(2):
        grads = grads_ref[:, chunk * half : (chunk + 1) * half, :].reshape(experts * half, width)
        out_ref[chunk * experts * half : (chunk + 1) * experts * half, :] = dot(grads, wout_ref[...], 1, 1)


def grads_inside(grads, weight_out):
    experts, rows, width = grads.shape
    count = experts * rows
    units = weight_out.shape[0]
    tile = 512
    return pl.pallas_call(
        slope_kernel,
        name="grads_inside",
        grid=(units // tile,),
        in_specs=[once(grads.shape), pl.BlockSpec((tile, width), lambda s: (s, 0))],
        out_specs=pl.BlockSpec((count, tile), lambda s: (0, s)),
        out_shape=jax.ShapeDtypeStruct((count, units), F32),
        compiler_params=params(62),
        cost_estimate=cost(2 * count * width * units, 4 * count * units),
    )(grads, weight_out)


def expert_kernel(block, has_previous, groups, perm_ref, rows_ref, grads_ref, slope_ref, win_ref, *refs):
    refs = list(refs)
    previous_ref = refs.pop(0) if has_previous else None
    act_ref, back_ref, back = refs[-3:]
    grad_refs = refs[:-3]
    count, width = rows_ref.shape
    step = pl.program_id(0)

    @pl.when(step == 0)
    def _():
        back[...] = jnp.zeros_like(back)

    weight_in = win_ref[...]
    all_grads = grads_ref[...].reshape(count, width)
    din = dout = None
    for first in range(0, count, block):
        span = slice(first, first + block)
        rows, grads = rows_ref[span, :], all_grads[span, :]
        inner = dot(rows, weight_in)
        square = inner * inner
        tanh = jnp.tanh(inner * (ROOT + (ROOT * CUBE) * square))
        gate = 0.5 + 0.5 * tanh
        act = inner * gate
        slope = gate + act * (1.0 - tanh) * (ROOT + (3.0 * ROOT * CUBE) * square)
        act = act.astype(BF)
        act_ref[span, :] = act
        grad_inner = (slope_ref[span, :] * slope).astype(BF)
        back[span, :] += dot(grad_inner, weight_in, 1, 1)
        part_in = dot(rows, grad_inner, 0, 0)
        part_out = dot(act, grads, 0, 0)
        din = part_in if din is None else din + part_in
        dout = part_out if dout is None else dout + part_out
    if has_previous:
        din = din + previous_ref[0, 0]
        dout = dout + previous_ref[0, 1]
        swap = perm_ref[groups + step % 2] == 1
        early = jnp.where(swap, din, dout).astype(BF)
        late = jnp.where(swap, dout, din).astype(BF)
        keep_ref = grad_refs[4]
        for group in range(2):

            @pl.when(step == group)
            def _():
                grad_refs[2 * group][...] = early
                grad_refs[2 * group + 1][...] = late

        @pl.when(step >= 2)
        def _():
            keep_ref[0, 0] = early
            keep_ref[0, 1] = late
    else:
        grad_refs[0][0, 0] = din
        grad_refs[0][0, 1] = dout

    @pl.when(step == groups - 1)
    def _():
        back_ref[...] = back[...].astype(BF)


def expert_rows(chunk, rows, grads, slopes, weight_in, perm, previous=None):
    count, width = rows.shape
    experts, slots, _ = grads.shape
    groups = 4
    units = weight_in.shape[1]
    tile = units // groups
    grad_spec = pl.BlockSpec((1, 2, tile, width), lambda s, perm: (s, 0, 0, 0))
    in_specs = [
        once((count, width)),
        pl.BlockSpec((experts, slots // 2, width), lambda s, perm: (0, chunk, 0), pipeline_mode=pl.Buffered(1)),
        pl.BlockSpec((count, tile), lambda s, perm: (chunk, perm[s])),
        pl.BlockSpec((width, tile), lambda s, perm: (0, perm[s])),
    ]
    operands = [rows, grads, slopes, weight_in]
    if previous is None:
        grad_specs = [grad_spec]
        grad_shapes = [jax.ShapeDtypeStruct((groups, 2, tile, width), F32)]
    else:
        in_specs.append(grad_spec)
        operands.append(previous)
        grad_specs = [
            *([once((tile, width))] * 4),
            pl.BlockSpec((1, 2, tile, width), lambda s, perm: (jnp.maximum(s - 2, 0), 0, 0, 0)),
        ]
        grad_shapes = [jax.ShapeDtypeStruct((tile, width), BF)] * 4
        grad_shapes += [jax.ShapeDtypeStruct((2, 2, tile, width), BF)]
    return pl.pallas_call(
        functools.partial(expert_kernel, 512, previous is not None, groups),
        name="expert_rows",
        grid_spec=pltpu.PrefetchScalarGridSpec(
            num_scalar_prefetch=1,
            grid=(groups,),
            in_specs=in_specs,
            out_specs=grad_specs
            + [pl.BlockSpec((count, tile), lambda s, perm: (0, perm[s])), whole((count, width))],
            scratch_shapes=[pltpu.VMEM((count, width), F32)],
        ),
        out_shape=grad_shapes
        + [jax.ShapeDtypeStruct((count, units), BF), jax.ShapeDtypeStruct((count, width), BF)],
        compiler_params=params(62),
        cost_estimate=cost(8 * count * width * units, 12 * width * units + 6 * count * units, count * units),
    )(perm, *operands)


def result_kernel(first_ref, second_ref, wout_ref, out_ref, total):
    step = pl.program_id(0)
    experts, rows, width = out_ref.shape
    half = rows // 2

    @pl.when(step == 0)
    def _():
        total[...] = jnp.zeros_like(total)

    weight_out = wout_ref[...]
    total[0] += dot(first_ref[...], weight_out)
    total[1] += dot(second_ref[...], weight_out)

    @pl.when(step == pl.num_programs(0) - 1)
    def _():
        for chunk in range(2):
            out_ref[:, chunk * half : (chunk + 1) * half, :] = (
                total[chunk].astype(BF).reshape(experts, half, width)
            )


def expert_result(first, second, weight_out, experts):
    count, units = first.shape
    width = weight_out.shape[1]
    tile = 768
    col = pl.BlockSpec((count, tile), lambda s: (0, s))
    shape = (experts, 2 * count // experts, width)
    return pl.pallas_call(
        result_kernel,
        name="expert_result",
        grid=(units // tile,),
        in_specs=[col, col, pl.BlockSpec((tile, width), lambda s: (s, 0))],
        out_specs=whole(shape),
        out_shape=jax.ShapeDtypeStruct(shape, BF),
        scratch_shapes=[pltpu.VMEM((2, count, width), F32)],
        compiler_params=params(62),
        cost_estimate=cost(4 * count * width * units, 4 * count * units),
    )(first, second, weight_out)


def place_kernel(count, flags_ref, *refs):
    sources, (in_ref, out_ref, wide, sems) = refs[:count], refs[-4:]
    rows, width = wide.shape[1:]
    for index, source in enumerate(sources):
        wide[index] = source[...].astype(F32)
        group, first = flags_ref[3 * index], pl.multiple_of(flags_ref[3 * index + 2] * rows, rows)
        to_in = flags_ref[3 * index + 1] == 0

        @pl.when(to_in)
        def _():
            columns = pl.ds(pl.multiple_of(group * width, width), width)
            pltpu.make_async_copy(wide.at[index], in_ref.at[pl.ds(first, rows), columns], sems.at[index]).start()

        @pl.when(jnp.logical_not(to_in))
        def _():
            place = pl.ds(pl.multiple_of(group * width + first, rows), rows)
            pltpu.make_async_copy(wide.at[index], out_ref.at[place, :], sems.at[index]).start()

    for index in range(count):
        pltpu.make_async_copy(wide.at[index], out_ref.at[pl.ds(0, rows), :], sems.at[index]).wait()


def place_blocks(flags, sources, previous=()):
    rows, width = sources[0].shape
    count = len(sources)
    anywhere = pl.BlockSpec(memory_space=pl.ANY)
    return pl.pallas_call(
        functools.partial(place_kernel, count),
        name="place_blocks",
        grid_spec=pltpu.PrefetchScalarGridSpec(
            num_scalar_prefetch=1,
            grid=(1,),
            in_specs=[once((rows, width))] * count + [anywhere] * len(previous),
            out_specs=[anywhere, anywhere],
            scratch_shapes=[pltpu.VMEM((count, rows, width), F32), pltpu.SemaphoreType.DMA((count,))],
        ),
        out_shape=[
            jax.ShapeDtypeStruct((width, 4 * width), F32),
            jax.ShapeDtypeStruct((4 * width, width), F32),
        ],
        input_output_aliases={count + 1: 0, count + 2: 1} if previous else {},
        compiler_params=params(62),
        cost_estimate=cost(rows * width, 6 * rows * width),
    )(jnp.stack(flags).astype(I32), *sources, *previous)


def gather_rows(block, target_ref, sources):
    count = sources[0].shape[0]
    target = target_ref[...]
    total = None
    for chunk, source in enumerate(sources):
        picked = (iota((block, count), 1) + chunk * count == target).astype(F32).astype(BF)
        part = dot(picked, source[...])
        total = part if total is None else total + part
    return total


def back_kernel(
    block, back_first_ref, back_second_ref, target_ref, middle_ref, mixed_ref, out_grad_ref, gain_ref, weight_ref, sel_ref,
    grad_middle_ref, grad_mixed_ref, branch_ref, delta_ref, small_ref,
):
    step = pl.program_id(0)
    grad_h = gather_rows(block, target_ref, (back_first_ref, back_second_ref))
    normed, inv_scale = norm_parts(middle_ref[...])
    gain = gain_ref[...]
    grad_middle = out_grad_ref[...].astype(F32) + norm_back(grad_h, normed, inv_scale, gain)
    grad_middle_ref[...] = grad_middle
    branch = grad_middle.astype(BF)
    branch_ref[...] = branch
    mixed = mixed_ref[...]
    grad_mixed = dot(branch, weight_ref[...], 1, 1).astype(BF)
    grad_mixed_ref[...] = grad_mixed
    product = grad_mixed.astype(F32) * mixed.astype(F32)
    high = product.astype(BF)
    low = (product - high.astype(F32)).astype(BF)
    sel = sel_ref[...]
    delta_ref[...] = dot(sel, high, 1, 1) + dot(sel, low, 1, 1)
    gain_grad = jnp.sum(grad_h * normed, 0, keepdims=True)
    bias_grad = jnp.sum(grad_h, 0, keepdims=True)

    @pl.when(step == 0)
    def _():
        small_ref[0:1, :] = gain_grad
        small_ref[1:2, :] = bias_grad

    @pl.when(step > 0)
    def _():
        small_ref[0:1, :] += gain_grad
        small_ref[1:2, :] += bias_grad


def middle_back(back_first, back_second, target_col, middle, mixed, out_grad, gain, weight):
    tokens, width = middle.shape
    slots = 2 * back_first.shape[0]
    block = 256
    heads = np.zeros((16, width), np.float32)
    for head in range(width // HEAD):
        heads[head, head * HEAD : (head + 1) * HEAD] = 1.0
    row = lambda w: pl.BlockSpec((block, w), lambda s: (s, 0))
    return pl.pallas_call(
        functools.partial(back_kernel, block),
        name="middle_back",
        grid=(tokens // block,),
        in_specs=[
            once((slots // 2, width)), once((slots // 2, width)), row(1), row(width), row(width), row(width),
            whole((1, width)), whole(weight.shape), whole((16, width)),
        ],
        out_specs=[
            row(width), row(width), row(width), pl.BlockSpec((16, block), lambda s: (0, s)),
            whole((8, width)),
        ],
        out_shape=[
            jax.ShapeDtypeStruct((tokens, width), F32),
            jax.ShapeDtypeStruct((tokens, width), BF),
            jax.ShapeDtypeStruct((tokens, width), BF),
            jax.ShapeDtypeStruct((16, tokens), F32),
            jax.ShapeDtypeStruct((8, width), F32),
        ],
        compiler_params=params(62),
        cost_estimate=cost(2 * slots * tokens * width + 4 * tokens * width * width, 24 * tokens * width),
    )(back_first, back_second, target_col, middle, mixed, out_grad, gain, weight, jnp.asarray(heads, BF))


def attend_back_kernel(
    block, start, q_ref, k_ref, v_ref, do_ref, lse_ref, delta_ref, seg_row_ref, seg_col_ref, cos_ref, sin_ref,
    dq_ref, dk_ref, dv_ref, total,
):
    tokens = q_ref.shape[0]
    pair = pl.program_id(0) + start
    cosine, sine = cos_ref[...], sin_ref[...]
    lse = [lse_ref[pl.ds(2 * pair + head, 1), :] for head in range(2)]
    delta = [delta_ref[pl.ds(2 * pair + head, 1), :] for head in range(2)]
    for first in range(0, tokens, block):
        last = first + block
        span = tokens - first
        keys, values = k_ref[first:last, :], v_ref[first:last, :]
        allowed = seg_col_ref[first:last, :] == seg_row_ref[:, first:]
        allowed &= iota((block, span), 0) <= iota((block, span), 1)
        dk = dv = dq = None
        for head in range(2):
            query = head_lanes(q_ref[first:, :], head)
            grads = head_lanes(do_ref[first:, :], head)
            scores = dot(keys, query, 1, 1)
            chance = jnp.where(allowed, jnp.exp(scores - lse[head][:, first:]), 0.0)
            grad_weights = dot(values, grads, 1, 1)
            grad_scores = (chance * (grad_weights - delta[head][:, first:])).astype(BF)
            part_v = dot(chance.astype(BF), grads)
            part_k = dot(grad_scores, query)
            part_q = dot(grad_scores, head_lanes(keys, head), 0, 0)
            dk = part_k if dk is None else dk + part_k
            dv = part_v if dv is None else dv + part_v
            dq = part_q if dq is None else dq + part_q
        dv_ref[first:last, :] = dv.astype(BF)
        cos_k, sin_k = cosine[first:last, :], sine[first:last, :]
        dk_ref[first:last, :] = (dk * cos_k - swap_halves(dk) * sin_k).astype(BF)
        if first == 0:
            total[...] = dq
        else:
            total[first:, :] += dq
    dq = total[...] * 0.125
    dq_ref[...] = (dq * cosine - swap_halves(dq) * sine).astype(BF)


def attend_back(qkv, grad_mixed, lse, delta, seg_row, seg_col, cosine, sine, start, count):
    tokens, width = grad_mixed.shape
    pairs = width // PAIR
    column = lambda part: pl.BlockSpec((tokens, PAIR), lambda g: (0, part * pairs + start + g))
    out = jax.ShapeDtypeStruct((tokens, count * PAIR), BF)
    return pl.pallas_call(
        functools.partial(attend_back_kernel, 256, start),
        name="attend_back",
        grid=(count,),
        in_specs=[
            column(0), column(1), column(2), column(0), whole(lse.shape), whole(delta.shape),
            whole((1, tokens)), whole((tokens, 1)), whole((tokens, PAIR)), whole((tokens, PAIR)),
        ],
        out_specs=[pl.BlockSpec((tokens, PAIR), lambda g: (0, g))] * 3,
        out_shape=[out] * 3,
        scratch_shapes=[pltpu.VMEM((tokens, PAIR), F32)],
        compiler_params=params(62),
        cost_estimate=cost(20 * tokens * tokens * PAIR * count, 14 * tokens * PAIR * count, 2 * tokens * tokens * count),
    )(qkv, qkv, qkv, grad_mixed, lse, delta, seg_row, seg_col, cosine, sine)


def shared_kernel(side_ref, h_ref, dq_ref, dk_ref, dv_ref, mixed_ref, branch_ref, keep_ref, send_ref):
    parts = [dot(h_ref[...], ref[...], 0, 0) for ref in (dq_ref, dk_ref, dv_ref)]
    parts.append(dot(mixed_ref[...], branch_ref[...], 0, 0))
    second = side_ref[0] == 1
    for part in range(2):
        keep_ref[part] = jnp.where(second, parts[2 + part], parts[part])
        send_ref[part] = jnp.where(second, parts[part], parts[2 + part]).astype(BF)


def shared_grads(side, h_one, grads, mixed, branch, which):
    tokens, width = h_one.shape
    columns = grads[0].shape[1]
    block = 256
    row = pl.BlockSpec((tokens, block), lambda s, side: (0, s))
    out = pl.BlockSpec((2, block, columns), lambda s, side: (0, s, 0))
    return pl.pallas_call(
        shared_kernel,
        name="shared_grads",
        grid_spec=pltpu.PrefetchScalarGridSpec(
            num_scalar_prefetch=1,
            grid=(width // block,),
            in_specs=[row] + [once((tokens, columns))] * 3
            + [row, pl.BlockSpec((tokens, columns), lambda s, side: (0, which), pipeline_mode=pl.Buffered(1))],
            out_specs=[out, out],
        ),
        out_shape=[
            jax.ShapeDtypeStruct((2, width, columns), F32),
            jax.ShapeDtypeStruct((2, width, columns), BF),
        ],
        compiler_params=params(62),
        cost_estimate=cost(8 * tokens * width * columns, 16 * width * columns + 12 * tokens * columns),
    )(side, h_one, *grads, mixed, branch)


def final_kernel(x_ref, *refs):
    grad_refs = refs[:6]
    grad_middle_ref, weight_ref, gain_ref, input_grad_ref, small_ref = refs[6:]
    step = pl.program_id(0)
    width = x_ref.shape[1]
    columns = grad_refs[0].shape[1]
    normed, inv_scale = norm_parts(x_ref[...].astype(F32))
    grad_h = None
    for index, ref in enumerate(grad_refs):
        start = (index % 3) * width + (index // 3) * columns
        piece = dot(ref[...], weight_ref[:, start : start + columns], 1, 1)
        grad_h = piece if grad_h is None else grad_h + piece
    input_grad_ref[...] = grad_middle_ref[...] + norm_back(grad_h, normed, inv_scale, gain_ref[...])
    gain_grad = jnp.sum(grad_h * normed, 0, keepdims=True)
    bias_grad = jnp.sum(grad_h, 0, keepdims=True)

    @pl.when(step == 0)
    def _():
        small_ref[0:1, :] = gain_grad
        small_ref[1:2, :] = bias_grad

    @pl.when(step > 0)
    def _():
        small_ref[0:1, :] += gain_grad
        small_ref[1:2, :] += bias_grad


def final_part(x, grads, grad_middle, weight, gain):
    tokens, width = x.shape
    columns = grads[0].shape[1]
    block = 256
    row = lambda w: pl.BlockSpec((block, w), lambda s: (s, 0))
    return pl.pallas_call(
        final_kernel,
        name="first_back",
        grid=(tokens // block,),
        in_specs=[row(width)] + [row(columns)] * 6 + [row(width), once(weight.shape), whole((1, width))],
        out_specs=[row(width), whole((8, width))],
        out_shape=[
            jax.ShapeDtypeStruct((tokens, width), F32),
            jax.ShapeDtypeStruct((8, width), F32),
        ],
        compiler_params=params(62),
        cost_estimate=cost(6 * tokens * width * width, 6 * width * width + 16 * tokens * width),
    )(x, *grads, grad_middle, weight, gain)


def output_kernel(block, result_ref, target_ref, middle_ref, out_ref):
    out_ref[...] = (middle_ref[...] + gather_rows(block, target_ref, (result_ref,))).astype(BF)


def block_output(result, place_col, middle):
    tokens, width = middle.shape
    slots = result.shape[0]
    block = 256
    row = lambda w: pl.BlockSpec((block, w), lambda s: (s, 0))
    return pl.pallas_call(
        functools.partial(output_kernel, block),
        name="block_output",
        grid=(tokens // block,),
        in_specs=[once((slots, width)), row(1), row(width)],
        out_specs=row(width),
        out_shape=jax.ShapeDtypeStruct((tokens, width), BF),
        compiler_params=params(62),
        cost_estimate=cost(2 * slots * tokens * width, 10 * tokens * width),
    )(result, place_col, middle)


def shared_out_kernel(flag_ref, low_ref, high_ref, *refs):
    qkv_ref, proj_ref, wide, sems = refs[-4:]
    width, columns = wide.shape[2:]
    for half in range(2):
        part = 2 * flag_ref[0] + half
        for index, source in enumerate((low_ref, high_ref)):
            slot = 2 * half + index
            wide[half, index] = source[half].astype(F32)
            start = pl.multiple_of(part * width + index * columns, columns)

            @pl.when(part < 3)
            def _():
                pltpu.make_async_copy(
                    wide.at[half, index], qkv_ref.at[:, pl.ds(start, columns)], sems.at[slot]
                ).start()

            @pl.when(part == 3)
            def _():
                pltpu.make_async_copy(
                    wide.at[half, index], proj_ref.at[:, pl.ds(index * columns, columns)], sems.at[slot]
                ).start()

    for slot in range(4):
        pltpu.make_async_copy(
            wide.at[slot // 2, slot % 2], proj_ref.at[:, pl.ds(0, columns)], sems.at[slot]
        ).wait()


def shared_outputs(flag, low, high, previous=()):
    _, width, columns = low.shape
    anywhere = pl.BlockSpec(memory_space=pl.ANY)
    return pl.pallas_call(
        shared_out_kernel,
        name="shared_outputs",
        grid_spec=pltpu.PrefetchScalarGridSpec(
            num_scalar_prefetch=1,
            grid=(1,),
            in_specs=[once(low.shape)] * 2 + [anywhere] * len(previous),
            out_specs=[anywhere, anywhere],
            scratch_shapes=[pltpu.VMEM((2, 2, width, columns), F32), pltpu.SemaphoreType.DMA((4,))],
        ),
        out_shape=[
            jax.ShapeDtypeStruct((width, 3 * width), F32),
            jax.ShapeDtypeStruct((width, width), F32),
        ],
        input_output_aliases={3: 0, 4: 1} if previous else {},
        compiler_params=params(62),
        cost_estimate=cost(width, width * width),
    )(flag, low, high, *previous)


def partner(axis, bit):
    return [(i, i ^ bit) for i in range(lax.axis_size(axis))]


def side(axis, bit):
    return (lax.axis_index(axis) // bit) % 2


def axis_bits(axis):
    bits, bit = [], 1
    while bit < lax.axis_size(axis):
        bits.append((axis, bit))
        bit *= 2
    return bits


def reduce_step(total, axis, bit):
    if total.shape[0] == 1:
        total = total.astype(BF)
        return total.astype(F32) + lax.ppermute(total, axis, partner(axis, bit)).astype(F32)
    mine = side(axis, bit)
    half = total.shape[0] // 2
    keep = lax.dynamic_slice_in_dim(total, mine * half, half, 0)
    send = lax.dynamic_slice_in_dim(total, (1 - mine) * half, half, 0)
    return keep + lax.ppermute(send.astype(BF), axis, partner(axis, bit)).astype(F32)


def gather_step(total, axis, bit):
    got = lax.ppermute(total, axis, partner(axis, bit))
    return jnp.where(side(axis, bit) == 0, jnp.concatenate([total, got], 0), jnp.concatenate([got, total], 0))


def add_partner(rows, axis, bit):
    return rows + lax.ppermute(rows, axis, partner(axis, bit))


def local(
    hidden_in, token_ids, hash_table, segment_ids, ln1_gain, ln1_bias, qkv_weight, proj_weight,
    ln2_gain, ln2_bias, expert_in, expert_out, out_grad,
):
    tokens, width = hidden_in.shape
    experts = lax.axis_size("expert")
    devices = lax.axis_size("dp") * experts
    half = tokens // experts
    row = lambda vector: vector.reshape(1, width)
    cosine, sine = (jnp.asarray(table) for table in angle_tables(tokens))
    seg_row, seg_col = segment_ids.reshape(1, tokens), segment_ids.reshape(tokens, 1)
    weight_in, weight_out = expert_in[0], expert_out[0]

    def exchange(rows):
        sent = rows.reshape(experts, rows.shape[0] // experts, width)
        return lax.all_to_all(sent, "expert", split_axis=0, concat_axis=0, tiled=True)

    def exchange_half(rows):
        return exchange(rows).reshape(tokens, width)

    def split(rows):
        return rows[:tokens], rows[tokens:]

    x_side, y_side = side("dp", 1), side("dp", 2)
    perm = jnp.stack([1 - x_side, 3 - y_side, x_side, 2 + y_side, y_side, x_side]).astype(I32)
    tie = lambda *values: lax.optimization_barrier(values)

    target, place, counts, sent_grads = route(token_ids, hash_table, out_grad, experts, half)
    target_col, place_col = target.reshape(tokens, 1), place.reshape(tokens, 1)
    sent_grads, hidden_in = tie(sent_grads, hidden_in)
    grad_rows = exchange(sent_grads)
    qkv, h_one = first_half(hidden_in, row(ln1_gain), row(ln1_bias), qkv_weight, cosine, sine)
    mixed, lse = attend(qkv, seg_row, seg_col)
    middle, sent_rows = middle_part(mixed, proj_weight, hidden_in, row(ln2_gain), row(ln2_bias), target)
    sent_first, sent_second = split(sent_rows)
    sent_first, grad_rows = tie(sent_first, grad_rows)
    rows_first = exchange_half(sent_first)
    slopes = grads_inside(grad_rows, weight_out)
    sent_second, rows_first, slopes = tie(sent_second, rows_first, slopes)
    rows_second = exchange_half(sent_second)

    previous, act_first, back_first = expert_rows(0, rows_first, grad_rows, slopes, weight_in, perm)
    back_first, rows_second = tie(back_first, rows_second)
    back_first = exchange_half(back_first)
    early_x, late_x, early_y, late_y, keep, act_second, back_second = expert_rows(
        1, rows_second, grad_rows, slopes, weight_in, perm, previous
    )
    across_x = lambda value: lax.ppermute(value, "dp", partner("dp", 1))
    across_y = lambda value: lax.ppermute(value, "dp", partner("dp", 2))
    back_second, back_first = tie(back_second, back_first)
    back_second = exchange_half(back_second)
    early_x, early_y = across_x(early_x), across_y(early_y)
    late_x, late_y = across_x(late_x), across_y(late_y)
    result = expert_result(act_first, act_second, weight_out, experts)
    result, back_second = tie(result, back_second)

    plus = lambda *values: sum(value.astype(F32) for value in values).astype(BF)
    send_x, send_y = plus(keep[0, 0], early_x), plus(keep[1, 0], early_y)
    send_x, send_y, back_second = tie(send_x, send_y, back_second)
    other_x, other_y = across_y(send_x), across_x(send_y)
    grad_middle, grad_mixed, branch, delta, small_two = middle_back(
        back_first, back_second, target_col, middle, mixed, out_grad, row(ln2_gain), proj_weight
    )
    grad_mixed, late_x, late_y, result = tie(grad_mixed, late_x, late_y, result)
    result = exchange(result.reshape(2 * tokens, width))

    pairs = width // PAIR
    back_of = lambda grads, start: attend_back(
        qkv, grads, lse, delta, seg_row, seg_col, cosine, sine, start, pairs // 2
    )
    core_side = jnp.reshape(side("expert", 1), (1,)).astype(I32)
    across_core = lambda value: lax.ppermute(value, "expert", partner("expert", 1))
    grads_low = back_of(grad_mixed, 0)
    other_x, other_y, grads_low, grad_mixed = tie(other_x, other_y, grads_low, grad_mixed)
    runs = [slice(0, width // 2), slice(width // 2, width)]
    total_x = [plus(keep[0, 1, run], late_x[run], other_x[run]) for run in runs]
    total_y = [plus(keep[1, 1, run], late_y[run], other_y[run]) for run in runs]
    total_x, total_y, grads_low = tie(total_x, total_y, grads_low)
    near_x, near_y = [across_y(run) for run in total_x], [across_x(run) for run in total_y]
    far_x, far_y = across_x(total_x[0]), across_y(total_y[0])
    low, send_low = shared_grads(core_side, h_one, grads_low, mixed, branch, 0)
    send_low, grad_mixed = tie(send_low, grad_mixed)
    got_low = across_core(send_low)
    grads_high = back_of(grad_mixed, pairs // 2)
    high, send_high = shared_grads(core_side, h_one, grads_high, mixed, branch, 1)
    near_x, near_y, far_x, far_y, got_low, send_high = tie(near_x, near_y, far_x, far_y, got_low, send_high)

    low = (low + got_low.astype(F32)).reshape(8, width // 4, width // 2)
    high = (high + across_core(send_high).astype(F32)).reshape(8, width // 4, width // 2)
    far_bits = axis_bits("expert")[1:]
    low_order = axis_bits("dp") + far_bits
    high_order = axis_bits("dp")[::-1] + far_bits

    def reduce_both(low, high, step):
        return reduce_step(low, *low_order[step]), reduce_step(high, *high_order[step])

    low, high = reduce_both(low, high, 0)
    input_grad, small_one = final_part(
        hidden_in, list(grads_low) + list(grads_high), grad_middle, qkv_weight, row(ln1_gain)
    )
    low, high, small_one = tie(low, high, small_one)
    small = jnp.concatenate(
        [small_one[:2], small_two[:2], jnp.pad(counts, (0, width - experts))[None], jnp.zeros((3, width), F32)], 0
    )
    for axis, bit in axis_bits("dp"):
        small = add_partner(small, axis, bit)
    low, high = reduce_both(low, high, 1)
    both_runs = lambda group, which: [group, which, 0, group, which, 1]
    grad_in, grad_out = place_blocks(
        both_runs(x_side, y_side) + both_runs(x_side, 1 - y_side)
        + both_runs(2 + y_side, x_side) + both_runs(2 + y_side, 1 - x_side),
        [*total_x, *near_x, *total_y, *near_y],
    )
    low, high, small, total_x, total_y, near_x, near_y, grad_in, result = tie(
        low, high, small, total_x, total_y, near_x, near_y, grad_in, result
    )
    far_x, far_y = [far_x, across_x(total_x[1])], [far_y, across_y(total_y[1])]
    last_x, last_y = [across_x(run) for run in near_x], [across_y(run) for run in near_y]
    both = jnp.concatenate([low, high], 2)
    small = add_partner(small, "expert", 1)
    both = reduce_step(both, *far_bits[0])
    both, small, far_x, far_y = tie(both, small, far_x, far_y)
    small = add_partner(small, *far_bits[0])
    both = reduce_step(both, *far_bits[1])
    both, small, last_x[0], last_y[0] = tie(both, small, last_x[0], last_y[0])
    for axis, bit in far_bits[2:]:
        both = reduce_step(both, axis, bit)
    for axis, bit in far_bits[1:]:
        small = add_partner(small, axis, bit)
    both = gather_step(both.astype(BF), *far_bits[0])
    both, last_x, last_y, small = tie(both, last_x, last_y, small)
    low, high = both[:, :, : width // 2], both[:, :, width // 2 :]
    low, high = gather_step(low, *low_order[1]), gather_step(high, *high_order[1])
    grad_in, grad_out = place_blocks(
        both_runs(1 - x_side, y_side) + both_runs(1 - x_side, 1 - y_side)
        + both_runs(3 - y_side, x_side) + both_runs(3 - y_side, 1 - x_side),
        [*far_x, *last_x, *far_y, *last_y], (grad_in, grad_out),
    )
    low, high, grad_in, grad_out = tie(low, high, grad_in, grad_out)
    low, high = gather_step(low, *low_order[0]), gather_step(high, *high_order[0])
    block_out = block_output(result.reshape(2 * tokens, width), place_col, middle)
    low, high, block_out = tie(low, high, block_out)
    low, high = low.reshape(2, width, width // 2), high.reshape(2, width, width // 2)
    got_low, got_high = across_core(low), across_core(high)
    qkv_grad, proj_sum = shared_outputs(core_side, low, high)
    got_low, got_high, qkv_grad, proj_sum = tie(got_low, got_high, qkv_grad, proj_sum)
    qkv_grad, proj_sum = shared_outputs(1 - core_side, got_low, got_high, (qkv_grad, proj_sum))
    load = small[4, :experts] * (experts / (tokens * devices))
    return (
        block_out,
        input_grad,
        small[0],
        small[1],
        qkv_grad,
        proj_sum,
        small[2],
        small[3],
        grad_in[None],
        grad_out[None],
        load,
    )


def solution(mesh):
    split, copied, owned = P(("dp", "expert")), P(), P("expert")
    in_specs = (
        split, split, copied, split, copied, copied, copied, copied, copied, copied, owned, owned, split,
    )
    out_specs = (
        split, split, copied, copied, copied, copied, copied, copied, owned, owned, copied,
    )
    return jax.shard_map(local, mesh=mesh, in_specs=in_specs, out_specs=out_specs, check_vma=False)
```

```python
import functools
import numpy as np
import jax
import jax.numpy as jnp
from jax import lax
from jax.experimental import pallas as pl
from jax.experimental.pallas import tpu as pltpu
from jax.sharding import PartitionSpec as P

HEAD = 64
EPSILON = 1e-05
BF = jnp.bfloat16
F32 = jnp.float32
I32 = jnp.int32
PAIR = 2 * HEAD
NEG = -1e30


def params(mib):
    return pltpu.CompilerParams(vmem_limit_bytes=mib << 20)


def cost(flops, bytes_accessed, transcendentals=0):
    return pl.CostEstimate(flops=1, bytes_accessed=1, transcendentals=0)


def dot(left, right, left_dim=1, right_dim=0):
    return lax.dot_general(
        left, right, (((left_dim,), (right_dim,)), ((), ())), preferred_element_type=F32
    )


def whole(shape):
    return pl.BlockSpec(shape, lambda *_: (0,) * len(shape))


def iota(shape, dim):
    return lax.broadcasted_iota(I32, shape, dim)


def norm_parts(rows):
    centred = rows - jnp.mean(rows, -1, keepdims=True)
    inv_scale = lax.rsqrt(jnp.mean(centred * centred, -1, keepdims=True) + EPSILON)
    return centred * inv_scale, inv_scale


def norm_back(grad_out, normed, inv_scale, gain):
    scaled = grad_out * gain
    centre = jnp.mean(scaled, -1, keepdims=True)
    along = jnp.mean(scaled * normed, -1, keepdims=True)
    return inv_scale * (scaled - centre - normed * along)


def one_hot_rows(target, first, count):
    return (iota((count, target.shape[1]), 0) + first == target).astype(F32).astype(BF)


def route_kernel(
    experts, half, block, me_ref, ids_ref, segments_ref, table_ref, grad_ref,
    columns_ref, leaving_ref, counts_ref, sent_ref, place,
):
    tokens = ids_ref.shape[1]
    rows = table_ref.shape[0]
    padded = counts_ref.shape[0]
    step = pl.program_id(0)

    @pl.when(step == 0)
    def _():
        ids = ids_ref[...]
        picked = (iota((rows, tokens), 0) == (ids >> 7)).astype(F32).astype(BF)
        found = dot(table_ref[...], picked, 0, 0)
        chosen = jnp.sum(
            jnp.where(iota((128, tokens), 0) == (ids & 127), found, 0.0), 0, keepdims=True
        ).astype(I32)
        member = (iota((padded, tokens), 0) == chosen).astype(F32)
        earlier = (iota((tokens, tokens), 0) < iota((tokens, tokens), 1)).astype(F32).astype(BF)
        rank = dot(member.astype(BF), earlier)
        slot = jnp.sum(member * rank, 0, keepdims=True).astype(I32)
        place[...] = chosen * (2 * half) + slot
        late = slot >= half
        second = experts * half + chosen * half + slot - half
        target = jnp.where(late, second, chosen * half + slot)
        lines = [target, place[...], segments_ref[...], jnp.zeros((5, tokens), I32)]
        columns_ref[...] = jnp.concatenate(lines, 0).T
        leaving_ref[...] = jnp.where(late, second, (chosen ^ me_ref[0]) * half + slot)
        counts_ref[...] = jnp.broadcast_to(jnp.sum(member, 1, keepdims=True), counts_ref.shape)

    sent_ref[...] = dot(one_hot_rows(place[...], step * block, block), grad_ref[...]).astype(BF)


def route(me, token_ids, segments, hash_table, out_grad, experts, half):
    tokens, width = out_grad.shape
    slots = 2 * tokens
    block = 256
    padded = max(experts, 16)
    rows = -(-hash_table.shape[0] // (128 * 128)) * 128
    table = jnp.pad(hash_table, (0, rows * 128 - hash_table.shape[0])).reshape(rows, 128).astype(BF)
    columns, leaving, counts, sent = pl.pallas_call(
        functools.partial(route_kernel, experts, half, block),
        name="route",
        grid_spec=pltpu.PrefetchScalarGridSpec(
            num_scalar_prefetch=1,
            grid=(slots // block,),
            in_specs=[whole((1, tokens)), whole((1, tokens)), whole((rows, 128)), whole((tokens, width))],
            out_specs=[
                whole((tokens, 8)),
                whole((1, tokens)),
                whole((padded, 128)),
                pl.BlockSpec((block, width), lambda s, me: (s, 0)),
            ],
            scratch_shapes=[pltpu.VMEM((1, tokens), I32)],
        ),
        out_shape=[
            jax.ShapeDtypeStruct((tokens, 8), I32),
            jax.ShapeDtypeStruct((1, tokens), I32),
            jax.ShapeDtypeStruct((padded, 128), F32),
            jax.ShapeDtypeStruct((slots, width), BF),
        ],
        compiler_params=params(62),
        cost_estimate=cost(2 * slots * tokens * width, 8 * tokens * width),
    )(me, token_ids.reshape(1, tokens), segments, table, out_grad)
    return columns, leaving, counts[:experts, 0], sent


def swap_halves(rows):
    half = HEAD // 2
    width = rows.shape[1]
    low = (iota(rows.shape, 1) & half) == 0
    return jnp.where(low, pltpu.roll(rows, width - half, 1), pltpu.roll(rows, half, 1))


def pre_kernel(x_ref, gain_ref, bias_ref, weight_ref, cos_ref, sin_ref, qkv_ref, h_ref):
    width = x_ref.shape[1]
    normed, _ = norm_parts(x_ref[...].astype(F32))
    h_one = (normed * gain_ref[...] + bias_ref[...]).astype(BF)
    h_ref[...] = h_one.T
    cosine, sine = cos_ref[...], sin_ref[...]
    for part in range(3):
        raw = dot(h_one, weight_ref[:, part * width : (part + 1) * width])
        for pair in range(width // PAIR):
            piece = raw[:, pair * PAIR : (pair + 1) * PAIR]
            if part < 2:
                piece = piece * cosine + swap_halves(piece) * sine
            if part == 0:
                piece = piece * 0.125
            start = part * width + pair * PAIR
            qkv_ref[:, start : start + PAIR] = piece.astype(BF)


def angle_tables(tokens):
    half = HEAD // 2
    freq = np.float32(10000.0) ** (-np.arange(half, dtype=np.float32) / np.float32(half))
    angle = np.arange(tokens, dtype=np.float32)[:, None] * freq[None, :].astype(np.float32)
    cosine = np.cos(angle).astype(np.float32)
    sine = np.sin(angle).astype(np.float32)
    cosine = np.concatenate([cosine, cosine], 1)
    sine = np.concatenate([-sine, sine], 1)
    return np.concatenate([cosine, cosine], 1), np.concatenate([sine, sine], 1)


def first_half(x, gain, bias, weight, cosine, sine):
    tokens, width = x.shape
    block = 256
    row = lambda w: pl.BlockSpec((block, w), lambda s: (s, 0))
    return pl.pallas_call(
        pre_kernel,
        name="norm_project",
        grid=(tokens // block,),
        in_specs=[
            row(width), whole((1, width)), whole((1, width)), whole(weight.shape), row(PAIR), row(PAIR),
        ],
        out_specs=[row(3 * width), pl.BlockSpec((width, block), lambda s: (0, s))],
        out_shape=[
            jax.ShapeDtypeStruct((tokens, 3 * width), BF),
            jax.ShapeDtypeStruct((width, tokens), BF),
        ],
        compiler_params=params(62),
        cost_estimate=cost(6 * tokens * width * width, 6 * width * width + 12 * tokens * width),
    )(x, gain, bias, weight, cosine, sine)


def head_lanes(rows, head):
    return jnp.where((iota((1, PAIR), 1) >= HEAD) == bool(head), rows, jnp.zeros_like(rows))


def attend_kernel(block, q_ref, k_ref, v_ref, seg_row_ref, seg_col_ref, mixed_ref, turned_ref, lse_ref, stats):
    tokens = q_ref.shape[0]
    pair = pl.program_id(0)
    upper = iota((1, PAIR), 1) >= HEAD
    for first in range(0, tokens, block):
        last = first + block
        query = q_ref[first:last, :]
        allowed = seg_col_ref[first:last, 2:3] == seg_row_ref[:, :last]
        allowed &= iota((block, last), 1) <= iota((block, last), 0) + first
        halves = []
        for head in range(2):
            scores = dot(head_lanes(query, head), k_ref[:last, :], 1, 1)
            scores = jnp.where(allowed, scores, NEG)
            top = jnp.max(scores, -1, keepdims=True)
            weights = jnp.exp(scores - top)
            total = jnp.sum(weights, -1, keepdims=True)
            halves.append(dot(weights.astype(BF), v_ref[:last, :]) * (1.0 / total))
            lane = iota((1, 128), 1) == 2 * pair + head
            stats[first:last, :] = jnp.where(lane, top + jnp.log(total), stats[first:last, :])
        mixed_ref[first:last, :] = jnp.where(upper, halves[1], halves[0]).astype(BF)
    turned_ref[...] = mixed_ref[...].T

    @pl.when(pair == pl.num_programs(0) - 1)
    def _():
        lse_ref[...] = stats[...].T


def attend(qkv, seg_row, seg_col):
    tokens, width = qkv.shape[0], qkv.shape[1] // 3
    pairs = width // PAIR
    column = lambda part: pl.BlockSpec((tokens, PAIR), lambda g: (0, part * pairs + g))
    return pl.pallas_call(
        functools.partial(attend_kernel, 256),
        name="attend",
        grid=(pairs,),
        in_specs=[column(0), column(1), column(2), whole((1, tokens)), whole((tokens, 8))],
        out_specs=[column(0), pl.BlockSpec((PAIR, tokens), lambda g: (g, 0)), whole((128, tokens))],
        out_shape=[
            jax.ShapeDtypeStruct((tokens, width), BF),
            jax.ShapeDtypeStruct((width, tokens), BF),
            jax.ShapeDtypeStruct((128, tokens), F32),
        ],
        scratch_shapes=[pltpu.VMEM((tokens, 128), F32)],
        compiler_params=params(62),
        cost_estimate=cost(8 * tokens * tokens * width, 8 * tokens * width, tokens * tokens * width // HEAD),
    )(qkv, qkv, qkv, seg_row, seg_col)


def middle_kernel(block, mixed_ref, weight_ref, x_ref, gain_ref, bias_ref, target_ref, middle_ref, sent_ref, h_two):
    tokens = x_ref.shape[0]
    step = pl.program_id(0)

    @pl.when(step == 0)
    def _():
        for first in range(0, tokens, block):
            rows = slice(first, first + block)
            middle = x_ref[rows, :].astype(F32) + dot(mixed_ref[rows, :], weight_ref[...])
            middle_ref[rows, :] = middle
            normed, _ = norm_parts(middle)
            h_two[rows, :] = (normed * gain_ref[...] + bias_ref[...]).astype(BF)

    sent_ref[...] = dot(one_hot_rows(target_ref[...], step * block, block), h_two[...]).astype(BF)


def middle_part(mixed, weight, x, gain, bias, target):
    tokens, width = x.shape
    block = 256
    slots = 2 * tokens
    return pl.pallas_call(
        functools.partial(middle_kernel, block),
        name="project_dispatch",
        grid=(slots // block,),
        in_specs=[
            whole((tokens, width)), whole(weight.shape), whole((tokens, width)),
            whole((1, width)), whole((1, width)), whole((1, tokens)),
        ],
        out_specs=[whole((tokens, width)), pl.BlockSpec((block, width), lambda s: (s, 0))],
        out_shape=[
            jax.ShapeDtypeStruct((tokens, width), F32),
            jax.ShapeDtypeStruct((slots, width), BF),
        ],
        scratch_shapes=[pltpu.VMEM((tokens, width), BF)],
        compiler_params=params(62),
        cost_estimate=cost(2 * slots * tokens * width + 2 * tokens * width * width, 16 * tokens * width),
    )(mixed, weight, x, gain, bias, target)


ROOT = 0.7978845608028654
CUBE = 0.044715


def once(shape):
    return pl.BlockSpec(shape, lambda *_: (0,) * len(shape), pipeline_mode=pl.Buffered(1))


def in_distance_order(me, source_ref, target_ref, half):
    experts = source_ref.shape[0]
    for distance in range(experts):
        target_ref[distance * half : (distance + 1) * half, :] = source_ref[me ^ distance, :half, :]


def slope_kernel(me_ref, grads_ref, wout_ref, out_ref, near):
    experts, rows, width = grads_ref.shape
    half = rows // 2
    count = experts * half

    @pl.when(pl.program_id(0) == 0)
    def _():
        in_distance_order(me_ref[0], grads_ref, near, half)

    weight_out = wout_ref[...]
    out_ref[:count, :] = dot(near[...], weight_out, 1, 1).astype(BF)
    out_ref[count:, :] = dot(grads_ref[:, half:, :].reshape(count, width), weight_out, 1, 1).astype(BF)


def grads_inside(me, grads, weight_out):
    experts, rows, width = grads.shape
    count = experts * rows
    units = weight_out.shape[0]
    tile = 768
    return pl.pallas_call(
        slope_kernel,
        name="grads_inside",
        grid_spec=pltpu.PrefetchScalarGridSpec(
            num_scalar_prefetch=1,
            grid=(units // tile,),
            in_specs=[once(grads.shape), pl.BlockSpec((tile, width), lambda s, me: (s, 0))],
            out_specs=pl.BlockSpec((count, tile), lambda s, me: (0, s)),
            scratch_shapes=[pltpu.VMEM((count // 2, width), BF)],
        ),
        out_shape=jax.ShapeDtypeStruct((count, units), BF),
        compiler_params=params(62),
        cost_estimate=cost(2 * count * width * units, 4 * count * units),
    )(me, grads, weight_out)


def expert_kernel(block, pieces, groups, perm_ref, *refs):
    refs = list(refs)
    rows_refs = [refs.pop(0) for _ in range(pieces)]
    grads_ref, slope_ref, win_ref = refs[:3]
    del refs[:3]
    first_chunk = pieces > 1
    if first_chunk:
        grad_ref, act_ref, back_ref, back, rows_ref, all_grads = refs
    else:
        previous_ref, *grad_refs, act_ref, back_ref, back = refs
        rows_ref = rows_refs[0]
    experts, half, width = grads_ref.shape
    count = experts * half
    step = pl.program_id(0)

    @pl.when(step == 0)
    def _():
        back[...] = jnp.zeros_like(back)
        if first_chunk:
            in_distance_order(perm_ref[groups + 2], grads_ref, all_grads, half)
            for distance, piece in enumerate(rows_refs):
                rows_ref[distance * half : (distance + 1) * half, :] = piece[...]

    weight_in = win_ref[...]
    grads_all = all_grads[...] if first_chunk else grads_ref[...].reshape(count, width)
    din = dout = None
    for first in range(0, count, block):
        span = slice(first, first + block)
        rows, grads = rows_ref[span, :], grads_all[span, :]
        inner = dot(rows, weight_in)
        square = inner * inner
        tanh = jnp.tanh(inner * (ROOT + (ROOT * CUBE) * square))
        gate = 0.5 + 0.5 * tanh
        act = inner * gate
        slope = gate + act * (1.0 - tanh) * (ROOT + (3.0 * ROOT * CUBE) * square)
        act = act.astype(BF)
        act_ref[span, :] = act
        grad_inner = (slope_ref[span, :] * slope).astype(BF)
        back[span, :] += dot(grad_inner, weight_in, 1, 1)
        part_in = dot(rows, grad_inner, 0, 0)
        part_out = dot(act, grads, 0, 0)
        din = part_in if din is None else din + part_in
        dout = part_out if dout is None else dout + part_out
    if first_chunk:
        grad_ref[0, 0] = din
        grad_ref[0, 1] = dout
    else:
        din = din + previous_ref[0, 0]
        dout = dout + previous_ref[0, 1]
        swap = perm_ref[groups + step % 2] == 1
        early = jnp.where(swap, din, dout).astype(BF)
        late = jnp.where(swap, dout, din).astype(BF)
        keep_ref = grad_refs[4]
        for group in range(2):

            @pl.when(step == group)
            def _():
                grad_refs[2 * group][...] = early
                grad_refs[2 * group + 1][...] = late

        @pl.when(step >= 2)
        def _():
            keep_ref[0, 0] = early
            keep_ref[0, 1] = late

    @pl.when(step == groups - 1)
    def _():
        if first_chunk:
            for distance in range(experts):
                place = pl.multiple_of((perm_ref[groups + 2] ^ distance) * half, half)
                back_ref[pl.ds(place, half), :] = back[distance * half : (distance + 1) * half, :].astype(BF)
        else:
            back_ref[...] = back[...].astype(BF)


def expert_rows(rows, grads, slopes, weight_in, perm, previous=None):
    chunk = 0 if previous is None else 1
    experts, slots, width = grads.shape
    half = slots // 2
    count = experts * half
    groups = 4
    units = weight_in.shape[1]
    tile = units // groups
    grad_spec = pl.BlockSpec((1, 2, tile, width), lambda s, perm: (s, 0, 0, 0))
    in_specs = [once(piece.shape) for piece in rows] + [
        pl.BlockSpec((experts, half, width), lambda s, perm: (0, chunk, 0), pipeline_mode=pl.Buffered(1)),
        pl.BlockSpec((count, tile), lambda s, perm: (chunk, perm[s])),
        pl.BlockSpec((width, tile), lambda s, perm: (0, perm[s])),
    ]
    operands = [*rows, grads, slopes, weight_in]
    scratch = [pltpu.VMEM((count, width), F32)]
    if previous is None:
        grad_specs = [grad_spec]
        grad_shapes = [jax.ShapeDtypeStruct((groups, 2, tile, width), F32)]
        scratch += [pltpu.VMEM((count, width), BF)] * 2
    else:
        in_specs.append(grad_spec)
        operands.append(previous)
        grad_specs = [
            *([once((tile, width))] * 4),
            pl.BlockSpec((1, 2, tile, width), lambda s, perm: (jnp.maximum(s - 2, 0), 0, 0, 0)),
        ]
        grad_shapes = [jax.ShapeDtypeStruct((tile, width), BF)] * 4
        grad_shapes += [jax.ShapeDtypeStruct((2, 2, tile, width), BF)]
    return pl.pallas_call(
        functools.partial(expert_kernel, 512, len(rows), groups),
        name="expert_rows",
        grid_spec=pltpu.PrefetchScalarGridSpec(
            num_scalar_prefetch=1,
            grid=(groups,),
            in_specs=in_specs,
            out_specs=grad_specs
            + [pl.BlockSpec((count, tile), lambda s, perm: (0, perm[s])), whole((count, width))],
            scratch_shapes=scratch,
        ),
        out_shape=grad_shapes
        + [jax.ShapeDtypeStruct((count, units), BF), jax.ShapeDtypeStruct((count, width), BF)],
        compiler_params=params(62),
        cost_estimate=cost(8 * count * width * units, 12 * width * units + 6 * count * units, count * units),
    )(perm, *operands)


def result_kernel(me_ref, first_ref, second_ref, wout_ref, out_ref, total):
    step = pl.program_id(0)
    experts, rows, width = out_ref.shape
    half = rows // 2

    @pl.when(step == 0)
    def _():
        total[...] = jnp.zeros_like(total)

    weight_out = wout_ref[...]
    total[0] += dot(first_ref[...], weight_out)
    total[1] += dot(second_ref[...], weight_out)

    @pl.when(step == pl.num_programs(0) - 1)
    def _():
        out_ref[:, half:, :] = total[1].astype(BF).reshape(experts, half, width)
        for distance in range(experts):
            piece = total[0, distance * half : (distance + 1) * half, :]
            out_ref[me_ref[0] ^ distance, :half, :] = piece.astype(BF)


def expert_result(me, first, second, weight_out, experts):
    count, units = first.shape
    width = weight_out.shape[1]
    tile = 768
    col = pl.BlockSpec((count, tile), lambda s, me: (0, s))
    shape = (experts, 2 * count // experts, width)
    return pl.pallas_call(
        result_kernel,
        name="expert_result",
        grid_spec=pltpu.PrefetchScalarGridSpec(
            num_scalar_prefetch=1,
            grid=(units // tile,),
            in_specs=[col, col, pl.BlockSpec((tile, width), lambda s, me: (s, 0))],
            out_specs=whole(shape),
            scratch_shapes=[pltpu.VMEM((2, count, width), F32)],
        ),
        out_shape=jax.ShapeDtypeStruct(shape, BF),
        compiler_params=params(62),
        cost_estimate=cost(4 * count * width * units, 4 * count * units),
    )(me, first, second, weight_out)


def place_kernel(count, flags_ref, *refs):
    sources, (in_ref, out_ref, wide, sems) = refs[:count], refs[-4:]
    rows, width = wide.shape[1:]
    for index, source in enumerate(sources):
        wide[index] = source[...].astype(F32)
        group, first = flags_ref[3 * index], pl.multiple_of(flags_ref[3 * index + 2] * rows, rows)
        to_in = flags_ref[3 * index + 1] == 0

        @pl.when(to_in)
        def _():
            columns = pl.ds(pl.multiple_of(group * width, width), width)
            pltpu.make_async_copy(wide.at[index], in_ref.at[pl.ds(first, rows), columns], sems.at[index]).start()

        @pl.when(jnp.logical_not(to_in))
        def _():
            place = pl.ds(pl.multiple_of(group * width + first, rows), rows)
            pltpu.make_async_copy(wide.at[index], out_ref.at[place, :], sems.at[index]).start()

    for index in range(count):
        pltpu.make_async_copy(wide.at[index], out_ref.at[pl.ds(0, rows), :], sems.at[index]).wait()


def place_blocks(flags, sources, previous=()):
    rows, width = sources[0].shape
    count = len(sources)
    anywhere = pl.BlockSpec(memory_space=pl.ANY)
    return pl.pallas_call(
        functools.partial(place_kernel, count),
        name="place_blocks",
        grid_spec=pltpu.PrefetchScalarGridSpec(
            num_scalar_prefetch=1,
            grid=(1,),
            in_specs=[once((rows, width))] * count + [anywhere] * len(previous),
            out_specs=[anywhere, anywhere],
            scratch_shapes=[pltpu.VMEM((count, rows, width), F32), pltpu.SemaphoreType.DMA((count,))],
        ),
        out_shape=[
            jax.ShapeDtypeStruct((width, 4 * width), F32),
            jax.ShapeDtypeStruct((4 * width, width), F32),
        ],
        input_output_aliases={count + 1: 0, count + 2: 1} if previous else {},
        compiler_params=params(62),
        cost_estimate=cost(rows * width, 6 * rows * width),
    )(jnp.stack(flags).astype(I32), *sources, *previous)


def gather_rows(block, target, sources):
    count = sources[0].shape[0]
    total = None
    for chunk, source in enumerate(sources):
        picked = (iota((block, count), 1) + chunk * count == target).astype(F32).astype(BF)
        part = dot(picked, source[...])
        total = part if total is None else total + part
    return total


def back_kernel(
    block, back_first_ref, back_second_ref, target_ref, middle_ref, mixed_ref, out_grad_ref, gain_ref, weight_ref, sel_ref,
    grad_middle_ref, grad_mixed_ref, branch_ref, delta_ref, small_ref,
):
    step = pl.program_id(0)
    grad_h = gather_rows(block, target_ref[:, 0:1], (back_first_ref, back_second_ref))
    normed, inv_scale = norm_parts(middle_ref[...])
    gain = gain_ref[...]
    grad_middle = out_grad_ref[...].astype(F32) + norm_back(grad_h, normed, inv_scale, gain)
    grad_middle_ref[...] = grad_middle
    branch = grad_middle.astype(BF)
    branch_ref[...] = branch
    mixed = mixed_ref[...]
    grad_mixed = dot(branch, weight_ref[...], 1, 1).astype(BF)
    grad_mixed_ref[...] = grad_mixed
    product = grad_mixed.astype(F32) * mixed.astype(F32)
    high = product.astype(BF)
    low = (product - high.astype(F32)).astype(BF)
    sel = sel_ref[...]
    delta_ref[...] = dot(sel, high, 1, 1) + dot(sel, low, 1, 1)
    gain_grad = jnp.sum(grad_h * normed, 0, keepdims=True)
    bias_grad = jnp.sum(grad_h, 0, keepdims=True)

    @pl.when(step == 0)
    def _():
        small_ref[0:1, :] = gain_grad
        small_ref[1:2, :] = bias_grad

    @pl.when(step > 0)
    def _():
        small_ref[0:1, :] += gain_grad
        small_ref[1:2, :] += bias_grad


def middle_back(back_first, back_second, target_col, middle, mixed, out_grad, gain, weight):
    tokens, width = middle.shape
    slots = 2 * back_first.shape[0]
    block = 256
    heads = np.zeros((16, width), np.float32)
    for head in range(width // HEAD):
        heads[head, head * HEAD : (head + 1) * HEAD] = 1.0
    row = lambda w: pl.BlockSpec((block, w), lambda s: (s, 0))
    return pl.pallas_call(
        functools.partial(back_kernel, block),
        name="middle_back",
        grid=(tokens // block,),
        in_specs=[
            once((slots // 2, width)), once((slots // 2, width)), row(8), row(width), row(width), row(width),
            whole((1, width)), whole(weight.shape), whole((16, width)),
        ],
        out_specs=[
            row(width), row(width), row(width), pl.BlockSpec((16, block), lambda s: (0, s)),
            whole((8, width)),
        ],
        out_shape=[
            jax.ShapeDtypeStruct((tokens, width), F32),
            jax.ShapeDtypeStruct((tokens, width), BF),
            jax.ShapeDtypeStruct((tokens, width), BF),
            jax.ShapeDtypeStruct((16, tokens), F32),
            jax.ShapeDtypeStruct((8, width), F32),
        ],
        compiler_params=params(62),
        cost_estimate=cost(2 * slots * tokens * width + 4 * tokens * width * width, 24 * tokens * width),
    )(back_first, back_second, target_col, middle, mixed, out_grad, gain, weight, jnp.asarray(heads, BF))


def attend_back_kernel(
    block, start, side_ref, q_ref, k_ref, v_ref, do_ref, lse_ref, delta_ref, seg_row_ref, seg_col_ref, cos_ref, sin_ref,
    h_ref, turned_ref, branch_ref, dq_ref, dk_ref, dv_ref, keep_ref, send_ref, total, gathered,
):
    tokens = q_ref.shape[0]
    pair = pl.program_id(0) + start
    cosine, sine = cos_ref[...], sin_ref[...]
    lse = [lse_ref[pl.ds(2 * pair + head, 1), :] for head in range(2)]
    delta = [delta_ref[pl.ds(2 * pair + head, 1), :] for head in range(2)]
    for first in range(0, tokens, block):
        last = first + block
        span = tokens - first
        keys, values = k_ref[first:last, :], v_ref[first:last, :]
        allowed = seg_col_ref[first:last, 2:3] == seg_row_ref[:, first:]
        allowed &= iota((block, span), 0) <= iota((block, span), 1)
        dk = dv = dq = None
        for head in range(2):
            query = head_lanes(q_ref[first:, :], head)
            grads = head_lanes(do_ref[first:, :], head)
            scores = dot(keys, query, 1, 1)
            chance = jnp.where(allowed, jnp.exp(scores - lse[head][:, first:]), 0.0)
            grad_weights = dot(values, grads, 1, 1)
            grad_scores = (chance * (grad_weights - delta[head][:, first:])).astype(BF)
            part_v = dot(chance.astype(BF), grads)
            part_k = dot(grad_scores, query)
            part_q = dot(grad_scores, head_lanes(keys, head), 0, 0)
            dk = part_k if dk is None else dk + part_k
            dv = part_v if dv is None else dv + part_v
            dq = part_q if dq is None else dq + part_q
        dv_ref[first:last, :] = dv.astype(BF)
        cos_k, sin_k = cosine[first:last, :], sine[first:last, :]
        dk_ref[first:last, :] = (dk * cos_k - swap_halves(dk) * sin_k).astype(BF)
        if first == 0:
            total[...] = dq
        else:
            total[first:, :] += dq
    dq = total[...] * 0.125
    dq_ref[...] = (dq * cosine - swap_halves(dq) * sine).astype(BF)
    columns = branch_ref.shape[1]
    for part, ref in enumerate((dq_ref, dk_ref, dv_ref)):
        place = pl.ds(pl.multiple_of(part * columns + pl.program_id(0) * PAIR, PAIR), PAIR)
        gathered[:, place] = ref[...]

    @pl.when(pl.program_id(0) == pl.num_programs(0) - 1)
    def _():
        second = side_ref[0] == 1
        for rows in range(0, h_ref.shape[0], block):
            rows = slice(rows, rows + block)
            early = dot(h_ref[rows, :], gathered[:, : 2 * columns])
            late = [dot(h_ref[rows, :], gathered[:, 2 * columns :]), dot(turned_ref[rows, :], branch_ref[...])]
            for part in range(2):
                first = early[:, part * columns : (part + 1) * columns]
                keep_ref[part, rows, :] = jnp.where(second, late[part], first)
                send_ref[part, rows, :] = jnp.where(second, first, late[part]).astype(BF)


def attend_back(side, qkv, grad_mixed, lse, delta, seg_row, seg_col, cosine, sine, h_turned, mixed_turned, branch, start, count):
    tokens, width = grad_mixed.shape
    pairs = width // PAIR
    column = lambda part: pl.BlockSpec((tokens, PAIR), lambda g, side: (0, part * pairs + start + g))
    shared = whole((2, width, count * PAIR))
    branches = pl.BlockSpec(
        (tokens, count * PAIR), lambda g, side: (0, start // count), pipeline_mode=pl.Buffered(1)
    )
    out = jax.ShapeDtypeStruct((tokens, count * PAIR), BF)
    return pl.pallas_call(
        functools.partial(attend_back_kernel, 256, start),
        name="attend_back",
        grid_spec=pltpu.PrefetchScalarGridSpec(
            num_scalar_prefetch=1,
            grid=(count,),
            in_specs=[
                column(0), column(1), column(2), column(0), once(lse.shape), once(delta.shape),
                once((1, tokens)), once((tokens, 8)), once((tokens, PAIR)), once((tokens, PAIR)),
                once((width, tokens)), once((width, tokens)), branches,
            ],
            out_specs=[pl.BlockSpec((tokens, PAIR), lambda g, side: (0, g))] * 3 + [shared, shared],
            scratch_shapes=[pltpu.VMEM((tokens, PAIR), F32), pltpu.VMEM((tokens, 3 * count * PAIR), BF)],
        ),
        out_shape=[out] * 3
        + [
            jax.ShapeDtypeStruct((2, width, count * PAIR), F32),
            jax.ShapeDtypeStruct((2, width, count * PAIR), BF),
        ],
        compiler_params=params(62),
        cost_estimate=cost(20 * tokens * tokens * PAIR * count, 14 * tokens * PAIR * count, 2 * tokens * tokens * count),
    )(side, qkv, qkv, qkv, grad_mixed, lse, delta, seg_row, seg_col, cosine, sine, h_turned, mixed_turned, branch)


def final_kernel(x_ref, *refs):
    grad_refs = refs[:6]
    grad_middle_ref, weight_ref, gain_ref, input_grad_ref, small_ref = refs[6:]
    step = pl.program_id(0)
    width = x_ref.shape[1]
    columns = grad_refs[0].shape[1]
    normed, inv_scale = norm_parts(x_ref[...].astype(F32))
    grad_h = None
    for index, ref in enumerate(grad_refs):
        start = (index % 3) * width + (index // 3) * columns
        piece = dot(ref[...], weight_ref[:, start : start + columns], 1, 1)
        grad_h = piece if grad_h is None else grad_h + piece
    input_grad_ref[...] = grad_middle_ref[...] + norm_back(grad_h, normed, inv_scale, gain_ref[...])
    gain_grad = jnp.sum(grad_h * normed, 0, keepdims=True)
    bias_grad = jnp.sum(grad_h, 0, keepdims=True)

    @pl.when(step == 0)
    def _():
        small_ref[0:1, :] = gain_grad
        small_ref[1:2, :] = bias_grad

    @pl.when(step > 0)
    def _():
        small_ref[0:1, :] += gain_grad
        small_ref[1:2, :] += bias_grad


def final_part(x, grads, grad_middle, weight, gain):
    tokens, width = x.shape
    columns = grads[0].shape[1]
    block = 256
    row = lambda w: pl.BlockSpec((block, w), lambda s: (s, 0))
    return pl.pallas_call(
        final_kernel,
        name="first_back",
        grid=(tokens // block,),
        in_specs=[row(width)] + [row(columns)] * 6 + [row(width), once(weight.shape), whole((1, width))],
        out_specs=[row(width), whole((8, width))],
        out_shape=[
            jax.ShapeDtypeStruct((tokens, width), F32),
            jax.ShapeDtypeStruct((8, width), F32),
        ],
        compiler_params=params(62),
        cost_estimate=cost(6 * tokens * width * width, 6 * width * width + 16 * tokens * width),
    )(x, *grads, grad_middle, weight, gain)


def output_kernel(block, result_ref, target_ref, middle_ref, out_ref):
    out_ref[...] = (middle_ref[...] + gather_rows(block, target_ref[:, 1:2], (result_ref,))).astype(BF)


def block_output(result, place_col, middle):
    tokens, width = middle.shape
    slots = result.shape[0]
    block = 256
    row = lambda w: pl.BlockSpec((block, w), lambda s: (s, 0))
    return pl.pallas_call(
        functools.partial(output_kernel, block),
        name="block_output",
        grid=(tokens // block,),
        in_specs=[once((slots, width)), row(8), row(width)],
        out_specs=row(width),
        out_shape=jax.ShapeDtypeStruct((tokens, width), BF),
        compiler_params=params(62),
        cost_estimate=cost(2 * slots * tokens * width, 10 * tokens * width),
    )(result, place_col, middle)


def shared_out_kernel(flag_ref, low_ref, high_ref, *refs):
    qkv_ref, proj_ref, wide, sems = refs[-4:]
    width, columns = wide.shape[2:]
    for half in range(2):
        part = 2 * flag_ref[0] + half
        for index, source in enumerate((low_ref, high_ref)):
            slot = 2 * half + index
            wide[half, index] = source[half].astype(F32)
            start = pl.multiple_of(part * width + index * columns, columns)

            @pl.when(part < 3)
            def _():
                pltpu.make_async_copy(
                    wide.at[half, index], qkv_ref.at[:, pl.ds(start, columns)], sems.at[slot]
                ).start()

            @pl.when(part == 3)
            def _():
                pltpu.make_async_copy(
                    wide.at[half, index], proj_ref.at[:, pl.ds(index * columns, columns)], sems.at[slot]
                ).start()

    for slot in range(4):
        pltpu.make_async_copy(
            wide.at[slot // 2, slot % 2], proj_ref.at[:, pl.ds(0, columns)], sems.at[slot]
        ).wait()


def shared_outputs(flag, low, high, previous=()):
    _, width, columns = low.shape
    anywhere = pl.BlockSpec(memory_space=pl.ANY)
    return pl.pallas_call(
        shared_out_kernel,
        name="shared_outputs",
        grid_spec=pltpu.PrefetchScalarGridSpec(
            num_scalar_prefetch=1,
            grid=(1,),
            in_specs=[once(low.shape)] * 2 + [anywhere] * len(previous),
            out_specs=[anywhere, anywhere],
            scratch_shapes=[pltpu.VMEM((2, 2, width, columns), F32), pltpu.SemaphoreType.DMA((4,))],
        ),
        out_shape=[
            jax.ShapeDtypeStruct((width, 3 * width), F32),
            jax.ShapeDtypeStruct((width, width), F32),
        ],
        input_output_aliases={3: 0, 4: 1} if previous else {},
        compiler_params=params(62),
        cost_estimate=cost(width, width * width),
    )(flag, low, high, *previous)


def partner(axis, bit):
    return [(i, i ^ bit) for i in range(lax.axis_size(axis))]


def side(axis, bit):
    return (lax.axis_index(axis) // bit) % 2


def axis_bits(axis):
    bits, bit = [], 1
    while bit < lax.axis_size(axis):
        bits.append((axis, bit))
        bit *= 2
    return bits


def reduce_step(total, axis, bit):
    if total.shape[0] == 1:
        total = total.astype(BF)
        return total.astype(F32) + lax.ppermute(total, axis, partner(axis, bit)).astype(F32)
    mine = side(axis, bit)
    half = total.shape[0] // 2
    keep = lax.dynamic_slice_in_dim(total, mine * half, half, 0)
    send = lax.dynamic_slice_in_dim(total, (1 - mine) * half, half, 0)
    return keep + lax.ppermute(send.astype(BF), axis, partner(axis, bit)).astype(F32)


def gather_step(total, axis, bit):
    got = lax.ppermute(total, axis, partner(axis, bit))
    return jnp.where(side(axis, bit) == 0, jnp.concatenate([total, got], 0), jnp.concatenate([got, total], 0))


def add_partner(rows, axis, bit):
    return rows + lax.ppermute(rows, axis, partner(axis, bit))


def local(
    hidden_in, token_ids, hash_table, segment_ids, ln1_gain, ln1_bias, qkv_weight, proj_weight,
    ln2_gain, ln2_bias, expert_in, expert_out, out_grad,
):
    tokens, width = hidden_in.shape
    experts = lax.axis_size("expert")
    devices = lax.axis_size("dp") * experts
    half = tokens // experts
    row = lambda vector: vector.reshape(1, width)
    cosine, sine = (jnp.asarray(table) for table in angle_tables(tokens))
    seg_row = segment_ids.reshape(1, tokens)
    weight_in, weight_out = expert_in[0], expert_out[0]

    def exchange(rows):
        sent = rows.reshape(experts, rows.shape[0] // experts, width)
        return lax.all_to_all(sent, "expert", split_axis=0, concat_axis=0, tiled=True)

    def exchange_half(rows):
        return exchange(rows).reshape(tokens, width)

    def split(rows):
        return rows[:tokens], rows[tokens:]

    x_side, y_side = side("dp", 1), side("dp", 2)
    place_here = lax.axis_index("expert")
    perm = jnp.stack([1 - x_side, 3 - y_side, x_side, 2 + y_side, y_side, x_side, place_here]).astype(I32)
    me = jnp.reshape(place_here, (1,)).astype(I32)
    tie = lambda *values: lax.optimization_barrier(values)

    columns, leaving, counts, sent_grads = route(me, token_ids, seg_row, hash_table, out_grad, experts, half)
    sent_grads, hidden_in = tie(sent_grads, hidden_in)
    grad_rows = exchange(sent_grads)
    qkv, h_turned = first_half(hidden_in, row(ln1_gain), row(ln1_bias), qkv_weight, cosine, sine)
    mixed, mixed_turned, lse = attend(qkv, seg_row, columns)
    middle, sent_rows = middle_part(mixed, proj_weight, hidden_in, row(ln2_gain), row(ln2_bias), leaving)
    sent_first, sent_second = split(sent_rows)
    sent_first = sent_first.reshape(experts, half, width)
    rows_first = [sent_first[0]] + [
        lax.ppermute(sent_first[bits], "expert", partner("expert", bits)) for bits in range(1, experts)
    ]
    slopes = grads_inside(me, grad_rows, weight_out)
    sent_second, grad_rows, slopes, *rows_first = tie(sent_second, grad_rows, slopes, *rows_first)
    rows_second = exchange_half(sent_second)

    previous, act_first, back_first = expert_rows(rows_first, grad_rows, slopes, weight_in, perm)
    back_first, rows_second = tie(back_first, rows_second)
    back_first = exchange_half(back_first)
    early_x, late_x, early_y, late_y, keep, act_second, back_second = expert_rows(
        [rows_second], grad_rows, slopes, weight_in, perm, previous
    )
    across_x = lambda value: lax.ppermute(value, "dp", partner("dp", 1))
    across_y = lambda value: lax.ppermute(value, "dp", partner("dp", 2))
    back_second, back_first = tie(back_second, back_first)
    back_second = exchange_half(back_second)
    early_x, early_y = across_x(early_x), across_y(early_y)
    late_x, late_y = across_x(late_x), across_y(late_y)
    result = expert_result(me, act_first, act_second, weight_out, experts)
    result, back_second = tie(result, back_second)

    plus = lambda *values: sum(value.astype(F32) for value in values).astype(BF)
    send_x, send_y = plus(keep[0, 0], early_x), plus(keep[1, 0], early_y)
    send_x, send_y, back_second = tie(send_x, send_y, back_second)
    other_x, other_y = across_y(send_x), across_x(send_y)
    grad_middle, grad_mixed, branch, delta, small_two = middle_back(
        back_first, back_second, columns, middle, mixed, out_grad, row(ln2_gain), proj_weight
    )
    grad_mixed, late_x, late_y = tie(grad_mixed, late_x, late_y)

    pairs = width // PAIR
    back_of = lambda grads, start: attend_back(
        core_side, qkv, grads, lse, delta, seg_row, columns, cosine, sine, h_turned, mixed_turned, branch, start, pairs // 2
    )
    core_side = jnp.reshape(side("expert", 1), (1,)).astype(I32)
    across_core = lambda value: lax.ppermute(value, "expert", partner("expert", 1))
    *grads_low, low, send_low = back_of(grad_mixed, 0)
    other_x, other_y, send_low, grad_mixed = tie(other_x, other_y, send_low, grad_mixed)
    runs = [slice(0, width // 2), slice(width // 2, width)]
    total_x = plus(keep[0, 1], late_x, other_x)
    total_y = plus(keep[1, 1], late_y, other_y)
    total_x, total_y, send_low, grad_mixed, result = tie(total_x, total_y, send_low, grad_mixed, result)
    result = exchange(result.reshape(2 * tokens, width))
    near_x, near_y = across_y(total_x), across_x(total_y)
    far_x, far_y = across_x(total_x[runs[0]]), across_y(total_y[runs[0]])
    got_low = across_core(send_low)
    *grads_high, high, send_high = back_of(grad_mixed, pairs // 2)
    near_x, near_y, got_low, send_high = tie(near_x, near_y, got_low, send_high)
    both_runs = lambda group, which: [group, which, 0, group, which, 1]
    grad_in, grad_out = place_blocks(
        [x_side, y_side, 0, x_side, 1 - y_side, 0, 2 + y_side, x_side, 0, 2 + y_side, 1 - x_side, 0],
        [total_x, near_x, total_y, near_y],
    )
    send_high, grad_in, grad_out, far_x, far_y = tie(send_high, grad_in, grad_out, far_x, far_y)
    got_high = across_core(send_high)

    low = (low + got_low.astype(F32)).reshape(8, width // 4, width // 2)
    high = (high + got_high.astype(F32)).reshape(8, width // 4, width // 2)
    far_bits = axis_bits("expert")[1:]
    low_order = axis_bits("dp") + far_bits
    high_order = axis_bits("dp")[::-1] + far_bits

    def reduce_both(low, high, step):
        return reduce_step(low, *low_order[step]), reduce_step(high, *high_order[step])

    low, high = reduce_both(low, high, 0)
    input_grad, small_one = final_part(
        hidden_in, list(grads_low) + list(grads_high), grad_middle, qkv_weight, row(ln1_gain)
    )
    low, high, small_one = tie(low, high, small_one)
    small = jnp.concatenate(
        [small_one[:2], small_two[:2], jnp.pad(counts, (0, width - experts))[None], jnp.zeros((3, width), F32)], 0
    )
    for axis, bit in axis_bits("dp"):
        small = add_partner(small, axis, bit)
    low, high = reduce_both(low, high, 1)
    total_x, total_y, near_x, near_y = (
        [value[run] for run in runs] for value in (total_x, total_y, near_x, near_y)
    )
    low, high, small, total_x, total_y, near_x, near_y, result = tie(
        low, high, small, total_x, total_y, near_x, near_y, result
    )
    far_x, far_y = [far_x, across_x(total_x[1])], [far_y, across_y(total_y[1])]
    last_x, last_y = [across_x(run) for run in near_x], [across_y(run) for run in near_y]
    both = jnp.concatenate([low, high], 2)
    small = add_partner(small, "expert", 1)
    both = reduce_step(both, *far_bits[0])
    both, small, far_x, far_y = tie(both, small, far_x, far_y)
    small = add_partner(small, *far_bits[0])
    both = reduce_step(both, *far_bits[1])
    both, small, last_x[0], last_y[0] = tie(both, small, last_x[0], last_y[0])
    for axis, bit in far_bits[2:]:
        both = reduce_step(both, axis, bit)
    for axis, bit in far_bits[1:]:
        small = add_partner(small, axis, bit)
    both = gather_step(both.astype(BF), *far_bits[0])
    both, last_x, last_y, small = tie(both, last_x, last_y, small)
    low, high = both[:, :, : width // 2], both[:, :, width // 2 :]
    low, high = gather_step(low, *low_order[1]), gather_step(high, *high_order[1])
    grad_in, grad_out = place_blocks(
        both_runs(1 - x_side, y_side) + both_runs(1 - x_side, 1 - y_side)
        + both_runs(3 - y_side, x_side) + both_runs(3 - y_side, 1 - x_side),
        [*far_x, *last_x, *far_y, *last_y], (grad_in, grad_out),
    )
    low, high, grad_in, grad_out = tie(low, high, grad_in, grad_out)
    low, high = gather_step(low, *low_order[0]), gather_step(high, *high_order[0])
    block_out = block_output(result.reshape(2 * tokens, width), columns, middle)
    low, high, block_out = tie(low, high, block_out)
    low, high = low.reshape(2, width, width // 2), high.reshape(2, width, width // 2)
    got_low, got_high = across_core(low), across_core(high)
    qkv_grad, proj_sum = shared_outputs(core_side, low, high)
    got_low, got_high, qkv_grad, proj_sum = tie(got_low, got_high, qkv_grad, proj_sum)
    qkv_grad, proj_sum = shared_outputs(1 - core_side, got_low, got_high, (qkv_grad, proj_sum))
    load = small[4, :experts] * (experts / (tokens * devices))
    return (
        block_out,
        input_grad,
        small[0],
        small[1],
        qkv_grad,
        proj_sum,
        small[2],
        small[3],
        grad_in[None],
        grad_out[None],
        load,
    )


def solution(mesh):
    split, copied, owned = P(("dp", "expert")), P(), P("expert")
    in_specs = (
        split, split, copied, split, copied, copied, copied, copied, copied, copied, owned, owned, split,
    )
    out_specs = (
        split, split, copied, copied, copied, copied, copied, copied, owned, owned, copied,
    )
    return jax.shard_map(local, mesh=mesh, in_specs=in_specs, out_specs=out_specs, check_vma=False)
```

```python
import functools
import numpy as np
import jax
import jax.numpy as jnp
from jax import lax
from jax.experimental import pallas as pl
from jax.experimental.pallas import tpu as pltpu
from jax.sharding import PartitionSpec as P

HEAD = 64
EPSILON = 1e-05
BF = jnp.bfloat16
F32 = jnp.float32
I32 = jnp.int32
PAIR = 2 * HEAD
NEG = -1e30


def params(mib):
    return pltpu.CompilerParams(vmem_limit_bytes=mib << 20)


def cost(flops, bytes_accessed, transcendentals=0):
    return pl.CostEstimate(flops=1, bytes_accessed=1, transcendentals=0)


def dot(left, right, left_dim=1, right_dim=0):
    return lax.dot_general(
        left, right, (((left_dim,), (right_dim,)), ((), ())), preferred_element_type=F32
    )


def whole(shape):
    return pl.BlockSpec(shape, lambda *_: (0,) * len(shape))


def iota(shape, dim):
    return lax.broadcasted_iota(I32, shape, dim)


def norm_parts(rows):
    centred = rows - jnp.mean(rows, -1, keepdims=True)
    inv_scale = lax.rsqrt(jnp.mean(centred * centred, -1, keepdims=True) + EPSILON)
    return centred * inv_scale, inv_scale


def norm_back(grad_out, normed, inv_scale, gain):
    scaled = grad_out * gain
    centre = jnp.mean(scaled, -1, keepdims=True)
    along = jnp.mean(scaled * normed, -1, keepdims=True)
    return inv_scale * (scaled - centre - normed * along)


def one_hot_rows(target, first, count):
    return (iota((count, target.shape[1]), 0) + first == target).astype(F32).astype(BF)


def route_kernel(
    experts, half, block, me_ref, ids_ref, segments_ref, table_ref, grad_ref,
    columns_ref, leaving_ref, counts_ref, sent_ref, place,
):
    tokens = ids_ref.shape[1]
    rows = table_ref.shape[0]
    padded = counts_ref.shape[0]
    step = pl.program_id(0)

    @pl.when(step == 0)
    def _():
        ids = ids_ref[...]
        picked = (iota((rows, tokens), 0) == (ids >> 7)).astype(F32).astype(BF)
        found = dot(table_ref[...], picked, 0, 0)
        chosen = jnp.sum(
            jnp.where(iota((128, tokens), 0) == (ids & 127), found, 0.0), 0, keepdims=True
        ).astype(I32)
        member = (iota((padded, tokens), 0) == chosen).astype(F32)
        earlier = (iota((tokens, tokens), 0) < iota((tokens, tokens), 1)).astype(F32).astype(BF)
        rank = dot(member.astype(BF), earlier)
        slot = jnp.sum(member * rank, 0, keepdims=True).astype(I32)
        place[...] = chosen * (2 * half) + slot
        late = slot >= half
        second = experts * half + chosen * half + slot - half
        target = jnp.where(late, second, chosen * half + slot)
        lines = [target, place[...], segments_ref[...], jnp.zeros((5, tokens), I32)]
        columns_ref[...] = jnp.concatenate(lines, 0).T
        leaving_ref[...] = jnp.where(late, second, (chosen ^ me_ref[0]) * half + slot)
        counts_ref[...] = jnp.broadcast_to(jnp.sum(member, 1, keepdims=True), counts_ref.shape)

    sent_ref[...] = dot(one_hot_rows(place[...], step * block, block), grad_ref[...]).astype(BF)


def route(me, token_ids, segments, hash_table, out_grad, experts, half):
    tokens, width = out_grad.shape
    slots = 2 * tokens
    block = 256
    padded = max(experts, 16)
    rows = -(-hash_table.shape[0] // (128 * 128)) * 128
    table = jnp.pad(hash_table, (0, rows * 128 - hash_table.shape[0])).reshape(rows, 128).astype(BF)
    columns, leaving, counts, sent = pl.pallas_call(
        functools.partial(route_kernel, experts, half, block),
        name="route",
        grid_spec=pltpu.PrefetchScalarGridSpec(
            num_scalar_prefetch=1,
            grid=(slots // block,),
            in_specs=[whole((1, tokens)), whole((1, tokens)), whole((rows, 128)), whole((tokens, width))],
            out_specs=[
                whole((tokens, 8)),
                whole((1, tokens)),
                whole((padded, 128)),
                pl.BlockSpec((block, width), lambda s, me: (s, 0)),
            ],
            scratch_shapes=[pltpu.VMEM((1, tokens), I32)],
        ),
        out_shape=[
            jax.ShapeDtypeStruct((tokens, 8), I32),
            jax.ShapeDtypeStruct((1, tokens), I32),
            jax.ShapeDtypeStruct((padded, 128), F32),
            jax.ShapeDtypeStruct((slots, width), BF),
        ],
        compiler_params=params(62),
        cost_estimate=cost(2 * slots * tokens * width, 8 * tokens * width),
    )(me, token_ids.reshape(1, tokens), segments, table, out_grad)
    return columns, leaving, counts[:experts, 0], sent


def swap_halves(rows):
    half = HEAD // 2
    width = rows.shape[1]
    low = (iota(rows.shape, 1) & half) == 0
    return jnp.where(low, pltpu.roll(rows, width - half, 1), pltpu.roll(rows, half, 1))


def pre_kernel(x_ref, gain_ref, bias_ref, weight_ref, cos_ref, sin_ref, qkv_ref, h_ref):
    width = x_ref.shape[1]
    normed, _ = norm_parts(x_ref[...].astype(F32))
    h_one = (normed * gain_ref[...] + bias_ref[...]).astype(BF)
    h_ref[...] = h_one.T
    cosine, sine = cos_ref[...], sin_ref[...]
    for part in range(3):
        raw = dot(h_one, weight_ref[:, part * width : (part + 1) * width])
        for pair in range(width // PAIR):
            piece = raw[:, pair * PAIR : (pair + 1) * PAIR]
            if part < 2:
                piece = piece * cosine + swap_halves(piece) * sine
            if part == 0:
                piece = piece * 0.125
            start = part * width + pair * PAIR
            qkv_ref[:, start : start + PAIR] = piece.astype(BF)


def angle_tables(tokens):
    half = HEAD // 2
    freq = np.float32(10000.0) ** (-np.arange(half, dtype=np.float32) / np.float32(half))
    angle = np.arange(tokens, dtype=np.float32)[:, None] * freq[None, :].astype(np.float32)
    cosine = np.cos(angle).astype(np.float32)
    sine = np.sin(angle).astype(np.float32)
    cosine = np.concatenate([cosine, cosine], 1)
    sine = np.concatenate([-sine, sine], 1)
    return np.concatenate([cosine, cosine], 1), np.concatenate([sine, sine], 1)


def first_half(x, gain, bias, weight, cosine, sine):
    tokens, width = x.shape
    block = 256
    row = lambda w: pl.BlockSpec((block, w), lambda s: (s, 0))
    return pl.pallas_call(
        pre_kernel,
        name="norm_project",
        grid=(tokens // block,),
        in_specs=[
            row(width), whole((1, width)), whole((1, width)), whole(weight.shape), row(PAIR), row(PAIR),
        ],
        out_specs=[row(3 * width), pl.BlockSpec((width, block), lambda s: (0, s))],
        out_shape=[
            jax.ShapeDtypeStruct((tokens, 3 * width), BF),
            jax.ShapeDtypeStruct((width, tokens), BF),
        ],
        compiler_params=params(62),
        cost_estimate=cost(6 * tokens * width * width, 6 * width * width + 12 * tokens * width),
    )(x, gain, bias, weight, cosine, sine)


def head_lanes(rows, head):
    return jnp.where((iota((1, PAIR), 1) >= HEAD) == bool(head), rows, jnp.zeros_like(rows))


def attend_kernel(block, q_ref, k_ref, v_ref, seg_row_ref, seg_col_ref, mixed_ref, turned_ref, lse_ref, stats):
    tokens = q_ref.shape[0]
    pair = pl.program_id(0)
    upper = iota((1, PAIR), 1) >= HEAD
    for first in range(0, tokens, block):
        last = first + block
        query = q_ref[first:last, :]
        allowed = seg_col_ref[first:last, 2:3] == seg_row_ref[:, :last]
        allowed &= iota((block, last), 1) <= iota((block, last), 0) + first
        halves = []
        for head in range(2):
            scores = dot(head_lanes(query, head), k_ref[:last, :], 1, 1)
            scores = jnp.where(allowed, scores, NEG)
            top = jnp.max(scores, -1, keepdims=True)
            weights = jnp.exp(scores - top)
            total = jnp.sum(weights, -1, keepdims=True)
            halves.append(dot(weights.astype(BF), v_ref[:last, :]) * (1.0 / total))
            lane = iota((1, 128), 1) == 2 * pair + head
            stats[first:last, :] = jnp.where(lane, top + jnp.log(total), stats[first:last, :])
        mixed_ref[first:last, :] = jnp.where(upper, halves[1], halves[0]).astype(BF)
    turned_ref[...] = mixed_ref[...].T

    @pl.when(pair == pl.num_programs(0) - 1)
    def _():
        lse_ref[...] = stats[...].T


def attend(qkv, seg_row, seg_col):
    tokens, width = qkv.shape[0], qkv.shape[1] // 3
    pairs = width // PAIR
    column = lambda part: pl.BlockSpec((tokens, PAIR), lambda g: (0, part * pairs + g))
    return pl.pallas_call(
        functools.partial(attend_kernel, 256),
        name="attend",
        grid=(pairs,),
        in_specs=[column(0), column(1), column(2), whole((1, tokens)), whole((tokens, 8))],
        out_specs=[column(0), pl.BlockSpec((PAIR, tokens), lambda g: (g, 0)), whole((128, tokens))],
        out_shape=[
            jax.ShapeDtypeStruct((tokens, width), BF),
            jax.ShapeDtypeStruct((width, tokens), BF),
            jax.ShapeDtypeStruct((128, tokens), F32),
        ],
        scratch_shapes=[pltpu.VMEM((tokens, 128), F32)],
        compiler_params=params(62),
        cost_estimate=cost(8 * tokens * tokens * width, 8 * tokens * width, tokens * tokens * width // HEAD),
    )(qkv, qkv, qkv, seg_row, seg_col)


def middle_kernel(block, mixed_ref, weight_ref, x_ref, gain_ref, bias_ref, target_ref, middle_ref, sent_ref, h_two):
    tokens = x_ref.shape[0]
    step = pl.program_id(0)

    @pl.when(step == 0)
    def _():
        for first in range(0, tokens, block):
            rows = slice(first, first + block)
            middle = x_ref[rows, :].astype(F32) + dot(mixed_ref[rows, :], weight_ref[...])
            middle_ref[rows, :] = middle
            normed, _ = norm_parts(middle)
            h_two[rows, :] = (normed * gain_ref[...] + bias_ref[...]).astype(BF)

    sent_ref[...] = dot(one_hot_rows(target_ref[...], step * block, block), h_two[...]).astype(BF)


def middle_part(mixed, weight, x, gain, bias, target):
    tokens, width = x.shape
    block = 256
    slots = 2 * tokens
    return pl.pallas_call(
        functools.partial(middle_kernel, block),
        name="project_dispatch",
        grid=(slots // block,),
        in_specs=[
            whole((tokens, width)), whole(weight.shape), whole((tokens, width)),
            whole((1, width)), whole((1, width)), whole((1, tokens)),
        ],
        out_specs=[whole((tokens, width)), pl.BlockSpec((block, width), lambda s: (s, 0))],
        out_shape=[
            jax.ShapeDtypeStruct((tokens, width), F32),
            jax.ShapeDtypeStruct((slots, width), BF),
        ],
        scratch_shapes=[pltpu.VMEM((tokens, width), BF)],
        compiler_params=params(62),
        cost_estimate=cost(2 * slots * tokens * width + 2 * tokens * width * width, 16 * tokens * width),
    )(mixed, weight, x, gain, bias, target)


ROOT = 0.7978845608028654
CUBE = 0.044715


def once(shape):
    return pl.BlockSpec(shape, lambda *_: (0,) * len(shape), pipeline_mode=pl.Buffered(1))


def in_distance_order(me, source_ref, target_ref, half):
    experts = source_ref.shape[0]
    for distance in range(experts):
        target_ref[distance * half : (distance + 1) * half, :] = source_ref[me ^ distance, :half, :]


def slope_kernel(me_ref, grads_ref, wout_ref, out_ref, near):
    experts, rows, width = grads_ref.shape
    half = rows // 2
    count = experts * half

    @pl.when(pl.program_id(0) == 0)
    def _():
        in_distance_order(me_ref[0], grads_ref, near, half)

    weight_out = wout_ref[...]
    out_ref[:count, :] = dot(near[...], weight_out, 1, 1).astype(BF)
    out_ref[count:, :] = dot(grads_ref[:, half:, :].reshape(count, width), weight_out, 1, 1).astype(BF)


def grads_inside(me, grads, weight_out):
    experts, rows, width = grads.shape
    count = experts * rows
    units = weight_out.shape[0]
    tile = 768
    return pl.pallas_call(
        slope_kernel,
        name="grads_inside",
        grid_spec=pltpu.PrefetchScalarGridSpec(
            num_scalar_prefetch=1,
            grid=(units // tile,),
            in_specs=[once(grads.shape), pl.BlockSpec((tile, width), lambda s, me: (s, 0))],
            out_specs=pl.BlockSpec((count, tile), lambda s, me: (0, s)),
            scratch_shapes=[pltpu.VMEM((count // 2, width), BF)],
        ),
        out_shape=jax.ShapeDtypeStruct((count, units), BF),
        compiler_params=params(62),
        cost_estimate=cost(2 * count * width * units, 4 * count * units),
    )(me, grads, weight_out)


def expert_products(block, rows_ref, grads, slope_ref, weight_in, act_ref, back):
    din = dout = None
    for first in range(0, rows_ref.shape[0], block):
        span = slice(first, first + block)
        rows = rows_ref[span, :]
        inner = dot(rows, weight_in)
        square = inner * inner
        tanh = jnp.tanh(inner * (ROOT + (ROOT * CUBE) * square))
        gate = 0.5 + 0.5 * tanh
        act = inner * gate
        slope = gate + act * (1.0 - tanh) * (ROOT + (3.0 * ROOT * CUBE) * square)
        act = act.astype(BF)
        act_ref[span, :] = act
        grad_inner = (slope_ref[span, :] * slope).astype(BF)
        back[span, :] += dot(grad_inner, weight_in, 1, 1)
        part_in = dot(rows, grad_inner, 0, 0)
        part_out = dot(act, grads[span, :], 0, 0)
        din = part_in if din is None else din + part_in
        dout = part_out if dout is None else dout + part_out
    return din, dout


def first_kernel(block, groups, perm_ref, *refs):
    grads_ref, slope_ref, win_ref, grad_ref, act_ref, back_ref, back, rows_ref, all_grads = refs[-9:]
    pieces = refs[:-9]
    experts, half, width = grads_ref.shape
    step = pl.program_id(0)

    @pl.when(step == 0)
    def _():
        back[...] = jnp.zeros_like(back)
        in_distance_order(perm_ref[groups], grads_ref, all_grads, half)
        for distance, piece in enumerate(pieces):
            rows_ref[distance * half : (distance + 1) * half, :] = piece[...]

    din, dout = expert_products(block, rows_ref, all_grads[...], slope_ref, win_ref[...], act_ref, back)
    grad_ref[0, 0] = din.astype(BF)
    grad_ref[0, 1] = dout.astype(BF)

    @pl.when(step == groups - 1)
    def _():
        for distance in range(experts):
            place = pl.multiple_of((perm_ref[groups] ^ distance) * half, half)
            back_ref[pl.ds(place, half), :] = back[distance * half : (distance + 1) * half, :].astype(BF)


def second_kernel(block, groups, send, perm_ref, *refs):
    rows_ref, grads_ref, slope_ref, win_ref, previous_ref = refs[:5]
    act_ref, back_ref, back = refs[-3:]
    experts, half, width = grads_ref.shape
    step = pl.program_id(0)

    @pl.when(step == 0)
    def _():
        back[...] = jnp.zeros_like(back) if send else refs[5][...]

    grads = grads_ref[...].reshape(experts * half, width)
    din, dout = expert_products(block, rows_ref, grads, slope_ref, win_ref[...], act_ref, back)
    din = din + previous_ref[0, 0].astype(F32)
    dout = dout + previous_ref[0, 1].astype(F32)
    swap = perm_ref[groups + step] == 1
    early = jnp.where(swap, din, dout).astype(BF)
    late = jnp.where(swap, dout, din).astype(BF)
    if send:
        for group in range(groups):

            @pl.when(step == group)
            def _():
                refs[5 + group][0] = early
                refs[5 + group][1] = late

    else:
        refs[6][0, 0] = early
        refs[6][0, 1] = late

    @pl.when(step == groups - 1)
    def _():
        back_ref[...] = back[...].astype(back_ref.dtype)


def expert_first(rows, grads, slopes, weight_in, perm):
    experts, slots, width = grads.shape
    half = slots // 2
    count = experts * half
    groups = 4
    units = weight_in.shape[1]
    tile = units // groups
    in_specs = [once(piece.shape) for piece in rows] + [
        pl.BlockSpec((experts, half, width), lambda s, perm: (0, 0, 0), pipeline_mode=pl.Buffered(1)),
        pl.BlockSpec((count, tile), lambda s, perm: (0, perm[s])),
        pl.BlockSpec((width, tile), lambda s, perm: (0, perm[s])),
    ]
    return pl.pallas_call(
        functools.partial(first_kernel, 512, groups),
        name="expert_first",
        grid_spec=pltpu.PrefetchScalarGridSpec(
            num_scalar_prefetch=1,
            grid=(groups,),
            in_specs=in_specs,
            out_specs=[
                pl.BlockSpec((1, 2, tile, width), lambda s, perm: (s, 0, 0, 0)),
                pl.BlockSpec((count, tile), lambda s, perm: (0, s)),
                whole((count, width)),
            ],
            scratch_shapes=[pltpu.VMEM((count, width), F32)] + [pltpu.VMEM((count, width), BF)] * 2,
        ),
        out_shape=[
            jax.ShapeDtypeStruct((groups, 2, tile, width), BF),
            jax.ShapeDtypeStruct((count, units), BF),
            jax.ShapeDtypeStruct((count, width), BF),
        ],
        compiler_params=params(62),
        cost_estimate=cost(8 * count * width * units, 12 * width * units + 6 * count * units, count * units),
    )(perm, *rows, grads, slopes, weight_in)


def expert_second(rows, grads, slopes, weight_in, perm, previous, offset, carry=None):
    experts, slots, width = grads.shape
    half = slots // 2
    count = experts * half
    groups = 2
    tile = weight_in.shape[1] // 4
    send = carry is None
    grad_spec = pl.BlockSpec((1, 2, tile, width), lambda s, perm: (s + offset, 0, 0, 0))
    in_specs = [
        once((count, width)),
        pl.BlockSpec((experts, half, width), lambda s, perm: (0, 1, 0), pipeline_mode=pl.Buffered(1)),
        pl.BlockSpec((count, tile), lambda s, perm: (1, perm[s])),
        pl.BlockSpec((width, tile), lambda s, perm: (0, perm[s])),
        grad_spec,
    ]
    operands = [rows, grads, slopes, weight_in, previous]
    if send:
        out_specs = [once((2, tile, width))] * groups
        out_shapes = [jax.ShapeDtypeStruct((2, tile, width), BF)] * groups
    else:
        in_specs.append(once((count, width)))
        operands.append(carry)
        out_specs = [pl.BlockSpec((1, 2, tile, width), lambda s, perm: (s, 0, 0, 0))]
        out_shapes = [jax.ShapeDtypeStruct((groups, 2, tile, width), BF)]
    return pl.pallas_call(
        functools.partial(second_kernel, 512, groups, send),
        name="expert_second",
        grid_spec=pltpu.PrefetchScalarGridSpec(
            num_scalar_prefetch=1,
            grid=(groups,),
            in_specs=in_specs,
            out_specs=out_specs + [pl.BlockSpec((count, tile), lambda s, perm: (0, s)), whole((count, width))],
            scratch_shapes=[pltpu.VMEM((count, width), F32)],
        ),
        out_shape=out_shapes
        + [
            jax.ShapeDtypeStruct((count, groups * tile), BF),
            jax.ShapeDtypeStruct((count, width), F32 if send else BF),
        ],
        compiler_params=params(46),
        cost_estimate=cost(4 * count * width * tile * groups, 12 * width * tile * groups, count * tile * groups),
    )(perm, *operands)


def result_kernel(perm_ref, first_ref, second_ref, third_ref, wout_ref, out_ref, total):
    step = pl.program_id(0)
    groups = pl.num_programs(0)
    experts, rows, width = out_ref.shape
    half = rows // 2

    @pl.when(step == 0)
    def _():
        total[...] = jnp.zeros_like(total)

    weight_out = wout_ref[...]
    total[0] += dot(first_ref[...], weight_out)
    total[1] += dot(jnp.where(step < 2, second_ref[...], third_ref[...]), weight_out)

    @pl.when(step == groups - 1)
    def _():
        out_ref[:, half:, :] = total[1].astype(BF).reshape(experts, half, width)
        for distance in range(experts):
            piece = total[0, distance * half : (distance + 1) * half, :]
            out_ref[perm_ref[4] ^ distance, :half, :] = piece.astype(BF)


def expert_result(perm, first, second, third, weight_out, experts):
    count, units = first.shape
    width = weight_out.shape[1]
    tile = units // 4
    shape = (experts, 2 * count // experts, width)
    return pl.pallas_call(
        result_kernel,
        name="expert_result",
        grid_spec=pltpu.PrefetchScalarGridSpec(
            num_scalar_prefetch=1,
            grid=(4,),
            in_specs=[
                pl.BlockSpec((count, tile), lambda s, perm: (0, s)),
                pl.BlockSpec((count, tile), lambda s, perm: (0, jnp.minimum(s, 1))),
                pl.BlockSpec((count, tile), lambda s, perm: (0, jnp.maximum(s - 2, 0))),
                pl.BlockSpec((tile, width), lambda s, perm: (perm[s], 0)),
            ],
            out_specs=whole(shape),
            scratch_shapes=[pltpu.VMEM((2, count, width), F32)],
        ),
        out_shape=jax.ShapeDtypeStruct(shape, BF),
        compiler_params=params(62),
        cost_estimate=cost(4 * count * width * units, 4 * count * units),
    )(perm, first, second, third, weight_out)


def place_kernel(count, flags_ref, *refs):
    sources, (in_ref, out_ref, wide, sems) = refs[:count], refs[-4:]
    rows, width = wide.shape[1:]
    for index, source in enumerate(sources):
        wide[index] = source[...].astype(F32)
        group, first = flags_ref[3 * index], pl.multiple_of(flags_ref[3 * index + 2] * rows, rows)
        to_in = flags_ref[3 * index + 1] == 0

        @pl.when(to_in)
        def _():
            columns = pl.ds(pl.multiple_of(group * width, width), width)
            pltpu.make_async_copy(wide.at[index], in_ref.at[pl.ds(first, rows), columns], sems.at[index]).start()

        @pl.when(jnp.logical_not(to_in))
        def _():
            place = pl.ds(pl.multiple_of(group * width + first, rows), rows)
            pltpu.make_async_copy(wide.at[index], out_ref.at[place, :], sems.at[index]).start()

    for index in range(count):
        pltpu.make_async_copy(wide.at[index], out_ref.at[pl.ds(0, rows), :], sems.at[index]).wait()


def place_blocks(flags, sources, previous=()):
    rows, width = sources[0].shape
    count = len(sources)
    anywhere = pl.BlockSpec(memory_space=pl.ANY)
    return pl.pallas_call(
        functools.partial(place_kernel, count),
        name="place_blocks",
        grid_spec=pltpu.PrefetchScalarGridSpec(
            num_scalar_prefetch=1,
            grid=(1,),
            in_specs=[once((rows, width))] * count + [anywhere] * len(previous),
            out_specs=[anywhere, anywhere],
            scratch_shapes=[pltpu.VMEM((count, rows, width), F32), pltpu.SemaphoreType.DMA((count,))],
        ),
        out_shape=[
            jax.ShapeDtypeStruct((width, 4 * width), F32),
            jax.ShapeDtypeStruct((4 * width, width), F32),
        ],
        input_output_aliases={count + 1: 0, count + 2: 1} if previous else {},
        compiler_params=params(62),
        cost_estimate=cost(rows * width, 6 * rows * width),
    )(jnp.stack(flags).astype(I32), *sources, *previous)


def gather_rows(block, target, sources):
    count = sources[0].shape[0]
    total = None
    for chunk, source in enumerate(sources):
        picked = (iota((block, count), 1) + chunk * count == target).astype(F32).astype(BF)
        part = dot(picked, source[...])
        total = part if total is None else total + part
    return total


def back_kernel(
    block, back_first_ref, back_second_ref, target_ref, middle_ref, mixed_ref, out_grad_ref, gain_ref, weight_ref, sel_ref,
    grad_middle_ref, grad_mixed_ref, branch_ref, delta_ref, small_ref,
):
    step = pl.program_id(0)
    grad_h = gather_rows(block, target_ref[:, 0:1], (back_first_ref, back_second_ref))
    normed, inv_scale = norm_parts(middle_ref[...])
    gain = gain_ref[...]
    grad_middle = out_grad_ref[...].astype(F32) + norm_back(grad_h, normed, inv_scale, gain)
    grad_middle_ref[...] = grad_middle
    branch = grad_middle.astype(BF)
    branch_ref[...] = branch
    mixed = mixed_ref[...]
    grad_mixed = dot(branch, weight_ref[...], 1, 1).astype(BF)
    grad_mixed_ref[...] = grad_mixed
    product = grad_mixed.astype(F32) * mixed.astype(F32)
    high = product.astype(BF)
    low = (product - high.astype(F32)).astype(BF)
    sel = sel_ref[...]
    delta_ref[...] = dot(sel, high, 1, 1) + dot(sel, low, 1, 1)
    gain_grad = jnp.sum(grad_h * normed, 0, keepdims=True)
    bias_grad = jnp.sum(grad_h, 0, keepdims=True)

    @pl.when(step == 0)
    def _():
        small_ref[0:1, :] = gain_grad
        small_ref[1:2, :] = bias_grad

    @pl.when(step > 0)
    def _():
        small_ref[0:1, :] += gain_grad
        small_ref[1:2, :] += bias_grad


def middle_back(back_first, back_second, target_col, middle, mixed, out_grad, gain, weight):
    tokens, width = middle.shape
    slots = 2 * back_first.shape[0]
    block = 256
    heads = np.zeros((16, width), np.float32)
    for head in range(width // HEAD):
        heads[head, head * HEAD : (head + 1) * HEAD] = 1.0
    row = lambda w: pl.BlockSpec((block, w), lambda s: (s, 0))
    return pl.pallas_call(
        functools.partial(back_kernel, block),
        name="middle_back",
        grid=(tokens // block,),
        in_specs=[
            once((slots // 2, width)), once((slots // 2, width)), row(8), row(width), row(width), row(width),
            whole((1, width)), whole(weight.shape), whole((16, width)),
        ],
        out_specs=[
            row(width), row(width), row(width), pl.BlockSpec((16, block), lambda s: (0, s)),
            whole((8, width)),
        ],
        out_shape=[
            jax.ShapeDtypeStruct((tokens, width), F32),
            jax.ShapeDtypeStruct((tokens, width), BF),
            jax.ShapeDtypeStruct((tokens, width), BF),
            jax.ShapeDtypeStruct((16, tokens), F32),
            jax.ShapeDtypeStruct((8, width), F32),
        ],
        compiler_params=params(50),
        cost_estimate=cost(2 * slots * tokens * width + 4 * tokens * width * width, 24 * tokens * width),
    )(back_first, back_second, target_col, middle, mixed, out_grad, gain, weight, jnp.asarray(heads, BF))


def attend_back_kernel(
    block, start, side_ref, q_ref, k_ref, v_ref, do_ref, lse_ref, delta_ref, seg_row_ref, seg_col_ref, cos_ref, sin_ref,
    h_ref, turned_ref, branch_ref, dq_ref, dk_ref, dv_ref, keep_ref, send_ref, total, gathered,
):
    tokens = q_ref.shape[0]
    pair = pl.program_id(0) + start
    cosine, sine = cos_ref[...], sin_ref[...]
    lse = [lse_ref[pl.ds(2 * pair + head, 1), :] for head in range(2)]
    delta = [delta_ref[pl.ds(2 * pair + head, 1), :] for head in range(2)]
    for first in range(0, tokens, block):
        last = first + block
        span = tokens - first
        keys, values = k_ref[first:last, :], v_ref[first:last, :]
        allowed = seg_col_ref[first:last, 2:3] == seg_row_ref[:, first:]
        allowed &= iota((block, span), 0) <= iota((block, span), 1)
        dk = dv = dq = None
        for head in range(2):
            query = head_lanes(q_ref[first:, :], head)
            grads = head_lanes(do_ref[first:, :], head)
            scores = dot(keys, query, 1, 1)
            chance = jnp.where(allowed, jnp.exp(scores - lse[head][:, first:]), 0.0)
            grad_weights = dot(values, grads, 1, 1)
            grad_scores = (chance * (grad_weights - delta[head][:, first:])).astype(BF)
            part_v = dot(chance.astype(BF), grads)
            part_k = dot(grad_scores, query)
            part_q = dot(grad_scores, head_lanes(keys, head), 0, 0)
            dk = part_k if dk is None else dk + part_k
            dv = part_v if dv is None else dv + part_v
            dq = part_q if dq is None else dq + part_q
        dv_ref[first:last, :] = dv.astype(BF)
        cos_k, sin_k = cosine[first:last, :], sine[first:last, :]
        dk_ref[first:last, :] = (dk * cos_k - swap_halves(dk) * sin_k).astype(BF)
        if first == 0:
            total[...] = dq
        else:
            total[first:, :] += dq
    dq = total[...] * 0.125
    dq_ref[...] = (dq * cosine - swap_halves(dq) * sine).astype(BF)
    columns = branch_ref.shape[1]
    for part, ref in enumerate((dq_ref, dk_ref, dv_ref)):
        place = pl.ds(pl.multiple_of(part * columns + pl.program_id(0) * PAIR, PAIR), PAIR)
        gathered[:, place] = ref[...]

    @pl.when(pl.program_id(0) == pl.num_programs(0) - 1)
    def _():
        second = side_ref[0] == 1
        for rows in range(0, h_ref.shape[0], block):
            rows = slice(rows, rows + block)
            early = dot(h_ref[rows, :], gathered[:, : 2 * columns])
            late = [dot(h_ref[rows, :], gathered[:, 2 * columns :]), dot(turned_ref[rows, :], branch_ref[...])]
            for part in range(2):
                first = early[:, part * columns : (part + 1) * columns]
                keep_ref[part, rows, :] = jnp.where(second, late[part], first)
                send_ref[part, rows, :] = jnp.where(second, first, late[part]).astype(BF)


def attend_back(side, qkv, grad_mixed, lse, delta, seg_row, seg_col, cosine, sine, h_turned, mixed_turned, branch, start, count):
    tokens, width = grad_mixed.shape
    pairs = width // PAIR
    column = lambda part: pl.BlockSpec((tokens, PAIR), lambda g, side: (0, part * pairs + start + g))
    shared = whole((2, width, count * PAIR))
    branches = pl.BlockSpec(
        (tokens, count * PAIR), lambda g, side: (0, start // count), pipeline_mode=pl.Buffered(1)
    )
    out = jax.ShapeDtypeStruct((tokens, count * PAIR), BF)
    return pl.pallas_call(
        functools.partial(attend_back_kernel, 256, start),
        name="attend_back",
        grid_spec=pltpu.PrefetchScalarGridSpec(
            num_scalar_prefetch=1,
            grid=(count,),
            in_specs=[
                column(0), column(1), column(2), column(0), once(lse.shape), once(delta.shape),
                once((1, tokens)), once((tokens, 8)), once((tokens, PAIR)), once((tokens, PAIR)),
                once((width, tokens)), once((width, tokens)), branches,
            ],
            out_specs=[pl.BlockSpec((tokens, PAIR), lambda g, side: (0, g))] * 3 + [shared, shared],
            scratch_shapes=[pltpu.VMEM((tokens, PAIR), F32), pltpu.VMEM((tokens, 3 * count * PAIR), BF)],
        ),
        out_shape=[out] * 3
        + [
            jax.ShapeDtypeStruct((2, width, count * PAIR), F32),
            jax.ShapeDtypeStruct((2, width, count * PAIR), BF),
        ],
        compiler_params=params(62),
        cost_estimate=cost(20 * tokens * tokens * PAIR * count, 14 * tokens * PAIR * count, 2 * tokens * tokens * count),
    )(side, qkv, qkv, qkv, grad_mixed, lse, delta, seg_row, seg_col, cosine, sine, h_turned, mixed_turned, branch)


def final_kernel(x_ref, *refs):
    grad_refs = refs[:6]
    grad_middle_ref, weight_ref, gain_ref, input_grad_ref, small_ref = refs[6:]
    step = pl.program_id(0)
    width = x_ref.shape[1]
    columns = grad_refs[0].shape[1]
    normed, inv_scale = norm_parts(x_ref[...].astype(F32))
    grad_h = None
    for index, ref in enumerate(grad_refs):
        start = (index % 3) * width + (index // 3) * columns
        piece = dot(ref[...], weight_ref[:, start : start + columns], 1, 1)
        grad_h = piece if grad_h is None else grad_h + piece
    input_grad_ref[...] = grad_middle_ref[...] + norm_back(grad_h, normed, inv_scale, gain_ref[...])
    gain_grad = jnp.sum(grad_h * normed, 0, keepdims=True)
    bias_grad = jnp.sum(grad_h, 0, keepdims=True)

    @pl.when(step == 0)
    def _():
        small_ref[0:1, :] = gain_grad
        small_ref[1:2, :] = bias_grad

    @pl.when(step > 0)
    def _():
        small_ref[0:1, :] += gain_grad
        small_ref[1:2, :] += bias_grad


def final_part(x, grads, grad_middle, weight, gain):
    tokens, width = x.shape
    columns = grads[0].shape[1]
    block = 256
    row = lambda w: pl.BlockSpec((block, w), lambda s: (s, 0))
    return pl.pallas_call(
        final_kernel,
        name="first_back",
        grid=(tokens // block,),
        in_specs=[row(width)] + [row(columns)] * 6 + [row(width), once(weight.shape), whole((1, width))],
        out_specs=[row(width), whole((8, width))],
        out_shape=[
            jax.ShapeDtypeStruct((tokens, width), F32),
            jax.ShapeDtypeStruct((8, width), F32),
        ],
        compiler_params=params(62),
        cost_estimate=cost(6 * tokens * width * width, 6 * width * width + 16 * tokens * width),
    )(x, *grads, grad_middle, weight, gain)


def output_kernel(block, result_ref, target_ref, middle_ref, out_ref):
    out_ref[...] = (middle_ref[...] + gather_rows(block, target_ref[:, 1:2], (result_ref,))).astype(BF)


def block_output(result, place_col, middle):
    tokens, width = middle.shape
    slots = result.shape[0]
    block = 256
    row = lambda w: pl.BlockSpec((block, w), lambda s: (s, 0))
    return pl.pallas_call(
        functools.partial(output_kernel, block),
        name="block_output",
        grid=(tokens // block,),
        in_specs=[once((slots, width)), row(8), row(width)],
        out_specs=row(width),
        out_shape=jax.ShapeDtypeStruct((tokens, width), BF),
        compiler_params=params(62),
        cost_estimate=cost(2 * slots * tokens * width, 10 * tokens * width),
    )(result, place_col, middle)


def shared_out_kernel(flag_ref, low_ref, high_ref, *refs):
    qkv_ref, proj_ref, wide, sems = refs[-4:]
    width, columns = wide.shape[2:]
    for half in range(2):
        part = 2 * flag_ref[0] + half
        for index, source in enumerate((low_ref, high_ref)):
            slot = 2 * half + index
            wide[half, index] = source[half].astype(F32)
            start = pl.multiple_of(part * width + index * columns, columns)

            @pl.when(part < 3)
            def _():
                pltpu.make_async_copy(
                    wide.at[half, index], qkv_ref.at[:, pl.ds(start, columns)], sems.at[slot]
                ).start()

            @pl.when(part == 3)
            def _():
                pltpu.make_async_copy(
                    wide.at[half, index], proj_ref.at[:, pl.ds(index * columns, columns)], sems.at[slot]
                ).start()

    for slot in range(4):
        pltpu.make_async_copy(
            wide.at[slot // 2, slot % 2], proj_ref.at[:, pl.ds(0, columns)], sems.at[slot]
        ).wait()


def shared_outputs(flag, low, high, previous=()):
    _, width, columns = low.shape
    anywhere = pl.BlockSpec(memory_space=pl.ANY)
    return pl.pallas_call(
        shared_out_kernel,
        name="shared_outputs",
        grid_spec=pltpu.PrefetchScalarGridSpec(
            num_scalar_prefetch=1,
            grid=(1,),
            in_specs=[once(low.shape)] * 2 + [anywhere] * len(previous),
            out_specs=[anywhere, anywhere],
            scratch_shapes=[pltpu.VMEM((2, 2, width, columns), F32), pltpu.SemaphoreType.DMA((4,))],
        ),
        out_shape=[
            jax.ShapeDtypeStruct((width, 3 * width), F32),
            jax.ShapeDtypeStruct((width, width), F32),
        ],
        input_output_aliases={3: 0, 4: 1} if previous else {},
        compiler_params=params(62),
        cost_estimate=cost(width, width * width),
    )(flag, low, high, *previous)


def partner(axis, bit):
    return [(i, i ^ bit) for i in range(lax.axis_size(axis))]


def side(axis, bit):
    return (lax.axis_index(axis) // bit) % 2


def axis_bits(axis):
    bits, bit = [], 1
    while bit < lax.axis_size(axis):
        bits.append((axis, bit))
        bit *= 2
    return bits


def reduce_step(total, axis, bit):
    if total.shape[0] == 1:
        total = total.astype(BF)
        return total.astype(F32) + lax.ppermute(total, axis, partner(axis, bit)).astype(F32)
    mine = side(axis, bit)
    half = total.shape[0] // 2
    keep = lax.dynamic_slice_in_dim(total, mine * half, half, 0)
    send = lax.dynamic_slice_in_dim(total, (1 - mine) * half, half, 0)
    return keep + lax.ppermute(send.astype(BF), axis, partner(axis, bit)).astype(F32)


def gather_step(total, axis, bit):
    got = lax.ppermute(total, axis, partner(axis, bit))
    return jnp.where(side(axis, bit) == 0, jnp.concatenate([total, got], 0), jnp.concatenate([got, total], 0))


def add_partner(rows, axis, bit):
    return rows + lax.ppermute(rows, axis, partner(axis, bit))


def local(
    hidden_in, token_ids, hash_table, segment_ids, ln1_gain, ln1_bias, qkv_weight, proj_weight,
    ln2_gain, ln2_bias, expert_in, expert_out, out_grad,
):
    tokens, width = hidden_in.shape
    experts = lax.axis_size("expert")
    devices = lax.axis_size("dp") * experts
    half = tokens // experts
    row = lambda vector: vector.reshape(1, width)
    cosine, sine = (jnp.asarray(table) for table in angle_tables(tokens))
    seg_row = segment_ids.reshape(1, tokens)
    weight_in, weight_out = expert_in[0], expert_out[0]

    def exchange(rows):
        sent = rows.reshape(experts, rows.shape[0] // experts, width)
        return lax.all_to_all(sent, "expert", split_axis=0, concat_axis=0, tiled=True)

    def exchange_half(rows):
        return exchange(rows).reshape(tokens, width)

    def split(rows):
        return rows[:tokens], rows[tokens:]

    x_side, y_side = side("dp", 1), side("dp", 2)
    place_here = lax.axis_index("expert")
    ints = lambda *values: jnp.stack(values).astype(I32)
    perm = ints(1 - x_side, 3 - y_side, x_side, 2 + y_side, place_here)
    perm_send = ints(1 - x_side, 3 - y_side, y_side, x_side)
    perm_keep = ints(x_side, 2 + y_side, y_side, x_side)
    me = jnp.reshape(place_here, (1,)).astype(I32)
    tie = lambda *values: lax.optimization_barrier(values)

    columns, leaving, counts, sent_grads = route(me, token_ids, seg_row, hash_table, out_grad, experts, half)
    sent_grads, hidden_in = tie(sent_grads, hidden_in)
    grad_rows = exchange(sent_grads)
    qkv, h_turned = first_half(hidden_in, row(ln1_gain), row(ln1_bias), qkv_weight, cosine, sine)
    mixed, mixed_turned, lse = attend(qkv, seg_row, columns)
    middle, sent_rows = middle_part(mixed, proj_weight, hidden_in, row(ln2_gain), row(ln2_bias), leaving)
    sent_first, sent_second = split(sent_rows)
    sent_first = sent_first.reshape(experts, half, width)
    rows_first = [sent_first[0]] + [
        lax.ppermute(sent_first[bits], "expert", partner("expert", bits)) for bits in range(1, experts)
    ]
    slopes = grads_inside(me, grad_rows, weight_out)
    sent_second, grad_rows, slopes, *rows_first = tie(sent_second, grad_rows, slopes, *rows_first)
    rows_second = exchange_half(sent_second)

    previous, act_first, back_first = expert_first(rows_first, grad_rows, slopes, weight_in, perm)
    back_first, rows_second = tie(back_first, rows_second)
    back_first = exchange_half(back_first)
    across_x = lambda value: lax.ppermute(value, "dp", partner("dp", 1))
    across_y = lambda value: lax.ppermute(value, "dp", partner("dp", 2))
    send_x, send_y, act_send, carry = expert_second(
        rows_second, grad_rows, slopes, weight_in, perm_send, previous, 0
    )
    got_x, got_y = across_x(send_x), across_y(send_y)
    keep, act_keep, back_second = expert_second(
        rows_second, grad_rows, slopes, weight_in, perm_keep, previous, 2, carry
    )
    back_second, back_first = tie(back_second, back_first)
    back_second = exchange_half(back_second)
    result = expert_result(perm, act_first, act_send, act_keep, weight_out, experts)
    got_x, got_y, result = tie(got_x, got_y, result)

    plus = lambda *values: sum(value.astype(F32) for value in values).astype(BF)
    other_x, other_y = across_y(plus(keep[0, 0], got_x[0])), across_x(plus(keep[1, 0], got_y[0]))
    grad_middle, grad_mixed, branch, delta, small_two = middle_back(
        back_first, back_second, columns, middle, mixed, out_grad, row(ln2_gain), proj_weight
    )
    grad_mixed, result = tie(grad_mixed, result)
    result = exchange(result.reshape(2 * tokens, width))
    grad_mixed, other_x, other_y = tie(grad_mixed, other_x, other_y)
    total_x, total_y = plus(keep[0, 1], got_x[1], other_x), plus(keep[1, 1], got_y[1], other_y)
    total_x, total_y, grad_mixed = tie(total_x, total_y, grad_mixed)
    near_x, near_y = across_y(total_x), across_x(total_y)
    far_x, far_y = across_x(total_x), across_y(total_y)

    pairs = width // PAIR
    back_of = lambda grads, start: attend_back(
        core_side, qkv, grads, lse, delta, seg_row, columns, cosine, sine, h_turned, mixed_turned, branch, start, pairs // 2
    )
    core_side = jnp.reshape(side("expert", 1), (1,)).astype(I32)
    across_core = lambda value: lax.ppermute(value, "expert", partner("expert", 1))
    *grads_low, low, send_low = back_of(grad_mixed, 0)
    send_low, grad_mixed, near_x, near_y = tie(send_low, grad_mixed, near_x, near_y)
    got_low = across_core(send_low)
    *grads_high, high, send_high = back_of(grad_mixed, pairs // 2)
    got_low, send_high = tie(got_low, send_high)
    low = (low + got_low.astype(F32)).reshape(8, width // 4, width // 2)
    got_high = across_core(send_high)
    got_high, far_x, far_y, low = tie(got_high, far_x, far_y, low)

    high = (high + got_high.astype(F32)).reshape(8, width // 4, width // 2)
    far_bits = axis_bits("expert")[1:]
    low_order = axis_bits("dp") + far_bits
    high_order = axis_bits("dp")[::-1] + far_bits

    def reduce_both(low, high, step):
        return reduce_step(low, *low_order[step]), reduce_step(high, *high_order[step])

    low, high = reduce_both(low, high, 0)
    input_grad, small_one = final_part(
        hidden_in, list(grads_low) + list(grads_high), grad_middle, qkv_weight, row(ln1_gain)
    )
    low, high, small_one = tie(low, high, small_one)
    small = jnp.concatenate(
        [small_one[:2], small_two[:2], jnp.pad(counts, (0, width - experts))[None], jnp.zeros((3, width), F32)], 0
    )
    for axis, bit in axis_bits("dp"):
        small = add_partner(small, axis, bit)
    low, high = reduce_both(low, high, 1)
    grad_in, grad_out = place_blocks(
        [x_side, y_side, 0, x_side, 1 - y_side, 0, 2 + y_side, x_side, 0, 2 + y_side, 1 - x_side, 0],
        [total_x, near_x, total_y, near_y],
    )
    low, high, small, near_x, near_y, result, grad_in, grad_out = tie(
        low, high, small, near_x, near_y, result, grad_in, grad_out
    )
    last_x, last_y = across_x(near_x), across_y(near_y)
    both = jnp.concatenate([low, high], 2)
    small = add_partner(small, "expert", 1)
    both = reduce_step(both, *far_bits[0])
    both, small = tie(both, small)
    small = add_partner(small, *far_bits[0])
    both = reduce_step(both, *far_bits[1])
    both, small = tie(both, small)
    for axis, bit in far_bits[2:]:
        both = reduce_step(both, axis, bit)
    for axis, bit in far_bits[1:]:
        small = add_partner(small, axis, bit)
    both = gather_step(both.astype(BF), *far_bits[0])
    both, last_x, last_y, small = tie(both, last_x, last_y, small)
    low, high = both[:, :, : width // 2], both[:, :, width // 2 :]
    low, high = gather_step(low, *low_order[1]), gather_step(high, *high_order[1])
    grad_in, grad_out = place_blocks(
        [1 - x_side, y_side, 0, 1 - x_side, 1 - y_side, 0, 3 - y_side, x_side, 0, 3 - y_side, 1 - x_side, 0],
        [far_x, last_x, far_y, last_y], (grad_in, grad_out),
    )
    low, high, grad_in, grad_out = tie(low, high, grad_in, grad_out)
    low, high = gather_step(low, *low_order[0]), gather_step(high, *high_order[0])
    block_out = block_output(result.reshape(2 * tokens, width), columns, middle)
    low, high, block_out = tie(low, high, block_out)
    low, high = low.reshape(2, width, width // 2), high.reshape(2, width, width // 2)
    got_low, got_high = across_core(low), across_core(high)
    qkv_grad, proj_sum = shared_outputs(core_side, low, high)
    got_low, got_high, qkv_grad, proj_sum = tie(got_low, got_high, qkv_grad, proj_sum)
    qkv_grad, proj_sum = shared_outputs(1 - core_side, got_low, got_high, (qkv_grad, proj_sum))
    load = small[4, :experts] * (experts / (tokens * devices))
    return (
        block_out,
        input_grad,
        small[0],
        small[1],
        qkv_grad,
        proj_sum,
        small[2],
        small[3],
        grad_in[None],
        grad_out[None],
        load,
    )


def solution(mesh):
    split, copied, owned = P(("dp", "expert")), P(), P("expert")
    in_specs = (
        split, split, copied, split, copied, copied, copied, copied, copied, copied, owned, owned, split,
    )
    out_specs = (
        split, split, copied, copied, copied, copied, copied, copied, owned, owned, copied,
    )
    return jax.shard_map(local, mesh=mesh, in_specs=in_specs, out_specs=out_specs, check_vma=False)
```

```python
import functools
import numpy as np
import jax
import jax.numpy as jnp
from jax import lax
from jax.experimental import pallas as pl
from jax.experimental.pallas import tpu as pltpu
from jax.sharding import PartitionSpec as P

HEAD = 64
EPSILON = 1e-05
BF = jnp.bfloat16
F32 = jnp.float32
I32 = jnp.int32
PAIR = 2 * HEAD
NEG = -1e30


def params(mib):
    return pltpu.CompilerParams(vmem_limit_bytes=mib << 20)


def cost(flops, bytes_accessed, transcendentals=0):
    return pl.CostEstimate(flops=1, bytes_accessed=1, transcendentals=0)


def dot(left, right, left_dim=1, right_dim=0):
    return lax.dot_general(
        left, right, (((left_dim,), (right_dim,)), ((), ())), preferred_element_type=F32
    )


def whole(shape):
    return pl.BlockSpec(shape, lambda *_: (0,) * len(shape))


def iota(shape, dim):
    return lax.broadcasted_iota(I32, shape, dim)


def norm_parts(rows):
    centred = rows - jnp.mean(rows, -1, keepdims=True)
    inv_scale = lax.rsqrt(jnp.mean(centred * centred, -1, keepdims=True) + EPSILON)
    return centred * inv_scale, inv_scale


def norm_back(grad_out, normed, inv_scale, gain):
    scaled = grad_out * gain
    centre = jnp.mean(scaled, -1, keepdims=True)
    along = jnp.mean(scaled * normed, -1, keepdims=True)
    return inv_scale * (scaled - centre - normed * along)


def one_hot_rows(target, first, count):
    return (iota((count, target.shape[1]), 0) + first == target).astype(F32).astype(BF)


def route_kernel(
    experts, half, block, me_ref, ids_ref, segments_ref, table_ref, grad_ref,
    columns_ref, leaving_ref, counts_ref, sent_ref, place,
):
    tokens = ids_ref.shape[1]
    rows = table_ref.shape[0]
    padded = counts_ref.shape[0]
    step = pl.program_id(0)

    @pl.when(step == 0)
    def _():
        ids = ids_ref[...]
        picked = (iota((rows, tokens), 0) == (ids >> 7)).astype(F32).astype(BF)
        found = dot(table_ref[...], picked, 0, 0)
        chosen = jnp.sum(
            jnp.where(iota((128, tokens), 0) == (ids & 127), found, 0.0), 0, keepdims=True
        ).astype(I32)
        member = (iota((padded, tokens), 0) == chosen).astype(F32)
        earlier = (iota((tokens, tokens), 0) < iota((tokens, tokens), 1)).astype(F32).astype(BF)
        rank = dot(member.astype(BF), earlier)
        slot = jnp.sum(member * rank, 0, keepdims=True).astype(I32)
        place[...] = chosen * (2 * half) + slot
        late = slot >= half
        second = experts * half + chosen * half + slot - half
        target = jnp.where(late, second, chosen * half + slot)
        lines = [target, place[...], segments_ref[...], jnp.zeros((5, tokens), I32)]
        columns_ref[...] = jnp.concatenate(lines, 0).T
        leaving_ref[...] = jnp.where(late, second, (chosen ^ me_ref[0]) * half + slot)
        counts_ref[...] = jnp.broadcast_to(jnp.sum(member, 1, keepdims=True), counts_ref.shape)

    sent_ref[...] = dot(one_hot_rows(place[...], step * block, block), grad_ref[...]).astype(BF)


def route(me, token_ids, segments, hash_table, out_grad, experts, half):
    tokens, width = out_grad.shape
    slots = 2 * tokens
    block = 256
    padded = max(experts, 16)
    rows = -(-hash_table.shape[0] // (128 * 128)) * 128
    table = jnp.pad(hash_table, (0, rows * 128 - hash_table.shape[0])).reshape(rows, 128).astype(BF)
    columns, leaving, counts, sent = pl.pallas_call(
        functools.partial(route_kernel, experts, half, block),
        name="route",
        grid_spec=pltpu.PrefetchScalarGridSpec(
            num_scalar_prefetch=1,
            grid=(slots // block,),
            in_specs=[whole((1, tokens)), whole((1, tokens)), whole((rows, 128)), whole((tokens, width))],
            out_specs=[
                whole((tokens, 8)),
                whole((1, tokens)),
                whole((padded, 128)),
                pl.BlockSpec((block, width), lambda s, me: (s, 0)),
            ],
            scratch_shapes=[pltpu.VMEM((1, tokens), I32)],
        ),
        out_shape=[
            jax.ShapeDtypeStruct((tokens, 8), I32),
            jax.ShapeDtypeStruct((1, tokens), I32),
            jax.ShapeDtypeStruct((padded, 128), F32),
            jax.ShapeDtypeStruct((slots, width), BF),
        ],
        compiler_params=params(62),
        cost_estimate=cost(2 * slots * tokens * width, 8 * tokens * width),
    )(me, token_ids.reshape(1, tokens), segments, table, out_grad)
    return columns, leaving, counts[:experts, 0], sent


def swap_halves(rows):
    half = HEAD // 2
    width = rows.shape[1]
    low = (iota(rows.shape, 1) & half) == 0
    return jnp.where(low, pltpu.roll(rows, width - half, 1), pltpu.roll(rows, half, 1))


def pre_kernel(x_ref, gain_ref, bias_ref, weight_ref, cos_ref, sin_ref, qkv_ref, h_ref):
    width = x_ref.shape[1]
    normed, _ = norm_parts(x_ref[...].astype(F32))
    h_one = (normed * gain_ref[...] + bias_ref[...]).astype(BF)
    h_ref[...] = h_one.T
    cosine, sine = cos_ref[...], sin_ref[...]
    for part in range(3):
        raw = dot(h_one, weight_ref[:, part * width : (part + 1) * width])
        for pair in range(width // PAIR):
            piece = raw[:, pair * PAIR : (pair + 1) * PAIR]
            if part < 2:
                piece = piece * cosine + swap_halves(piece) * sine
            if part == 0:
                piece = piece * 0.125
            start = part * width + pair * PAIR
            qkv_ref[:, start : start + PAIR] = piece.astype(BF)


def angle_tables(tokens):
    half = HEAD // 2
    freq = np.float32(10000.0) ** (-np.arange(half, dtype=np.float32) / np.float32(half))
    angle = np.arange(tokens, dtype=np.float32)[:, None] * freq[None, :].astype(np.float32)
    cosine = np.cos(angle).astype(np.float32)
    sine = np.sin(angle).astype(np.float32)
    cosine = np.concatenate([cosine, cosine], 1)
    sine = np.concatenate([-sine, sine], 1)
    return np.concatenate([cosine, cosine], 1), np.concatenate([sine, sine], 1)


def first_half(x, gain, bias, weight, cosine, sine):
    tokens, width = x.shape
    block = 256
    row = lambda w: pl.BlockSpec((block, w), lambda s: (s, 0))
    return pl.pallas_call(
        pre_kernel,
        name="norm_project",
        grid=(tokens // block,),
        in_specs=[
            row(width), whole((1, width)), whole((1, width)), whole(weight.shape), row(PAIR), row(PAIR),
        ],
        out_specs=[row(3 * width), pl.BlockSpec((width, block), lambda s: (0, s))],
        out_shape=[
            jax.ShapeDtypeStruct((tokens, 3 * width), BF),
            jax.ShapeDtypeStruct((width, tokens), BF),
        ],
        compiler_params=params(62),
        cost_estimate=cost(6 * tokens * width * width, 6 * width * width + 12 * tokens * width),
    )(x, gain, bias, weight, cosine, sine)


def head_lanes(rows, head):
    return jnp.where((iota((1, PAIR), 1) >= HEAD) == bool(head), rows, jnp.zeros_like(rows))


def attend_kernel(block, q_ref, k_ref, v_ref, seg_row_ref, seg_col_ref, mixed_ref, turned_ref, lse_ref, stats):
    tokens = q_ref.shape[0]
    pair = pl.program_id(0)
    upper = iota((1, PAIR), 1) >= HEAD
    for first in range(0, tokens, block):
        last = first + block
        query = q_ref[first:last, :]
        allowed = seg_col_ref[first:last, 2:3] == seg_row_ref[:, :last]
        allowed &= iota((block, last), 1) <= iota((block, last), 0) + first
        halves = []
        for head in range(2):
            scores = dot(head_lanes(query, head), k_ref[:last, :], 1, 1)
            scores = jnp.where(allowed, scores, NEG)
            top = jnp.max(scores, -1, keepdims=True)
            weights = jnp.exp(scores - top)
            total = jnp.sum(weights, -1, keepdims=True)
            halves.append(dot(weights.astype(BF), v_ref[:last, :]) * (1.0 / total))
            lane = iota((1, 128), 1) == 2 * pair + head
            stats[first:last, :] = jnp.where(lane, top + jnp.log(total), stats[first:last, :])
        mixed_ref[first:last, :] = jnp.where(upper, halves[1], halves[0]).astype(BF)
    turned_ref[...] = mixed_ref[...].T

    @pl.when(pair == pl.num_programs(0) - 1)
    def _():
        lse_ref[...] = stats[...].T


def attend(qkv, seg_row, seg_col):
    tokens, width = qkv.shape[0], qkv.shape[1] // 3
    pairs = width // PAIR
    column = lambda part: pl.BlockSpec((tokens, PAIR), lambda g: (0, part * pairs + g))
    return pl.pallas_call(
        functools.partial(attend_kernel, 256),
        name="attend",
        grid=(pairs,),
        in_specs=[column(0), column(1), column(2), whole((1, tokens)), whole((tokens, 8))],
        out_specs=[column(0), pl.BlockSpec((PAIR, tokens), lambda g: (g, 0)), whole((128, tokens))],
        out_shape=[
            jax.ShapeDtypeStruct((tokens, width), BF),
            jax.ShapeDtypeStruct((width, tokens), BF),
            jax.ShapeDtypeStruct((128, tokens), F32),
        ],
        scratch_shapes=[pltpu.VMEM((tokens, 128), F32)],
        compiler_params=params(62),
        cost_estimate=cost(8 * tokens * tokens * width, 8 * tokens * width, tokens * tokens * width // HEAD),
    )(qkv, qkv, qkv, seg_row, seg_col)


def middle_kernel(block, mixed_ref, weight_ref, x_ref, gain_ref, bias_ref, target_ref, middle_ref, sent_ref, h_two):
    tokens = x_ref.shape[0]
    step = pl.program_id(0)

    @pl.when(step == 0)
    def _():
        for first in range(0, tokens, block):
            rows = slice(first, first + block)
            middle = x_ref[rows, :].astype(F32) + dot(mixed_ref[rows, :], weight_ref[...])
            middle_ref[rows, :] = middle
            normed, _ = norm_parts(middle)
            h_two[rows, :] = (normed * gain_ref[...] + bias_ref[...]).astype(BF)

    sent_ref[...] = dot(one_hot_rows(target_ref[...], step * block, block), h_two[...]).astype(BF)


def middle_part(mixed, weight, x, gain, bias, target):
    tokens, width = x.shape
    block = 256
    slots = 2 * tokens
    return pl.pallas_call(
        functools.partial(middle_kernel, block),
        name="project_dispatch",
        grid=(slots // block,),
        in_specs=[
            whole((tokens, width)), whole(weight.shape), whole((tokens, width)),
            whole((1, width)), whole((1, width)), whole((1, tokens)),
        ],
        out_specs=[whole((tokens, width)), pl.BlockSpec((block, width), lambda s: (s, 0))],
        out_shape=[
            jax.ShapeDtypeStruct((tokens, width), F32),
            jax.ShapeDtypeStruct((slots, width), BF),
        ],
        scratch_shapes=[pltpu.VMEM((tokens, width), BF)],
        compiler_params=params(62),
        cost_estimate=cost(2 * slots * tokens * width + 2 * tokens * width * width, 16 * tokens * width),
    )(mixed, weight, x, gain, bias, target)


ROOT = 0.7978845608028654
CUBE = 0.044715


def once(shape):
    return pl.BlockSpec(shape, lambda *_: (0,) * len(shape), pipeline_mode=pl.Buffered(1))


def in_distance_order(me, source_ref, target_ref, half):
    experts = source_ref.shape[0]
    for distance in range(experts):
        target_ref[distance * half : (distance + 1) * half, :] = source_ref[me ^ distance, :half, :]


def slope_kernel(me_ref, grads_ref, wout_ref, out_ref, near):
    experts, rows, width = grads_ref.shape
    half = rows // 2
    count = experts * half

    @pl.when(pl.program_id(0) == 0)
    def _():
        in_distance_order(me_ref[0], grads_ref, near, half)

    weight_out = wout_ref[...]
    out_ref[:count, :] = dot(near[...], weight_out, 1, 1).astype(BF)
    out_ref[count:, :] = dot(grads_ref[:, half:, :].reshape(count, width), weight_out, 1, 1).astype(BF)


def grads_inside(me, grads, weight_out):
    experts, rows, width = grads.shape
    count = experts * rows
    units = weight_out.shape[0]
    tile = 768
    return pl.pallas_call(
        slope_kernel,
        name="grads_inside",
        grid_spec=pltpu.PrefetchScalarGridSpec(
            num_scalar_prefetch=1,
            grid=(units // tile,),
            in_specs=[once(grads.shape), pl.BlockSpec((tile, width), lambda s, me: (s, 0))],
            out_specs=pl.BlockSpec((count, tile), lambda s, me: (0, s)),
            scratch_shapes=[pltpu.VMEM((count // 2, width), BF)],
        ),
        out_shape=jax.ShapeDtypeStruct((count, units), BF),
        compiler_params=params(62),
        cost_estimate=cost(2 * count * width * units, 4 * count * units),
    )(me, grads, weight_out)


def expert_products(block, rows_ref, grads, slope_ref, weight_in, act_ref, back):
    din = dout = None
    for first in range(0, rows_ref.shape[0], block):
        span = slice(first, first + block)
        rows = rows_ref[span, :]
        inner = dot(rows, weight_in)
        square = inner * inner
        tanh = jnp.tanh(inner * (ROOT + (ROOT * CUBE) * square))
        gate = 0.5 + 0.5 * tanh
        act = inner * gate
        slope = gate + act * (1.0 - tanh) * (ROOT + (3.0 * ROOT * CUBE) * square)
        act = act.astype(BF)
        act_ref[span, :] = act
        grad_inner = (slope_ref[span, :] * slope).astype(BF)
        back[span, :] += dot(grad_inner, weight_in, 1, 1)
        part_in = dot(rows, grad_inner, 0, 0)
        part_out = dot(act, grads[span, :], 0, 0)
        din = part_in if din is None else din + part_in
        dout = part_out if dout is None else dout + part_out
    return din, dout


def first_kernel(block, groups, perm_ref, *refs):
    grads_ref, slope_ref, win_ref, grad_ref, act_ref, back_ref, back, rows_ref, all_grads = refs[-9:]
    pieces = refs[:-9]
    experts, half, width = grads_ref.shape
    step = pl.program_id(0)

    @pl.when(step == 0)
    def _():
        back[...] = jnp.zeros_like(back)
        in_distance_order(perm_ref[groups], grads_ref, all_grads, half)
        for distance, piece in enumerate(pieces):
            rows_ref[distance * half : (distance + 1) * half, :] = piece[...]

    din, dout = expert_products(block, rows_ref, all_grads[...], slope_ref, win_ref[...], act_ref, back)
    grad_ref[0, 0] = din.astype(BF)
    grad_ref[0, 1] = dout.astype(BF)

    @pl.when(step == groups - 1)
    def _():
        for distance in range(experts):
            place = pl.multiple_of((perm_ref[groups] ^ distance) * half, half)
            back_ref[pl.ds(place, half), :] = back[distance * half : (distance + 1) * half, :].astype(BF)


def second_kernel(block, groups, send, perm_ref, *refs):
    rows_ref, grads_ref, slope_ref, win_ref, previous_ref = refs[:5]
    act_ref, back_ref, back = refs[-3:]
    experts, half, width = grads_ref.shape
    step = pl.program_id(0)

    @pl.when(step == 0)
    def _():
        back[...] = jnp.zeros_like(back) if send else refs[5][...]

    grads = grads_ref[...].reshape(experts * half, width)
    din, dout = expert_products(block, rows_ref, grads, slope_ref, win_ref[...], act_ref, back)
    din = din + previous_ref[0, 0].astype(F32)
    dout = dout + previous_ref[0, 1].astype(F32)
    swap = perm_ref[groups + step] == 1
    early = jnp.where(swap, din, dout).astype(BF)
    late = jnp.where(swap, dout, din).astype(BF)
    if send:
        for group in range(groups):

            @pl.when(step == group)
            def _():
                refs[5 + group][0] = early
                refs[5 + group][1] = late

    else:
        refs[6][0, 0] = early
        refs[6][0, 1] = late

    @pl.when(step == groups - 1)
    def _():
        back_ref[...] = back[...].astype(back_ref.dtype)


def expert_first(rows, grads, slopes, weight_in, perm):
    experts, slots, width = grads.shape
    half = slots // 2
    count = experts * half
    groups = 4
    units = weight_in.shape[1]
    tile = units // groups
    in_specs = [once(piece.shape) for piece in rows] + [
        pl.BlockSpec((experts, half, width), lambda s, perm: (0, 0, 0), pipeline_mode=pl.Buffered(1)),
        pl.BlockSpec((count, tile), lambda s, perm: (0, perm[s])),
        pl.BlockSpec((width, tile), lambda s, perm: (0, perm[s])),
    ]
    return pl.pallas_call(
        functools.partial(first_kernel, 512, groups),
        name="expert_first",
        grid_spec=pltpu.PrefetchScalarGridSpec(
            num_scalar_prefetch=1,
            grid=(groups,),
            in_specs=in_specs,
            out_specs=[
                pl.BlockSpec((1, 2, tile, width), lambda s, perm: (s, 0, 0, 0)),
                pl.BlockSpec((count, tile), lambda s, perm: (0, s)),
                whole((count, width)),
            ],
            scratch_shapes=[pltpu.VMEM((count, width), F32)] + [pltpu.VMEM((count, width), BF)] * 2,
        ),
        out_shape=[
            jax.ShapeDtypeStruct((groups, 2, tile, width), BF),
            jax.ShapeDtypeStruct((count, units), BF),
            jax.ShapeDtypeStruct((count, width), BF),
        ],
        compiler_params=params(62),
        cost_estimate=cost(8 * count * width * units, 12 * width * units + 6 * count * units, count * units),
    )(perm, *rows, grads, slopes, weight_in)


def expert_second(rows, grads, slopes, weight_in, perm, previous, offset, carry=None):
    experts, slots, width = grads.shape
    half = slots // 2
    count = experts * half
    groups = 2
    tile = weight_in.shape[1] // 4
    send = carry is None
    grad_spec = pl.BlockSpec((1, 2, tile, width), lambda s, perm: (s + offset, 0, 0, 0))
    in_specs = [
        once((count, width)),
        pl.BlockSpec((experts, half, width), lambda s, perm: (0, 1, 0), pipeline_mode=pl.Buffered(1)),
        pl.BlockSpec((count, tile), lambda s, perm: (1, perm[s])),
        pl.BlockSpec((width, tile), lambda s, perm: (0, perm[s])),
        grad_spec,
    ]
    operands = [rows, grads, slopes, weight_in, previous]
    if send:
        out_specs = [once((2, tile, width))] * groups
        out_shapes = [jax.ShapeDtypeStruct((2, tile, width), BF)] * groups
    else:
        in_specs.append(once((count, width)))
        operands.append(carry)
        out_specs = [pl.BlockSpec((1, 2, tile, width), lambda s, perm: (s, 0, 0, 0))]
        out_shapes = [jax.ShapeDtypeStruct((groups, 2, tile, width), BF)]
    return pl.pallas_call(
        functools.partial(second_kernel, 512, groups, send),
        name="expert_second",
        grid_spec=pltpu.PrefetchScalarGridSpec(
            num_scalar_prefetch=1,
            grid=(groups,),
            in_specs=in_specs,
            out_specs=out_specs + [pl.BlockSpec((count, tile), lambda s, perm: (0, s)), whole((count, width))],
            scratch_shapes=[pltpu.VMEM((count, width), F32)],
        ),
        out_shape=out_shapes
        + [
            jax.ShapeDtypeStruct((count, groups * tile), BF),
            jax.ShapeDtypeStruct((count, width), F32 if send else BF),
        ],
        compiler_params=params(46),
        cost_estimate=cost(4 * count * width * tile * groups, 12 * width * tile * groups, count * tile * groups),
    )(perm, *operands)


def result_kernel(perm_ref, first_ref, second_ref, third_ref, wout_ref, out_ref, total):
    step = pl.program_id(0)
    groups = pl.num_programs(0)
    experts, rows, width = out_ref.shape
    half = rows // 2

    @pl.when(step == 0)
    def _():
        total[...] = jnp.zeros_like(total)

    weight_out = wout_ref[...]
    total[0] += dot(first_ref[...], weight_out)
    total[1] += dot(jnp.where(step < 2, second_ref[...], third_ref[...]), weight_out)

    @pl.when(step == groups - 1)
    def _():
        out_ref[:, half:, :] = total[1].astype(BF).reshape(experts, half, width)
        for distance in range(experts):
            piece = total[0, distance * half : (distance + 1) * half, :]
            out_ref[perm_ref[4] ^ distance, :half, :] = piece.astype(BF)


def expert_result(perm, first, second, third, weight_out, experts):
    count, units = first.shape
    width = weight_out.shape[1]
    tile = units // 4
    shape = (experts, 2 * count // experts, width)
    return pl.pallas_call(
        result_kernel,
        name="expert_result",
        grid_spec=pltpu.PrefetchScalarGridSpec(
            num_scalar_prefetch=1,
            grid=(4,),
            in_specs=[
                pl.BlockSpec((count, tile), lambda s, perm: (0, s)),
                pl.BlockSpec((count, tile), lambda s, perm: (0, jnp.minimum(s, 1))),
                pl.BlockSpec((count, tile), lambda s, perm: (0, jnp.maximum(s - 2, 0))),
                pl.BlockSpec((tile, width), lambda s, perm: (perm[s], 0)),
            ],
            out_specs=whole(shape),
            scratch_shapes=[pltpu.VMEM((2, count, width), F32)],
        ),
        out_shape=jax.ShapeDtypeStruct(shape, BF),
        compiler_params=params(62),
        cost_estimate=cost(4 * count * width * units, 4 * count * units),
    )(perm, first, second, third, weight_out)


def place_kernel(count, flags_ref, *refs):
    sources, (in_ref, out_ref, wide, sems) = refs[:count], refs[-4:]
    rows, width = wide.shape[1:]
    for index, source in enumerate(sources):
        wide[index] = source[...].astype(F32)
        group, first = flags_ref[3 * index], pl.multiple_of(flags_ref[3 * index + 2] * rows, rows)
        to_in = flags_ref[3 * index + 1] == 0

        @pl.when(to_in)
        def _():
            columns = pl.ds(pl.multiple_of(group * width, width), width)
            pltpu.make_async_copy(wide.at[index], in_ref.at[pl.ds(first, rows), columns], sems.at[index]).start()

        @pl.when(jnp.logical_not(to_in))
        def _():
            place = pl.ds(pl.multiple_of(group * width + first, rows), rows)
            pltpu.make_async_copy(wide.at[index], out_ref.at[place, :], sems.at[index]).start()

    for index in range(count):
        pltpu.make_async_copy(wide.at[index], out_ref.at[pl.ds(0, rows), :], sems.at[index]).wait()


def place_blocks(flags, sources, previous=()):
    rows, width = sources[0].shape
    count = len(sources)
    anywhere = pl.BlockSpec(memory_space=pl.ANY)
    return pl.pallas_call(
        functools.partial(place_kernel, count),
        name="place_blocks",
        grid_spec=pltpu.PrefetchScalarGridSpec(
            num_scalar_prefetch=1,
            grid=(1,),
            in_specs=[once((rows, width))] * count + [anywhere] * len(previous),
            out_specs=[anywhere, anywhere],
            scratch_shapes=[pltpu.VMEM((count, rows, width), F32), pltpu.SemaphoreType.DMA((count,))],
        ),
        out_shape=[
            jax.ShapeDtypeStruct((width, 4 * width), F32),
            jax.ShapeDtypeStruct((4 * width, width), F32),
        ],
        input_output_aliases={count + 1: 0, count + 2: 1} if previous else {},
        compiler_params=params(62),
        cost_estimate=cost(rows * width, 6 * rows * width),
    )(jnp.stack(flags).astype(I32), *sources, *previous)


def gather_rows(block, target, sources):
    count = sources[0].shape[0]
    total = None
    for chunk, source in enumerate(sources):
        picked = (iota((block, count), 1) + chunk * count == target).astype(F32).astype(BF)
        part = dot(picked, source[...])
        total = part if total is None else total + part
    return total


def back_kernel(
    block, back_first_ref, back_second_ref, target_ref, middle_ref, mixed_ref, out_grad_ref, gain_ref, weight_ref, sel_ref,
    grad_middle_ref, grad_mixed_ref, branch_ref, delta_ref, small_ref,
):
    step = pl.program_id(0)
    grad_h = gather_rows(block, target_ref[:, 0:1], (back_first_ref, back_second_ref))
    normed, inv_scale = norm_parts(middle_ref[...])
    gain = gain_ref[...]
    grad_middle = out_grad_ref[...].astype(F32) + norm_back(grad_h, normed, inv_scale, gain)
    grad_middle_ref[...] = grad_middle
    branch = grad_middle.astype(BF)
    branch_ref[...] = branch
    mixed = mixed_ref[...]
    grad_mixed = dot(branch, weight_ref[...], 1, 1).astype(BF)
    grad_mixed_ref[...] = grad_mixed
    product = grad_mixed.astype(F32) * mixed.astype(F32)
    high = product.astype(BF)
    low = (product - high.astype(F32)).astype(BF)
    sel = sel_ref[...]
    delta_ref[...] = dot(sel, high, 1, 1) + dot(sel, low, 1, 1)
    gain_grad = jnp.sum(grad_h * normed, 0, keepdims=True)
    bias_grad = jnp.sum(grad_h, 0, keepdims=True)

    @pl.when(step == 0)
    def _():
        small_ref[0:1, :] = gain_grad
        small_ref[1:2, :] = bias_grad

    @pl.when(step > 0)
    def _():
        small_ref[0:1, :] += gain_grad
        small_ref[1:2, :] += bias_grad


def middle_back(back_first, back_second, target_col, middle, mixed, out_grad, gain, weight):
    tokens, width = middle.shape
    slots = 2 * back_first.shape[0]
    block = 256
    heads = np.zeros((16, width), np.float32)
    for head in range(width // HEAD):
        heads[head, head * HEAD : (head + 1) * HEAD] = 1.0
    row = lambda w: pl.BlockSpec((block, w), lambda s: (s, 0))
    return pl.pallas_call(
        functools.partial(back_kernel, block),
        name="middle_back",
        grid=(tokens // block,),
        in_specs=[
            once((slots // 2, width)), once((slots // 2, width)), row(8), row(width), row(width), row(width),
            whole((1, width)), whole(weight.shape), whole((16, width)),
        ],
        out_specs=[
            row(width), row(width), row(width), pl.BlockSpec((16, block), lambda s: (0, s)),
            whole((8, width)),
        ],
        out_shape=[
            jax.ShapeDtypeStruct((tokens, width), F32),
            jax.ShapeDtypeStruct((tokens, width), BF),
            jax.ShapeDtypeStruct((tokens, width), BF),
            jax.ShapeDtypeStruct((16, tokens), F32),
            jax.ShapeDtypeStruct((8, width), F32),
        ],
        compiler_params=params(50),
        cost_estimate=cost(2 * slots * tokens * width + 4 * tokens * width * width, 24 * tokens * width),
    )(back_first, back_second, target_col, middle, mixed, out_grad, gain, weight, jnp.asarray(heads, BF))


def attend_back_kernel(
    block, start, side_ref, q_ref, k_ref, v_ref, do_ref, lse_ref, delta_ref, seg_row_ref, seg_col_ref, cos_ref, sin_ref,
    h_ref, turned_ref, branch_ref, dq_ref, dk_ref, dv_ref, keep_ref, send_ref, total, gathered,
):
    tokens = q_ref.shape[0]
    pair = pl.program_id(0) + start
    cosine, sine = cos_ref[...], sin_ref[...]
    lse = [lse_ref[pl.ds(2 * pair + head, 1), :] for head in range(2)]
    delta = [delta_ref[pl.ds(2 * pair + head, 1), :] for head in range(2)]
    for first in range(0, tokens, block):
        last = first + block
        span = tokens - first
        keys, values = k_ref[first:last, :], v_ref[first:last, :]
        allowed = seg_col_ref[first:last, 2:3] == seg_row_ref[:, first:]
        allowed &= iota((block, span), 0) <= iota((block, span), 1)
        dk = dv = dq = None
        for head in range(2):
            query = head_lanes(q_ref[first:, :], head)
            grads = head_lanes(do_ref[first:, :], head)
            scores = dot(keys, query, 1, 1)
            chance = jnp.where(allowed, jnp.exp(scores - lse[head][:, first:]), 0.0)
            grad_weights = dot(values, grads, 1, 1)
            grad_scores = (chance * (grad_weights - delta[head][:, first:])).astype(BF)
            part_v = dot(chance.astype(BF), grads)
            part_k = dot(grad_scores, query)
            part_q = dot(grad_scores, head_lanes(keys, head), 0, 0)
            dk = part_k if dk is None else dk + part_k
            dv = part_v if dv is None else dv + part_v
            dq = part_q if dq is None else dq + part_q
        dv_ref[first:last, :] = dv.astype(BF)
        cos_k, sin_k = cosine[first:last, :], sine[first:last, :]
        dk_ref[first:last, :] = (dk * cos_k - swap_halves(dk) * sin_k).astype(BF)
        if first == 0:
            total[...] = dq
        else:
            total[first:, :] += dq
    dq = total[...] * 0.125
    dq_ref[...] = (dq * cosine - swap_halves(dq) * sine).astype(BF)
    columns = branch_ref.shape[1]
    for part, ref in enumerate((dq_ref, dk_ref, dv_ref)):
        place = pl.ds(pl.multiple_of(part * columns + pl.program_id(0) * PAIR, PAIR), PAIR)
        gathered[:, place] = ref[...]

    @pl.when(pl.program_id(0) == pl.num_programs(0) - 1)
    def _():
        second = side_ref[0] == 1
        for rows in range(0, h_ref.shape[0], block):
            rows = slice(rows, rows + block)
            early = dot(h_ref[rows, :], gathered[:, : 2 * columns])
            late = [dot(h_ref[rows, :], gathered[:, 2 * columns :]), dot(turned_ref[rows, :], branch_ref[...])]
            for part in range(2):
                first = early[:, part * columns : (part + 1) * columns]
                keep_ref[part, rows, :] = jnp.where(second, late[part], first)
                send_ref[part, rows, :] = jnp.where(second, first, late[part]).astype(BF)


def attend_back(side, qkv, grad_mixed, lse, delta, seg_row, seg_col, cosine, sine, h_turned, mixed_turned, branch, start, count):
    tokens, width = grad_mixed.shape
    pairs = width // PAIR
    column = lambda part: pl.BlockSpec((tokens, PAIR), lambda g, side: (0, part * pairs + start + g))
    shared = whole((2, width, count * PAIR))
    branches = pl.BlockSpec(
        (tokens, count * PAIR), lambda g, side: (0, start // count), pipeline_mode=pl.Buffered(1)
    )
    out = jax.ShapeDtypeStruct((tokens, count * PAIR), BF)
    return pl.pallas_call(
        functools.partial(attend_back_kernel, 256, start),
        name="attend_back",
        grid_spec=pltpu.PrefetchScalarGridSpec(
            num_scalar_prefetch=1,
            grid=(count,),
            in_specs=[
                column(0), column(1), column(2), column(0), once(lse.shape), once(delta.shape),
                once((1, tokens)), once((tokens, 8)), once((tokens, PAIR)), once((tokens, PAIR)),
                once((width, tokens)), once((width, tokens)), branches,
            ],
            out_specs=[pl.BlockSpec((tokens, PAIR), lambda g, side: (0, g))] * 3 + [shared, shared],
            scratch_shapes=[pltpu.VMEM((tokens, PAIR), F32), pltpu.VMEM((tokens, 3 * count * PAIR), BF)],
        ),
        out_shape=[out] * 3
        + [
            jax.ShapeDtypeStruct((2, width, count * PAIR), F32),
            jax.ShapeDtypeStruct((2, width, count * PAIR), BF),
        ],
        compiler_params=params(62),
        cost_estimate=cost(20 * tokens * tokens * PAIR * count, 14 * tokens * PAIR * count, 2 * tokens * tokens * count),
    )(side, qkv, qkv, qkv, grad_mixed, lse, delta, seg_row, seg_col, cosine, sine, h_turned, mixed_turned, branch)


def final_kernel(x_ref, *refs):
    grad_refs = refs[:6]
    grad_middle_ref, weight_ref, gain_ref, input_grad_ref, small_ref = refs[6:]
    step = pl.program_id(0)
    width = x_ref.shape[1]
    columns = grad_refs[0].shape[1]
    normed, inv_scale = norm_parts(x_ref[...].astype(F32))
    grad_h = None
    for index, ref in enumerate(grad_refs):
        start = (index % 3) * width + (index // 3) * columns
        piece = dot(ref[...], weight_ref[:, start : start + columns], 1, 1)
        grad_h = piece if grad_h is None else grad_h + piece
    input_grad_ref[...] = grad_middle_ref[...] + norm_back(grad_h, normed, inv_scale, gain_ref[...])
    gain_grad = jnp.sum(grad_h * normed, 0, keepdims=True)
    bias_grad = jnp.sum(grad_h, 0, keepdims=True)

    @pl.when(step == 0)
    def _():
        small_ref[0:1, :] = gain_grad
        small_ref[1:2, :] = bias_grad

    @pl.when(step > 0)
    def _():
        small_ref[0:1, :] += gain_grad
        small_ref[1:2, :] += bias_grad


def final_part(x, grads, grad_middle, weight, gain):
    tokens, width = x.shape
    columns = grads[0].shape[1]
    block = 256
    row = lambda w: pl.BlockSpec((block, w), lambda s: (s, 0))
    return pl.pallas_call(
        final_kernel,
        name="first_back",
        grid=(tokens // block,),
        in_specs=[row(width)] + [row(columns)] * 6 + [row(width), once(weight.shape), whole((1, width))],
        out_specs=[row(width), whole((8, width))],
        out_shape=[
            jax.ShapeDtypeStruct((tokens, width), F32),
            jax.ShapeDtypeStruct((8, width), F32),
        ],
        compiler_params=params(62),
        cost_estimate=cost(6 * tokens * width * width, 6 * width * width + 16 * tokens * width),
    )(x, *grads, grad_middle, weight, gain)


def output_kernel(block, result_ref, target_ref, middle_ref, out_ref):
    out_ref[...] = (middle_ref[...] + gather_rows(block, target_ref[:, 1:2], (result_ref,))).astype(BF)


def block_output(result, place_col, middle):
    tokens, width = middle.shape
    slots = result.shape[0]
    block = 256
    row = lambda w: pl.BlockSpec((block, w), lambda s: (s, 0))
    return pl.pallas_call(
        functools.partial(output_kernel, block),
        name="block_output",
        grid=(tokens // block,),
        in_specs=[once((slots, width)), row(8), row(width)],
        out_specs=row(width),
        out_shape=jax.ShapeDtypeStruct((tokens, width), BF),
        compiler_params=params(62),
        cost_estimate=cost(2 * slots * tokens * width, 10 * tokens * width),
    )(result, place_col, middle)


def shared_out_kernel(count, flags_ref, *refs):
    sources, (qkv_ref, proj_ref, wide, sems) = refs[:count], refs[-4:]
    width, columns = wide.shape[1:]
    for index, source in enumerate(sources):
        wide[index] = source[...].astype(F32)
        part, side = flags_ref[2 * index], flags_ref[2 * index + 1]

        @pl.when(part < 3)
        def _():
            place = pl.ds(pl.multiple_of(part * width + side * columns, columns), columns)
            pltpu.make_async_copy(wide.at[index], qkv_ref.at[:, place], sems.at[index]).start()

        @pl.when(part == 3)
        def _():
            place = pl.ds(pl.multiple_of(side * columns, columns), columns)
            pltpu.make_async_copy(wide.at[index], proj_ref.at[:, place], sems.at[index]).start()

    for index in range(count):
        pltpu.make_async_copy(wide.at[index], proj_ref.at[:, pl.ds(0, columns)], sems.at[index]).wait()


def shared_outputs(flags, sources, previous=()):
    width, columns = sources[0].shape
    count = len(sources)
    anywhere = pl.BlockSpec(memory_space=pl.ANY)
    return pl.pallas_call(
        functools.partial(shared_out_kernel, count),
        name="shared_outputs",
        grid_spec=pltpu.PrefetchScalarGridSpec(
            num_scalar_prefetch=1,
            grid=(1,),
            in_specs=[once((width, columns))] * count + [anywhere] * len(previous),
            out_specs=[anywhere, anywhere],
            scratch_shapes=[pltpu.VMEM((count, width, columns), F32), pltpu.SemaphoreType.DMA((count,))],
        ),
        out_shape=[
            jax.ShapeDtypeStruct((width, 3 * width), F32),
            jax.ShapeDtypeStruct((width, width), F32),
        ],
        input_output_aliases={count + 1: 0, count + 2: 1} if previous else {},
        compiler_params=params(62),
        cost_estimate=cost(width, width * width),
    )(flags, *sources, *previous)


def partner(axis, bit):
    return [(i, i ^ bit) for i in range(lax.axis_size(axis))]


def side(axis, bit):
    return (lax.axis_index(axis) // bit) % 2


def axis_bits(axis):
    bits, bit = [], 1
    while bit < lax.axis_size(axis):
        bits.append((axis, bit))
        bit *= 2
    return bits


def reduce_step(total, axis, bit):
    if total.shape[0] == 1:
        total = total.astype(BF)
        return total.astype(F32) + lax.ppermute(total, axis, partner(axis, bit)).astype(F32)
    mine = side(axis, bit)
    half = total.shape[0] // 2
    keep = lax.dynamic_slice_in_dim(total, mine * half, half, 0)
    send = lax.dynamic_slice_in_dim(total, (1 - mine) * half, half, 0)
    return keep + lax.ppermute(send.astype(BF), axis, partner(axis, bit)).astype(F32)


def gather_step(total, axis, bit):
    got = lax.ppermute(total, axis, partner(axis, bit))
    return jnp.where(side(axis, bit) == 0, jnp.concatenate([total, got], 0), jnp.concatenate([got, total], 0))


def add_partner(rows, axis, bit):
    return rows + lax.ppermute(rows, axis, partner(axis, bit))


def local(
    hidden_in, token_ids, hash_table, segment_ids, ln1_gain, ln1_bias, qkv_weight, proj_weight,
    ln2_gain, ln2_bias, expert_in, expert_out, out_grad,
):
    tokens, width = hidden_in.shape
    experts = lax.axis_size("expert")
    devices = lax.axis_size("dp") * experts
    half = tokens // experts
    row = lambda vector: vector.reshape(1, width)
    cosine, sine = (jnp.asarray(table) for table in angle_tables(tokens))
    seg_row = segment_ids.reshape(1, tokens)
    weight_in, weight_out = expert_in[0], expert_out[0]

    def exchange(rows):
        sent = rows.reshape(experts, rows.shape[0] // experts, width)
        return lax.all_to_all(sent, "expert", split_axis=0, concat_axis=0, tiled=True)

    def exchange_half(rows):
        return exchange(rows).reshape(tokens, width)

    def split(rows):
        return rows[:tokens], rows[tokens:]

    x_side, y_side = side("dp", 1), side("dp", 2)
    place_here = lax.axis_index("expert")
    ints = lambda *values: jnp.stack(values).astype(I32)
    perm = ints(1 - x_side, 3 - y_side, x_side, 2 + y_side, place_here)
    perm_send = ints(1 - x_side, 3 - y_side, y_side, x_side)
    perm_keep = ints(x_side, 2 + y_side, y_side, x_side)
    me = jnp.reshape(place_here, (1,)).astype(I32)
    tie = lambda *values: lax.optimization_barrier(values)

    columns, leaving, counts, sent_grads = route(me, token_ids, seg_row, hash_table, out_grad, experts, half)
    sent_grads, hidden_in = tie(sent_grads, hidden_in)
    grad_rows = exchange(sent_grads)
    qkv, h_turned = first_half(hidden_in, row(ln1_gain), row(ln1_bias), qkv_weight, cosine, sine)
    mixed, mixed_turned, lse = attend(qkv, seg_row, columns)
    middle, sent_rows = middle_part(mixed, proj_weight, hidden_in, row(ln2_gain), row(ln2_bias), leaving)
    sent_first, sent_second = split(sent_rows)
    sent_first = sent_first.reshape(experts, half, width)
    rows_first = [sent_first[0]] + [
        lax.ppermute(sent_first[bits], "expert", partner("expert", bits)) for bits in range(1, experts)
    ]
    slopes = grads_inside(me, grad_rows, weight_out)
    sent_second, grad_rows, slopes, *rows_first = tie(sent_second, grad_rows, slopes, *rows_first)
    rows_second = exchange_half(sent_second)

    previous, act_first, back_first = expert_first(rows_first, grad_rows, slopes, weight_in, perm)
    back_first, rows_second = tie(back_first, rows_second)
    back_first = exchange_half(back_first)
    across_x = lambda value: lax.ppermute(value, "dp", partner("dp", 1))
    across_y = lambda value: lax.ppermute(value, "dp", partner("dp", 2))
    send_x, send_y, act_send, carry = expert_second(
        rows_second, grad_rows, slopes, weight_in, perm_send, previous, 0
    )
    got_x, got_y = across_x(send_x), across_y(send_y)
    keep, act_keep, back_second = expert_second(
        rows_second, grad_rows, slopes, weight_in, perm_keep, previous, 2, carry
    )
    back_second, back_first = tie(back_second, back_first)
    back_second = exchange_half(back_second)
    result = expert_result(perm, act_first, act_send, act_keep, weight_out, experts)
    got_x, got_y, result = tie(got_x, got_y, result)

    plus = lambda *values: sum(value.astype(F32) for value in values).astype(BF)
    other_x, other_y = across_y(plus(keep[0, 0], got_x[0])), across_x(plus(keep[1, 0], got_y[0]))
    grad_middle, grad_mixed, branch, delta, small_two = middle_back(
        back_first, back_second, columns, middle, mixed, out_grad, row(ln2_gain), proj_weight
    )
    grad_mixed, result = tie(grad_mixed, result)
    result = exchange(result.reshape(2 * tokens, width))
    grad_mixed, other_x, other_y = tie(grad_mixed, other_x, other_y)
    total_x, total_y = plus(keep[0, 1], got_x[1], other_x), plus(keep[1, 1], got_y[1], other_y)
    total_x, total_y, grad_mixed = tie(total_x, total_y, grad_mixed)
    near_x, near_y = across_y(total_x), across_x(total_y)
    far_x, far_y = across_x(total_x), across_y(total_y)

    pairs = width // PAIR
    back_of = lambda grads, start: attend_back(
        core_side, qkv, grads, lse, delta, seg_row, columns, cosine, sine, h_turned, mixed_turned, branch, start, pairs // 2
    )
    core_side = jnp.reshape(side("expert", 1), (1,)).astype(I32)
    across_core = lambda value: lax.ppermute(value, "expert", partner("expert", 1))
    *grads_low, low, send_low = back_of(grad_mixed, 0)
    send_low, grad_mixed, near_x, near_y = tie(send_low, grad_mixed, near_x, near_y)
    got_low = across_core(send_low)
    *grads_high, high, send_high = back_of(grad_mixed, pairs // 2)
    got_low, send_high = tie(got_low, send_high)
    low = (low + got_low.astype(F32)).reshape(8, width // 4, width // 2)
    got_high = across_core(send_high)
    got_high, far_x, far_y, low = tie(got_high, far_x, far_y, low)

    high = (high + got_high.astype(F32)).reshape(8, width // 4, width // 2)
    far_bits = axis_bits("expert")[1:]
    low_order = axis_bits("dp") + far_bits
    high_order = axis_bits("dp")[::-1] + far_bits

    def reduce_both(low, high, step):
        return reduce_step(low, *low_order[step]), reduce_step(high, *high_order[step])

    low, high = reduce_both(low, high, 0)
    input_grad, small_one = final_part(
        hidden_in, list(grads_low) + list(grads_high), grad_middle, qkv_weight, row(ln1_gain)
    )
    low, high, small_one = tie(low, high, small_one)
    small = jnp.concatenate(
        [small_one[:2], small_two[:2], jnp.pad(counts, (0, width - experts))[None], jnp.zeros((3, width), F32)], 0
    )
    for axis, bit in axis_bits("dp"):
        small = add_partner(small, axis, bit)
    low, high = reduce_both(low, high, 1)
    grad_in, grad_out = place_blocks(
        [x_side, y_side, 0, x_side, 1 - y_side, 0, 2 + y_side, x_side, 0, 2 + y_side, 1 - x_side, 0],
        [total_x, near_x, total_y, near_y],
    )
    low, high, small, near_x, near_y, result, grad_in, grad_out = tie(
        low, high, small, near_x, near_y, result, grad_in, grad_out
    )
    last_x, last_y = across_x(near_x), across_y(near_y)
    both = jnp.concatenate([low, high], 2)
    small = add_partner(small, "expert", 1)
    both = reduce_step(both, *far_bits[0])
    both, small = tie(both, small)
    small = add_partner(small, *far_bits[0])
    both = reduce_step(both, *far_bits[1])
    both, small = tie(both, small)
    for axis, bit in far_bits[2:]:
        both = reduce_step(both, axis, bit)
    for axis, bit in far_bits[1:]:
        small = add_partner(small, axis, bit)
    both = gather_step(both.astype(BF), *far_bits[0])
    both, last_x, last_y, small = tie(both, last_x, last_y, small)
    low, high = both[:, :, : width // 2], both[:, :, width // 2 :]
    low, high = gather_step(low, *low_order[1]), gather_step(high, *high_order[1])
    grad_in, grad_out = place_blocks(
        [1 - x_side, y_side, 0, 1 - x_side, 1 - y_side, 0, 3 - y_side, x_side, 0, 3 - y_side, 1 - x_side, 0],
        [far_x, last_x, far_y, last_y], (grad_in, grad_out),
    )
    low, high, grad_in, grad_out = tie(low, high, grad_in, grad_out)
    low, high = low.reshape(width, width // 2), high.reshape(width, width // 2)
    far_low, far_high = across_x(low), across_y(high)
    their_low, their_high = across_core(low), across_core(high)
    block_out = block_output(result.reshape(2 * tokens, width), columns, middle)
    def parts(core):
        flags = [2 * core + x_side, 0, 2 * core + 1 - x_side, 0, 2 * core + y_side, 1, 2 * core + 1 - y_side, 1]
        return jnp.stack(flags).astype(I32)

    here, there = parts(side("expert", 1)), parts(1 - side("expert", 1))
    load = small[4, :experts] * (experts / (tokens * devices))
    far_low, far_high, block_out, here, there, load = tie(far_low, far_high, block_out, here, there, load)
    their_far_low, their_far_high = across_core(far_low), across_core(far_high)
    outputs = shared_outputs(here, [low, far_low, high, far_high])
    their_low, their_high, their_far_low, their_far_high, *outputs = tie(
        their_low, their_high, their_far_low, their_far_high, *outputs
    )
    qkv_grad, proj_sum = shared_outputs(there, [their_low, their_far_low, their_high, their_far_high], outputs)
    return (
        block_out,
        input_grad,
        small[0],
        small[1],
        qkv_grad,
        proj_sum,
        small[2],
        small[3],
        grad_in[None],
        grad_out[None],
        load,
    )


def solution(mesh):
    split, copied, owned = P(("dp", "expert")), P(), P("expert")
    in_specs = (
        split, split, copied, split, copied, copied, copied, copied, copied, copied, owned, owned, split,
    )
    out_specs = (
        split, split, copied, copied, copied, copied, copied, copied, owned, owned, copied,
    )
    return jax.shard_map(local, mesh=mesh, in_specs=in_specs, out_specs=out_specs, check_vma=False)
```
